32 devices in a mesh: ctx: 16 (over z, x, core), head: 2 (over y).
Axes of the slice: x: 2, y: 2, z: 4, core: 2. Of those that a mesh axis runs over, the one named last changes fastest.
Arguments:
- queries: bfloat16 [4096, 3072], P(('ctx', 'head')), may hold values from -48 to 48
- key_rows: bfloat16 [4096, 3072], P(('ctx', 'head')), may hold values from -6 to 6
- value_rows: bfloat16 [4096, 3072], P(('ctx', 'head')), may hold values from -6 to 6
- out_cotangent: bfloat16 [4096, 3072], P(('ctx', 'head')), may hold values from -6 to 6
- gate_table: float32 [128, 3072], replicated, may hold values from -6 to 6
- span_ids: int32 [4096], replicated, may hold values from 0 to 23, never falling along the last dimension, each value on 1 to 256 neighbouring positions
- noise_level: int32 [24], replicated, may hold values from 0 to 127
- block_mask: int32 [24, 24], replicated, may hold values from 0 to 1, as said below
Outputs:
- mixed_out: bfloat16 [4096, 3072], P(('ctx', 'head'))
- query_grad: bfloat16 [4096, 3072], P(('ctx', 'head'))
- key_grad: bfloat16 [4096, 3072], P(('ctx', 'head'))
- value_grad: bfloat16 [4096, 3072], P(('ctx', 'head'))
- gate_grad: float32 [128, 3072], replicated
The draws below stay inside these ranges and needn't reach their ends.
Inputs may be any that keep to these rules, and one draw needn't show every extreme that they name: `span_ids`: span ids never fall along the tokens; every span holds 1 to 256 tokens, one span exactly 256. `block_mask`: entries are 0 or 1; entries [c, c] and [c, c - 1] are 1 for every span c.
All inputs are finite; a program needn't handle non-finite values.
Results may differ from the reference program's by a relative error of at most 0.023.
Values may be sent and summed in bfloat16 or wider, within the bound.
No kernel may reach another device: no remote copies, remote signals or barrier semaphores. Data moves between devices by JAX's collectives and lax.ppermute only.
A program may use at most 128 MiB of HBM per device.

```python
import math
import jax
import jax.numpy as jnp
import numpy as np
from jax import lax

HEADS = 24
DH = 128
SPAN = 256
LEVELS = 128
TOKENS = 4096
WINDOW = 256
SPANS = 24


def shared_rows(key):
    full_width = HEADS * DH
    normal_q = jax.random.normal(jax.random.fold_in(key, 101), (TOKENS, full_width), jnp.float32)
    normal_k = jax.random.normal(jax.random.fold_in(key, 102), (TOKENS, full_width), jnp.float32)
    return (normal_q, normal_k)


def draw_queries(key, part):
    normal_q, normal_k = shared_rows(key)
    result = 2.0 * jnp.clip(normal_q, -6.0, 6.0)
    return result.astype(jnp.bfloat16)


def draw_key_rows(key, part):
    normal_q, normal_k = shared_rows(key)
    result = jnp.clip(normal_k, -6.0, 6.0)
    return result.astype(jnp.bfloat16)


def draw_noise_level(key, part):
    key = jax.random.fold_in(key, 3)
    order_key, level_key = jax.random.split(key)
    order = jax.random.permutation(order_key, SPANS).astype(jnp.int32)
    levels = jax.random.randint(level_key, (SPANS,), 0, LEVELS).astype(jnp.int32)
    levels = jnp.where(order == 0, 0, levels)
    levels = jnp.where(order == SPANS - 1, LEVELS - 1, levels)
    return levels.astype(jnp.int32)


def draw_block_mask(key, part):
    key = jax.random.fold_in(key, 4)
    density_key, entry_key = jax.random.split(key)
    density = jax.random.randint(density_key, (SPANS, 1), 0, 9)
    entries = jax.random.randint(entry_key, (SPANS, SPANS), 0, 8)
    row_index = jnp.arange(SPANS, dtype=jnp.int32)[:, None]
    col_index = jnp.arange(SPANS, dtype=jnp.int32)[None, :]
    chosen = (entries < density) | (col_index == row_index) | (col_index == row_index - 1)
    return chosen.astype(jnp.int32)


def steps_of(own_key, shape, pieces, smallest, top_value):
    gain = 1.0
    for position, parts in pieces:
        draws = jax.random.uniform(jax.random.fold_in(jax.random.fold_in(own_key, 6), position), (parts,), jnp.float32, smallest / len(pieces), top_value / len(pieces))
        gain = gain * jnp.repeat(jnp.exp(draws), shape[position] // parts).reshape((-1,) + (1,) * (len(shape) - 1 - position))
    return gain


def profile(number_of, total, limit, skew):
    weights = [(1 << 20) // math.isqrt(standing ** skew) + 1 for standing in range(2, number_of + 1)]
    rest, given = total - limit - (number_of - 1), [1] * (number_of - 1)
    while rest > 0:
        free = [i for i in range(number_of - 1) if given[i] < limit]
        mass, left = sum([weights[i] for i in free]), rest
        for i in free:
            addition = min(limit - given[i], max(1, left * weights[i] // mass), rest)
            given[i] = given[i] + addition
            rest = rest - addition
    return np.array([limit] + given)


def ragged(key, amount, total, most, skew):
    if amount == 2:
        one = jax.random.randint(key, (), max(1, total - most), min(most, total - 1) + 1)
        return jnp.stack([one, total - one])
    sizes = jnp.asarray(profile(amount, total, most, skew), jnp.int32)
    twos = (amount - 1) // 2
    donor, taker = sizes[1:1 + 2 * twos:2], sizes[2:2 + 2 * twos:2]
    margin = jnp.minimum(donor - 1, most - taker)
    shifted = jax.random.randint(jax.random.fold_in(key, 1), (twos,), 0, 1 << 20) % (margin + 1)
    sizes = sizes.at[1:1 + 2 * twos:2].set(donor - shifted).at[2:2 + 2 * twos:2].set(taker + shifted)
    return sizes[jax.random.permutation(jax.random.fold_in(key, 2), amount)]


def normal_values(rng, extent, scale, bound, shards=(), kind=jnp.bfloat16):
    values = scale * jax.random.normal(rng, extent, jnp.float32)
    if shards:
        values = values * steps_of(rng, extent, shards, -0.22, 0.18)
    return jnp.clip(values, -bound, bound).astype(kind)


def setup_inputs(seed: int = 0) -> dict:
    streams_of = jax.random.split(jax.random.key(seed), 9)
    queries = draw_queries(jax.random.fold_in(streams_of[8], 71), 0)
    key_rows = draw_key_rows(jax.random.fold_in(streams_of[8], 71), 0)
    value_rows = normal_values(streams_of[2], (TOKENS, HEADS * DH), 1.0, 6.0, ((0, 32),))
    out_cotangent = normal_values(streams_of[3], (TOKENS, HEADS * DH), 1.0, 6.0, ((0, 32),))
    gate_table = normal_values(streams_of[4], (LEVELS, HEADS * DH), 1.5, 6.0, (), jnp.float32)
    span_ids = jnp.searchsorted(jnp.cumsum(ragged(streams_of[5], SPANS, TOKENS, SPAN, 0)), jnp.arange(TOKENS), side="right").astype(jnp.int32)
    noise_level = draw_noise_level(jax.random.fold_in(streams_of[8], 71), 0)
    block_mask = draw_block_mask(jax.random.fold_in(streams_of[8], 71), 0)
    return {"queries": queries, "key_rows": key_rows, "value_rows": value_rows, "out_cotangent": out_cotangent, "gate_table": gate_table, "span_ids": span_ids, "noise_level": noise_level, "block_mask": block_mask}


def attend(q_block, k_block, v_block, g_block, visible, score_scale):
    count_q = q_block.shape[0]
    count_k = k_block.shape[0]
    head_count = q_block.shape[1] // DH
    q_heads = q_block.astype(jnp.float32).reshape(count_q, head_count, DH)
    k_heads = k_block.astype(jnp.float32).reshape(count_k, head_count, DH)
    v_heads = v_block.astype(jnp.float32).reshape(count_k, head_count, DH)
    g_heads = g_block.astype(jnp.float32).reshape(count_q, head_count, DH)
    scores = jnp.einsum('qhd,khd->hqk', q_heads, k_heads) * score_scale
    scores = jnp.where(visible[None], scores, -jnp.inf)
    row_max = lax.optimization_barrier(jnp.max(scores, axis=2, keepdims=True))
    log_total = row_max + jnp.log(lax.optimization_barrier(jnp.sum(jnp.exp(scores - row_max), axis=2, keepdims=True)))
    attention = jnp.exp(scores - log_total)
    attention_low = attention.astype(jnp.bfloat16)
    attention_back = lax.optimization_barrier(attention_low).astype(jnp.float32)
    attended = jnp.einsum('hqk,khd->qhd', attention_back, v_heads).astype(jnp.bfloat16)
    attended_back = lax.optimization_barrier(attended).astype(jnp.float32)
    row_dot = jnp.einsum('qhd,qhd->hq', g_heads, attended_back)[:, :, None]
    prob_grad = jnp.einsum('qhd,khd->hqk', g_heads, v_heads)
    score_grad = (attention * (prob_grad - row_dot)).astype(jnp.bfloat16)
    score_back = lax.optimization_barrier(score_grad).astype(jnp.float32)
    query_grad = (jnp.einsum('hqk,khd->qhd', score_back, k_heads) * score_scale).astype(jnp.bfloat16)
    key_grad = jnp.einsum('hqk,qhd->khd', score_back, q_heads) * score_scale
    value_grad = jnp.einsum('hqk,qhd->khd', attention_back, g_heads)
    return (attended.reshape(count_q, -1), query_grad.reshape(count_q, -1), key_grad.reshape(count_k, -1), value_grad.reshape(count_k, -1))

def reference(queries, key_rows, value_rows, out_cotangent, gate_table, span_ids, noise_level, block_mask):
    full_width = HEADS * DH
    score_scale = 1.0 / math.sqrt(DH)
    q_size = min(512, WINDOW)
    k_size = WINDOW + q_size + SPAN
    token_level = jnp.take(noise_level, span_ids).astype(jnp.int32)
    level_onehot = (token_level[:, None] == jnp.arange(LEVELS, dtype=jnp.int32)[None, :]).astype(jnp.float32)
    gate_rows = jnp.dot(level_onehot, gate_table, precision=lax.Precision.HIGHEST)
    grad_attended = (gate_rows * out_cotangent.astype(jnp.float32)).astype(jnp.bfloat16)
    padding = ((WINDOW, SPAN), (0, 0))
    key_padded = jnp.pad(key_rows, padding)
    value_padded = jnp.pad(value_rows, padding)
    key_pos = jnp.arange(TOKENS + WINDOW + SPAN, dtype=jnp.int32) - WINDOW
    key_span = jnp.take(span_ids, jnp.clip(key_pos, 0, TOKENS - 1)).astype(jnp.int32)
    key_valid = (key_pos >= 0) & (key_pos < TOKENS)
    query_pos = jnp.arange(TOKENS, dtype=jnp.int32)

    def one_block(partials, offset):
        key_acc, value_acc = partials
        q_block = lax.dynamic_slice_in_dim(queries, offset, q_size, 0)
        g_block = lax.dynamic_slice_in_dim(grad_attended, offset, q_size, 0)
        k_block = lax.dynamic_slice_in_dim(key_padded, offset, k_size, 0)
        v_block = lax.dynamic_slice_in_dim(value_padded, offset, k_size, 0)
        span_q = lax.dynamic_slice_in_dim(span_ids, offset, q_size, 0)
        pos_q = lax.dynamic_slice_in_dim(query_pos, offset, q_size, 0)
        span_k = lax.dynamic_slice_in_dim(key_span, offset, k_size, 0)
        pos_k = lax.dynamic_slice_in_dim(key_pos, offset, k_size, 0)
        valid_k = lax.dynamic_slice_in_dim(key_valid, offset, k_size, 0)
        allowed = jnp.take(jnp.take(block_mask, span_q, axis=0), span_k, axis=1) == 1
        visible = allowed & (span_k[None, :] <= span_q[:, None]) & (pos_q[:, None] - pos_k[None, :] < WINDOW) & valid_k[None, :]
        attended, query_grad, key_grad, value_grad = attend(q_block, k_block, v_block, g_block, visible, score_scale)
        key_part = lax.dynamic_slice_in_dim(key_acc, offset, k_size, 0) + key_grad
        value_part = lax.dynamic_slice_in_dim(value_acc, offset, k_size, 0) + value_grad
        key_acc = lax.dynamic_update_slice_in_dim(key_acc, key_part, offset, 0)
        value_acc = lax.dynamic_update_slice_in_dim(value_acc, value_part, offset, 0)
        return ((key_acc, value_acc), (attended, query_grad))
    offsets = jnp.arange(0, TOKENS, q_size, dtype=jnp.int32)
    zero_rows = jnp.zeros((TOKENS + WINDOW + SPAN, full_width), jnp.float32)
    (key_acc, value_acc), (attended, query_grad) = lax.scan(one_block, (zero_rows, zero_rows), offsets)
    attended = attended.reshape(TOKENS, full_width)
    query_grad = query_grad.reshape(TOKENS, full_width)
    mixed_out = (gate_rows * attended.astype(jnp.float32)).astype(jnp.bfloat16)
    key_grad = key_acc[WINDOW:WINDOW + TOKENS].astype(jnp.bfloat16)
    value_grad = value_acc[WINDOW:WINDOW + TOKENS].astype(jnp.bfloat16)
    products = out_cotangent.astype(jnp.float32) * attended.astype(jnp.float32)
    gate_grad = jnp.dot(level_onehot.T, products, precision=lax.Precision.HIGHEST)
    return (mixed_out, query_grad, key_grad, value_grad, gate_grad)
```

```python
import functools
import math

import jax
import jax.numpy as jnp
from jax import lax
from jax.experimental import pallas as pl
from jax.experimental.pallas import tpu as pltpu
from jax.sharding import PartitionSpec as P

DH = 128
HIDDEN = -1e30
LOG2E = 1.4426950408889634


def other_ctx(c, near):
    odd = lax.rem(c, 2)
    return c + 1 - 2 * odd if near else c - 1 + 2 * odd


def prep_kernel(
    place_ref, span_ref, noise_ref, mask_ref, table_ref, bias_ref, gate_ref, slot_ref, *, sizes
):
    ctx_count, groups, rows, span_total, level_count, by_span = sizes
    c, h = place_ref[0], place_ref[1]
    tokens = groups * rows
    total = ctx_count * tokens
    bf16, f32 = jnp.bfloat16, jnp.float32

    def block_of(ctx, k):
        return ctx * groups + lax.rem(h - k + groups, groups)

    def spans_of(ctx, k):
        at = jnp.clip(ctx, 0, ctx_count - 1)
        return span_ref[pl.ds(block_of(at, k), 1), :]

    def as_column(row):
        return jnp.broadcast_to(row.astype(f32), (rows, rows)).T[:, :1].astype(jnp.int32)

    across = lax.broadcasted_iota(jnp.int32, (1, rows), 1)
    down = lax.broadcasted_iota(jnp.int32, (rows, 1), 0)
    span_lane = lax.broadcasted_iota(jnp.int32, (rows, span_total), 1)
    span_down = lax.broadcasted_iota(jnp.int32, (span_total, rows), 0)
    level_lane = lax.broadcasted_iota(jnp.int32, (rows, level_count), 1)
    query_span = [spans_of(c, k) for k in range(groups)]
    query_pos = [block_of(c, k) * rows + across for k in range(groups)]
    mask_low = mask_ref[...].astype(bf16)
    allowed_q = [
        lax.dot_general(
            mask_low,
            (span_down == row).astype(bf16),
            (((0,), (0,)), ((), ())),
            preferred_element_type=f32,
        ).astype(bf16)
        for row in query_span
    ]
    noise = noise_ref[...].astype(f32)
    for i, ctx in enumerate((c, other_ctx(c, True), other_ctx(c, False))):
        for k in range(groups):
            key_span = as_column(spans_of(ctx, k))
            key_pos = block_of(ctx, k) * rows + down
            valid = (key_pos >= 0) & (key_pos < total)
            onehot = key_span == span_lane
            at = slice((i * groups + k) * rows, (i * groups + k + 1) * rows)
            for p in range(groups):
                allowed = jnp.dot(
                    onehot.astype(bf16), allowed_q[p], preferred_element_type=f32
                )
                visible = (
                    (allowed > 0.5)
                    & (key_span <= query_span[p])
                    & (query_pos[p] - key_pos < tokens)
                    & valid
                )
                bias_ref[at, p * rows : (p + 1) * rows] = jnp.where(visible, 0.0, HIDDEN)
            if i > 0:
                continue
            level = jnp.sum(jnp.where(onehot, noise, 0.0), axis=1, keepdims=True)
            level_onehot = (level.astype(jnp.int32) == level_lane).astype(f32)
            gate_ref[at, :] = jnp.dot(
                level_onehot,
                table_ref[...],
                precision=lax.Precision.HIGHEST,
                preferred_element_type=f32,
            )
            if by_span:
                slot_ref[:, at] = (span_down == query_span[k]).astype(bf16)
            else:
                slot_ref[:, at] = level_onehot.T.astype(bf16)


def attention_kernel(
    place_ref,
    q_ref, k_ref, v_ref, o_ref,
    qo_ref, kv_ref,
    near_own_ref, near_far_ref, side_own_ref, side_far_ref,
    gate_ref, bias_ref, slot_ref,
    mixed_ref, dq_ref, back_ref,
    own_ref, far_ref, near_ref, side_grad_own_ref, side_grad_far_ref,
    sums_ref,
    *, rows, tokens, q_size, heads,
):
    scale = 1.0 / math.sqrt(DH)
    bf16, f32 = jnp.bfloat16, jnp.float32
    tile = 32

    def dot(left, right, left_dim, right_dim):
        return lax.dot_general(
            left, right, (((left_dim,), (right_dim,)), ((), ())), preferred_element_type=f32
        )

    def load(j):
        at = slice(j * DH, (j + 1) * DH)
        keys, values = [k_ref[:, at], kv_ref[0, :, at]], [v_ref[:, at], kv_ref[1, :, at]]
        for ref in (near_own_ref, near_far_ref, side_own_ref, side_far_ref):
            keys.append(ref[0, :, at])
            values.append(ref[1, :, at])
        keys, values = jnp.concatenate(keys, axis=0), jnp.concatenate(values, axis=0)
        queries = jnp.concatenate([q_ref[:, at], qo_ref[0, :, at]], axis=0)
        cotangent = jnp.concatenate([o_ref[:, at], qo_ref[1, :, at]], axis=0)
        blocks = []
        for start in range(0, tokens, q_size):
            span = slice(start, start + q_size)
            q, o = queries[span], cotangent[span].astype(f32)
            gate = gate_ref[span, at]
            g = (gate * o).astype(bf16)
            blocks.append((q, o, gate, g, dot(keys, q, 1, 1), dot(values, g, 1, 1)))
        return keys, values, blocks

    def work(j, keys, values, blocks):
        at = slice(j * DH, (j + 1) * DH)
        keys_t, values_t = keys.T, values.T
        key_grad = value_grad = sums = None
        for number, (q, o, gate, g, scores, prob_grad) in enumerate(blocks):
            start = number * q_size
            span = slice(start, start + q_size)
            count = scores.shape[0]
            tiles = [slice(r, r + tile) for r in range(0, count, tile)]
            raised, top = [], None
            for t in tiles:
                part = scores[t] * (scale * LOG2E) + bias_ref[t, span]
                raised.append(part)
                high = jnp.max(part.reshape(tile // 8, 8, q_size), axis=0)
                top = high if top is None else jnp.maximum(top, high)
            top = jnp.max(top, axis=0, keepdims=True)
            total = None
            for i in range(len(tiles)):
                raised[i] = jnp.exp2(raised[i] - top)
                part = jnp.sum(raised[i].reshape(tile // 8, 8, q_size), axis=0)
                total = part if total is None else total + part
            inverse = 1.0 / jnp.sum(total, axis=0, keepdims=True)
            low = jnp.concatenate([(part * inverse).astype(bf16) for part in raised], axis=0)
            attended_t = dot(values_t, low, 1, 0).astype(bf16)
            row_dot = jnp.sum(g.T.astype(f32) * attended_t.astype(f32), axis=0, keepdims=True)
            attended = attended_t.T.astype(f32)
            score_grad = jnp.concatenate(
                [
                    (part * ((prob_grad[t] - row_dot) * inverse)).astype(bf16)
                    for part, t in zip(raised, tiles)
                ],
                axis=0,
            )
            query_grad = (dot(keys_t, score_grad, 1, 0) * scale).astype(bf16).T
            mixed = (gate * attended).astype(bf16)
            if start == 0:
                mixed_ref[:, at] = mixed[:rows]
                dq_ref[:, at] = query_grad[:rows]
                back_ref[0, : q_size - rows, at] = mixed[rows:]
                back_ref[1, : q_size - rows, at] = query_grad[rows:]
            else:
                back_ref[0, start - rows : start - rows + q_size, at] = mixed
                back_ref[1, start - rows : start - rows + q_size, at] = query_grad
            dk, dv = dot(score_grad, q, 1, 0), dot(low, g, 1, 0)
            product = o * attended
            high = product.astype(bf16)
            rest = (product - high.astype(f32)).astype(bf16)
            both = dot(slot_ref[:, span], jnp.concatenate([high, rest], axis=1), 1, 0)
            part = both[:, :DH] + both[:, DH:]
            key_grad = dk if key_grad is None else key_grad + dk
            value_grad = dv if value_grad is None else value_grad + dv
            sums = part if sums is None else sums + part
        sums_ref[:, at] = sums
        for i, grad in ((0, key_grad * scale), (1, value_grad)):
            own_ref[i, :, at] = grad[:rows]
            far_ref[i, :, at] = grad[rows:tokens]
            low = grad[tokens:].astype(bf16)
            near_ref[i, :, at] = low[:tokens]
            side_grad_own_ref[i, :, at] = low[tokens : tokens + rows]
            side_grad_far_ref[i, :, at] = low[tokens + rows :]

    ready = load(0)
    for j in range(heads):
        following = load(j + 1) if j + 1 < heads else None
        work(j, *ready)
        ready = following


def per_device(
    queries, key_rows, value_rows, out_cotangent, gate_table, span_ids, noise_level, block_mask
):
    groups = lax.axis_size("head")
    ctx_count = lax.axis_size("ctx")
    rows, full_width = queries.shape
    width = full_width // groups
    heads = width // DH
    tokens = rows * groups
    far_rows = tokens - rows
    span_total = noise_level.shape[0]
    level_count = gate_table.shape[0]
    by_span = span_total <= level_count // 2
    slots = span_total if by_span else level_count
    c = lax.axis_index("ctx")
    h = lax.axis_index("head")
    place = jnp.stack([c, h]).astype(jnp.int32)
    bf16, f32 = jnp.bfloat16, jnp.float32

    near_pairs = [(i, i ^ 1) for i in range(ctx_count)]
    side_pairs = [
        (i, i - 1 + 2 * (i % 2)) for i in range(ctx_count) if 0 <= i - 1 + 2 * (i % 2) < ctx_count
    ]

    def columns(array, group):
        return lax.dynamic_slice_in_dim(array, group * width, width, 1)

    def to_peers(first, second, after=None):
        parts = []
        for k in range(1, groups):
            group = lax.rem(h + k, groups)
            slab = jnp.stack([columns(first, group), columns(second, group)])
            if after is not None:
                slab, _ = lax.optimization_barrier((slab, after))
            pairs = [(i, (i + k) % groups) for i in range(groups)]
            parts.append(lax.ppermute(slab, "head", pairs))
        return parts[0] if groups == 2 else jnp.concatenate(parts, axis=1)

    def from_peers(slab):
        parts = []
        for k in range(1, groups):
            part = slab if groups == 2 else slab[:, (k - 1) * rows : k * rows]
            pairs = [(i, (i - k) % groups) for i in range(groups)]
            parts.append(lax.ppermute(part, "head", pairs))
        return parts

    kv_far = to_peers(key_rows, value_rows)
    kv_own = jnp.stack([columns(key_rows, h), columns(value_rows, h)])
    side_own = lax.ppermute(kv_own, "ctx", side_pairs)
    near_own = lax.ppermute(kv_own, "ctx", near_pairs)
    side_far = lax.ppermute(kv_far, "ctx", side_pairs)
    near_far = lax.ppermute(kv_far, "ctx", near_pairs)
    qo_far = to_peers(queries, out_cotangent, kv_far)

    limit = (28 if tokens <= 256 else 56) * 1024 * 1024
    params = pltpu.CompilerParams(vmem_limit_bytes=limit)
    sizes = (ctx_count, groups, rows, span_total, level_count, by_span)
    whole = lambda shape: pl.BlockSpec(shape, lambda i, place: (0,) * len(shape))
    bias, gate, slot = pl.pallas_call(
        functools.partial(prep_kernel, sizes=sizes),
        grid_spec=pltpu.PrefetchScalarGridSpec(
            num_scalar_prefetch=1,
            grid=(1,),
            in_specs=[
                whole((ctx_count * groups, rows)),
                whole((1, span_total)),
                whole((span_total, span_total)),
                pl.BlockSpec((level_count, width), lambda i, place: (0, place[1])),
            ],
            out_specs=[
                whole((3 * tokens, tokens)),
                whole((tokens, width)),
                whole((slots, tokens)),
            ],
        ),
        out_shape=[
            jax.ShapeDtypeStruct((3 * tokens, tokens), f32),
            jax.ShapeDtypeStruct((tokens, width), f32),
            jax.ShapeDtypeStruct((slots, tokens), bf16),
        ],
        compiler_params=params,
        name="prep",
    )(
        place,
        span_ids.reshape(ctx_count * groups, rows),
        noise_level.reshape(1, span_total),
        block_mask,
        gate_table,
    )

    batch = next(n for n in (4, 3, 2, 1) if heads % n == 0) if tokens <= 256 else 1
    steps = heads // batch
    own_block = pl.BlockSpec((rows, batch * DH), lambda i, place: (0, place[1] * steps + i))
    pair = lambda count: pl.BlockSpec((2, count, batch * DH), lambda i, place: (0, 0, i))
    column = lambda count: pl.BlockSpec((count, batch * DH), lambda i, place: (0, i))
    q_size = min(256, tokens)
    flops = 6 * 2 * tokens * 3 * tokens * DH * heads
    (mixed, query_grad, back, own, far, near_grad, side_grad_own, side_grad_far, sums) = (
        pl.pallas_call(
            functools.partial(
                attention_kernel, rows=rows, tokens=tokens, q_size=q_size, heads=batch
            ),
            grid_spec=pltpu.PrefetchScalarGridSpec(
                num_scalar_prefetch=1,
                grid=(steps,),
                in_specs=[
                    own_block, own_block, own_block, own_block,
                    pair(far_rows), pair(far_rows),
                    pair(rows), pair(far_rows), pair(rows), pair(far_rows),
                    column(tokens), whole((3 * tokens, tokens)), whole((slots, tokens)),
                ],
                out_specs=[
                    own_block, own_block, pair(far_rows),
                    pair(rows), pair(far_rows), pair(tokens), pair(rows), pair(far_rows),
                    column(slots),
                ],
            ),
            out_shape=[
                jax.ShapeDtypeStruct((rows, full_width), bf16),
                jax.ShapeDtypeStruct((rows, full_width), bf16),
                jax.ShapeDtypeStruct((2, far_rows, width), bf16),
                jax.ShapeDtypeStruct((2, rows, width), f32),
                jax.ShapeDtypeStruct((2, far_rows, width), f32),
                jax.ShapeDtypeStruct((2, tokens, width), bf16),
                jax.ShapeDtypeStruct((2, rows, width), bf16),
                jax.ShapeDtypeStruct((2, far_rows, width), bf16),
                jax.ShapeDtypeStruct((slots, width), f32),
            ],
            compiler_params=params,
            cost_estimate=pl.CostEstimate(
                flops=flops, bytes_accessed=16 * tokens * width, transcendentals=0
            ),
            name="attention",
        )(
            place,
            queries, key_rows, value_rows, out_cotangent,
            qo_far, kv_far,
            near_own, near_far, side_own, side_far,
            gate, bias, slot,
        )
    )

    side_back_far = lax.ppermute(side_grad_far, "ctx", side_pairs)
    near_back = lax.ppermute(near_grad, "ctx", near_pairs)
    back_parts = from_peers(back)
    side_back_own = lax.ppermute(side_grad_own, "ctx", side_pairs)
    far_sum = lax.optimization_barrier(far + near_back[:, rows:].astype(f32))
    far_grad = (far_sum + side_back_far.astype(f32)).astype(bf16)
    grad_parts = from_peers(far_grad)
    own_grad = (
        own + near_back[:, :rows].astype(f32) + side_back_own.astype(f32)
    ).astype(bf16)

    slot_sums = sums
    for step in (1 << n for n in range(ctx_count.bit_length() - 1)):
        pairs = [(i, i ^ step) for i in range(ctx_count)]
        slot_sums = slot_sums + lax.ppermute(slot_sums, "ctx", pairs)
    for step in (1 << n for n in range(groups.bit_length() - 1)):
        pairs = [(i, i ^ step) for i in range(groups)]
        other = lax.ppermute(slot_sums, "head", pairs)
        slot_sums = jnp.where(
            (h // step) % 2 == 0,
            jnp.concatenate([slot_sums, other], axis=1),
            jnp.concatenate([other, slot_sums], axis=1),
        )
    if by_span:
        level_onehot = (
            jnp.arange(level_count, dtype=jnp.int32)[:, None] == noise_level[None, :]
        ).astype(f32)
        gate_grad = jnp.dot(level_onehot, slot_sums, precision=lax.Precision.HIGHEST)
    else:
        gate_grad = slot_sums

    def placed(array, part, k):
        group = lax.rem(h + k, groups)
        return lax.dynamic_update_slice_in_dim(array, part, group * width, 1)

    key_grad = placed(jnp.zeros((rows, full_width), bf16), own_grad[0], 0)
    value_grad = placed(jnp.zeros((rows, full_width), bf16), own_grad[1], 0)
    for k in range(1, groups):
        mixed = placed(mixed, back_parts[k - 1][0], k)
        query_grad = placed(query_grad, back_parts[k - 1][1], k)
        key_grad = placed(key_grad, grad_parts[k - 1][0], k)
        value_grad = placed(value_grad, grad_parts[k - 1][1], k)
    return (mixed, query_grad, key_grad, value_grad, gate_grad)


def solution(mesh):
    sharded = P(("ctx", "head"), None)
    return jax.shard_map(
        per_device,
        mesh=mesh,
        in_specs=(sharded,) * 4 + (P(),) * 4,
        out_specs=(sharded,) * 4 + (P(),),
        check_vma=False,
    )
```

```python
import functools
import math

import jax
import jax.numpy as jnp
from jax import lax
from jax.experimental import pallas as pl
from jax.experimental.pallas import tpu as pltpu
from jax.sharding import PartitionSpec as P

DH = 128
HIDDEN = -1e30
LOG2E = 1.4426950408889634


def other_ctx(c, near):
    odd = lax.rem(c, 2)
    return c + 1 - 2 * odd if near else c - 1 + 2 * odd


def prep_kernel(
    place_ref, span_ref, noise_ref, mask_ref, table_ref, bias_ref, gate_ref, slot_ref, *, sizes
):
    ctx_count, groups, rows, span_total, level_count, by_span = sizes
    c, h = place_ref[0], place_ref[1]
    tokens = groups * rows
    total = ctx_count * tokens
    bf16, f32 = jnp.bfloat16, jnp.float32

    def block_of(ctx, k):
        return ctx * groups + lax.rem(h - k + groups, groups)

    def spans_of(ctx, k):
        at = jnp.clip(ctx, 0, ctx_count - 1)
        return span_ref[pl.ds(block_of(at, k), 1), :]

    def as_column(row):
        return jnp.broadcast_to(row.astype(f32), (rows, rows)).T[:, :1].astype(jnp.int32)

    across = lax.broadcasted_iota(jnp.int32, (1, rows), 1)
    down = lax.broadcasted_iota(jnp.int32, (rows, 1), 0)
    span_lane = lax.broadcasted_iota(jnp.int32, (rows, span_total), 1)
    span_down = lax.broadcasted_iota(jnp.int32, (span_total, rows), 0)
    level_lane = lax.broadcasted_iota(jnp.int32, (rows, level_count), 1)
    query_span = [spans_of(c, k) for k in range(groups)]
    query_pos = [block_of(c, k) * rows + across for k in range(groups)]
    mask_low = mask_ref[...].astype(bf16)
    allowed_q = [
        lax.dot_general(
            mask_low,
            (span_down == row).astype(bf16),
            (((0,), (0,)), ((), ())),
            preferred_element_type=f32,
        ).astype(bf16)
        for row in query_span
    ]
    noise = noise_ref[...].astype(f32)
    for i, ctx in enumerate((c, other_ctx(c, True), other_ctx(c, False))):
        for k in range(groups):
            key_span = as_column(spans_of(ctx, k))
            key_pos = block_of(ctx, k) * rows + down
            valid = (key_pos >= 0) & (key_pos < total)
            onehot = key_span == span_lane
            at = slice((i * groups + k) * rows, (i * groups + k + 1) * rows)
            for p in range(groups):
                allowed = jnp.dot(
                    onehot.astype(bf16), allowed_q[p], preferred_element_type=f32
                )
                visible = (
                    (allowed > 0.5)
                    & (key_span <= query_span[p])
                    & (query_pos[p] - key_pos < tokens)
                    & valid
                )
                bias_ref[at, p * rows : (p + 1) * rows] = jnp.where(visible, 0.0, HIDDEN)
            if i > 0:
                continue
            level = jnp.sum(jnp.where(onehot, noise, 0.0), axis=1, keepdims=True)
            level_onehot = (level.astype(jnp.int32) == level_lane).astype(f32)
            gate_ref[at, :] = jnp.dot(
                level_onehot,
                table_ref[...],
                precision=lax.Precision.HIGHEST,
                preferred_element_type=f32,
            )
            if by_span:
                slot_ref[:, at] = (span_down == query_span[k]).astype(bf16)
            else:
                slot_ref[:, at] = level_onehot.T.astype(bf16)


def attention_kernel(
    place_ref,
    qo_own_ref, kv_own_ref, qo_ref, kv_ref,
    near_own_ref, near_far_ref, side_own_ref, side_far_ref,
    gate_ref, bias_ref, slot_ref,
    *rest, rows, tokens, q_size, heads,
):
    (
        back_ref, side_grad_far_ref, mixed_ref, dq_ref, own_ref, far_ref,
        near_grad_own_ref, near_grad_far_ref, side_grad_own_ref, sums_ref,
    ) = rest[-10:]
    scale = 1.0 / math.sqrt(DH)
    bf16, f32 = jnp.bfloat16, jnp.float32
    tile = 32

    def dot(left, right, left_dim, right_dim):
        return lax.dot_general(
            left, right, (((left_dim,), (right_dim,)), ((), ())), preferred_element_type=f32
        )

    def load(j):
        at = slice(j * DH, (j + 1) * DH)
        keys, values = [], []
        for ref in (
            kv_own_ref, kv_ref, near_own_ref, near_far_ref, side_own_ref, side_far_ref
        ):
            keys.append(ref[0, :, at])
            values.append(ref[1, :, at])
        keys, values = jnp.concatenate(keys, axis=0), jnp.concatenate(values, axis=0)
        queries = jnp.concatenate([qo_own_ref[0, :, at], qo_ref[0, :, at]], axis=0)
        cotangent = jnp.concatenate([qo_own_ref[1, :, at], qo_ref[1, :, at]], axis=0)
        blocks = []
        for start in range(0, tokens, q_size):
            span = slice(start, start + q_size)
            q, o = queries[span], cotangent[span].astype(f32)
            gate = gate_ref[span, at]
            g = (gate * o).astype(bf16)
            blocks.append((q, o, gate, g, dot(keys, q, 1, 1), dot(values, g, 1, 1)))
        return keys, values, blocks

    def work(j, keys, values, blocks):
        at = slice(j * DH, (j + 1) * DH)
        keys_t, values_t = keys.T, values.T
        key_grad = value_grad = sums = None
        for number, (q, o, gate, g, scores, prob_grad) in enumerate(blocks):
            start = number * q_size
            span = slice(start, start + q_size)
            count = scores.shape[0]
            tiles = [slice(r, r + tile) for r in range(0, count, tile)]
            raised, top = [], None
            for t in tiles:
                part = scores[t] * (scale * LOG2E) + bias_ref[t, span]
                raised.append(part)
                high = jnp.max(part.reshape(tile // 8, 8, q_size), axis=0)
                top = high if top is None else jnp.maximum(top, high)
            top = jnp.max(top, axis=0, keepdims=True)
            total = None
            for i in range(len(tiles)):
                raised[i] = jnp.exp2(raised[i] - top)
                part = jnp.sum(raised[i].reshape(tile // 8, 8, q_size), axis=0)
                total = part if total is None else total + part
            inverse = 1.0 / jnp.sum(total, axis=0, keepdims=True)
            low = jnp.concatenate([(part * inverse).astype(bf16) for part in raised], axis=0)
            attended_t = dot(values_t, low, 1, 0).astype(bf16)
            row_dot = jnp.sum(g.T.astype(f32) * attended_t.astype(f32), axis=0, keepdims=True)
            attended = attended_t.T.astype(f32)
            score_grad = jnp.concatenate(
                [
                    (part * ((prob_grad[t] - row_dot) * inverse)).astype(bf16)
                    for part, t in zip(raised, tiles)
                ],
                axis=0,
            )
            query_grad = (dot(keys_t, score_grad, 1, 0) * scale).astype(bf16).T
            mixed = (gate * attended).astype(bf16)
            if start == 0:
                mixed_ref[:, at] = mixed[:rows]
                dq_ref[:, at] = query_grad[:rows]
                back_ref[0, : q_size - rows, at] = mixed[rows:]
                back_ref[1, : q_size - rows, at] = query_grad[rows:]
            else:
                back_ref[0, start - rows : start - rows + q_size, at] = mixed
                back_ref[1, start - rows : start - rows + q_size, at] = query_grad
            dk, dv = dot(score_grad, q, 1, 0), dot(low, g, 1, 0)
            product = o * attended
            high = product.astype(bf16)
            rest = (product - high.astype(f32)).astype(bf16)
            both = dot(slot_ref[:, span], jnp.concatenate([high, rest], axis=1), 1, 0)
            part = both[:, :DH] + both[:, DH:]
            key_grad = dk if key_grad is None else key_grad + dk
            value_grad = dv if value_grad is None else value_grad + dv
            sums = part if sums is None else sums + part
        sums_ref[:, at] = sums
        for i, grad in ((0, key_grad * scale), (1, value_grad)):
            own_ref[i, :, at] = grad[:rows]
            far_ref[i, :, at] = grad[rows:tokens]
            low = grad[tokens:].astype(bf16)
            near_grad_own_ref[i, :, at] = low[:rows]
            near_grad_far_ref[i, :, at] = low[rows:tokens]
            side_grad_own_ref[i, :, at] = low[tokens : tokens + rows]
            side_grad_far_ref[i, :, at] = low[tokens + rows :]

    ready = load(0)
    for j in range(heads):
        following = load(j + 1) if j + 1 < heads else None
        work(j, *ready)
        ready = following


def far_sum_kernel(part_ref, near_ref, side_ref, out_ref):
    total = part_ref[...] + near_ref[...].astype(jnp.float32) + side_ref[...].astype(jnp.float32)
    out_ref[...] = total.astype(out_ref.dtype)


def own_sum_kernel(place_ref, part_ref, near_ref, side_ref, key_ref, value_ref):
    total = part_ref[...] + near_ref[...].astype(jnp.float32) + side_ref[...].astype(jnp.float32)
    key_ref[...] = total[0].astype(key_ref.dtype)
    value_ref[...] = total[1].astype(value_ref.dtype)


def put_kernel(place_ref, part_ref, first_in, second_in, first_ref, second_ref):
    first_ref[...] = part_ref[0]
    second_ref[...] = part_ref[1]


def per_device(
    queries, key_rows, value_rows, out_cotangent, gate_table, span_ids, noise_level, block_mask
):
    groups = lax.axis_size("head")
    ctx_count = lax.axis_size("ctx")
    rows, full_width = queries.shape
    width = full_width // groups
    heads = width // DH
    tokens = rows * groups
    far_rows = tokens - rows
    parts = 2 if heads % 2 == 0 else 1
    part_width = width // parts
    part_heads = heads // parts
    span_total = noise_level.shape[0]
    level_count = gate_table.shape[0]
    by_span = span_total <= level_count // 2
    slots = span_total if by_span else level_count
    c = lax.axis_index("ctx")
    h = lax.axis_index("head")
    place = jnp.stack([c, h]).astype(jnp.int32)
    bf16, f32 = jnp.bfloat16, jnp.float32
    tie = lax.optimization_barrier

    near_pairs = [(i, i ^ 1) for i in range(ctx_count)]
    side_of = [i - 1 + 2 * (i % 2) for i in range(ctx_count)]
    side_pairs = [(i, j if 0 <= j < ctx_count else i) for i, j in enumerate(side_of)]

    def columns(array, group, part=None):
        start, size = group * width, width
        if part is not None:
            start, size = start + part * part_width, part_width
        return lax.dynamic_slice_in_dim(array, start, size, 1)

    def to_peers(first, second, part=None, after=None):
        arrived = []
        for k in range(1, groups):
            group = lax.rem(h + k, groups)
            slab = jnp.stack([columns(first, group, part), columns(second, group, part)])
            if after is not None:
                slab, _ = tie((slab, after))
            pairs = [(i, (i + k) % groups) for i in range(groups)]
            arrived.append(lax.ppermute(slab, "head", pairs))
        return arrived[0] if groups == 2 else jnp.concatenate(arrived, axis=1)

    def from_peers(slab):
        arrived = []
        for k in range(1, groups):
            part = slab if groups == 2 else slab[:, (k - 1) * rows : k * rows]
            pairs = [(i, (i - k) % groups) for i in range(groups)]
            arrived.append(lax.ppermute(part, "head", pairs))
        return arrived

    kv_own = jnp.stack([columns(key_rows, h), columns(value_rows, h)])
    side_own = lax.ppermute(kv_own, "ctx", side_pairs)
    kv_far = to_peers(key_rows, value_rows)
    near_own = lax.ppermute(kv_own, "ctx", near_pairs)
    near_far = lax.ppermute(kv_far, "ctx", near_pairs)
    qo_own = jnp.stack([columns(queries, h), columns(out_cotangent, h)])
    side_far, qo_far = [], []
    side_after, qo_after = None, kv_far
    for p in range(parts):
        piece = kv_far[:, :, p * part_width : (p + 1) * part_width]
        if side_after is not None:
            piece, _ = tie((piece, side_after))
        side_after = lax.ppermute(piece, "ctx", side_pairs)
        side_far.append(side_after)
        qo_after = to_peers(queries, out_cotangent, p, qo_after)
        qo_far.append(qo_after)

    limit = (30 if tokens <= 256 else 56) * 1024 * 1024
    params = pltpu.CompilerParams(vmem_limit_bytes=limit)
    small = pltpu.CompilerParams(vmem_limit_bytes=(12 if tokens <= 256 else 36) * 1024 * 1024)
    sizes = (ctx_count, groups, rows, span_total, level_count, by_span)
    whole = lambda shape: pl.BlockSpec(shape, lambda i, place: (0,) * len(shape))
    bias, gate, slot = pl.pallas_call(
        functools.partial(prep_kernel, sizes=sizes),
        grid_spec=pltpu.PrefetchScalarGridSpec(
            num_scalar_prefetch=1,
            grid=(1,),
            in_specs=[
                whole((ctx_count * groups, rows)),
                whole((1, span_total)),
                whole((span_total, span_total)),
                pl.BlockSpec((level_count, width), lambda i, place: (0, place[1])),
            ],
            out_specs=[
                whole((3 * tokens, tokens)),
                whole((tokens, width)),
                whole((slots, tokens)),
            ],
        ),
        out_shape=[
            jax.ShapeDtypeStruct((3 * tokens, tokens), f32),
            jax.ShapeDtypeStruct((tokens, width), f32),
            jax.ShapeDtypeStruct((slots, tokens), bf16),
        ],
        compiler_params=small,
        name="prep",
    )(
        place,
        span_ids.reshape(ctx_count * groups, rows),
        noise_level.reshape(1, span_total),
        block_mask,
        gate_table,
    )

    batch = next(n for n in (3, 2, 1) if part_heads % n == 0) if tokens <= 256 else 1
    steps = part_heads // batch
    block = batch * DH
    q_size = min(256, tokens)
    flops = 6 * 2 * tokens * 3 * tokens * DH * part_heads

    def attention(p, joint):
        pair = lambda count: pl.BlockSpec((2, count, block), lambda i, place: (0, 0, i))
        at_part = lambda count: pl.BlockSpec(
            (2, count, block), lambda i, place: (0, 0, p * steps + i)
        )
        at_head = pl.BlockSpec(
            (rows, block), lambda i, place: (0, (place[1] * parts + p) * steps + i)
        )
        column = lambda count: pl.BlockSpec((count, block), lambda i, place: (0, p * steps + i))
        struct = jax.ShapeDtypeStruct
        inputs = [
            qo_own, kv_own, qo_far[p], kv_far, near_own, near_far, side_own, side_far[p],
            gate, bias, slot,
        ]
        return pl.pallas_call(
            functools.partial(
                attention_kernel, rows=rows, tokens=tokens, q_size=q_size, heads=batch
            ),
            grid_spec=pltpu.PrefetchScalarGridSpec(
                num_scalar_prefetch=1,
                grid=(steps,),
                in_specs=[
                    at_part(rows), at_part(rows), pair(far_rows), at_part(far_rows),
                    at_part(rows), at_part(far_rows), at_part(rows), pair(far_rows),
                    column(tokens), whole((3 * tokens, tokens)), whole((slots, tokens)),
                ]
                + [pl.BlockSpec(memory_space=pl.ANY)] * len(joint),
                out_specs=[
                    pair(far_rows), pair(far_rows),
                    at_head, at_head, at_part(rows), at_part(far_rows),
                    at_part(rows), at_part(far_rows), at_part(rows), column(slots),
                ],
            ),
            out_shape=[
                struct((2, far_rows, part_width), bf16),
                struct((2, far_rows, part_width), bf16),
                struct((rows, full_width), bf16),
                struct((rows, full_width), bf16),
                struct((2, rows, width), f32),
                struct((2, far_rows, width), f32),
                struct((2, rows, width), bf16),
                struct((2, far_rows, width), bf16),
                struct((2, rows, width), bf16),
                struct((slots, width), f32),
            ],
            input_output_aliases={1 + len(inputs) + i: 2 + i for i in range(len(joint))},
            compiler_params=params,
            cost_estimate=pl.CostEstimate(
                flops=flops, bytes_accessed=16 * tokens * part_width, transcendentals=0
            ),
            name="attention",
        )(place, *inputs, *joint)

    joint, back_far, side_back_far = (), [], []
    for p in range(parts):
        back, side_grad_far, *joint = attention(p, joint)
        if p > 0:
            back, side_grad_far, joint, back_far, side_back_far = tie(
                (back, side_grad_far, joint, back_far, side_back_far)
            )
        side_back_far.append(lax.ppermute(side_grad_far, "ctx", side_pairs))
        back_far.append(from_peers(back))
    mixed, query_grad, own, far, near_grad_own, near_grad_far, side_grad_own, sums = joint

    near_back_far = lax.ppermute(near_grad_far, "ctx", near_pairs)
    near_back_own = lax.ppermute(near_grad_own, "ctx", near_pairs)
    side_grad_own, _ = tie((side_grad_own, side_back_far[-1]))
    side_back_own = lax.ppermute(side_grad_own, "ctx", side_pairs)
    grad_far = []
    for p in range(parts):
        at_part = pl.BlockSpec((2, far_rows, part_width), lambda i, p=p: (0, 0, p))
        alone = pl.BlockSpec((2, far_rows, part_width), lambda i: (0, 0, 0))
        far_grad = pl.pallas_call(
            far_sum_kernel,
            grid=(1,),
            in_specs=[at_part, at_part, alone],
            out_specs=alone,
            out_shape=jax.ShapeDtypeStruct((2, far_rows, part_width), bf16),
            compiler_params=small,
            name="far_sum",
        )(far, near_back_far, side_back_far[p])
        grad_far.append(from_peers(far_grad))
    key_grad, value_grad = pl.pallas_call(
        own_sum_kernel,
        grid_spec=pltpu.PrefetchScalarGridSpec(
            num_scalar_prefetch=1,
            grid=(parts,),
            in_specs=[pl.BlockSpec((2, rows, part_width), lambda i, place: (0, 0, i))] * 3,
            out_specs=[
                pl.BlockSpec((rows, part_width), lambda i, place: (0, place[1] * parts + i))
            ]
            * 2,
        ),
        out_shape=[jax.ShapeDtypeStruct((rows, full_width), bf16)] * 2,
        compiler_params=small,
        name="own_sum",
    )(place, own, near_back_own, side_back_own)

    slot_sums = sums
    steps_of_two = [1 << n for n in range(ctx_count.bit_length() - 1)]
    for step in steps_of_two[:1] + steps_of_two[2:] + steps_of_two[1:2]:
        pairs = [(i, i ^ step) for i in range(ctx_count)]
        slot_sums = slot_sums + lax.ppermute(slot_sums, "ctx", pairs)
    for step in (1 << n for n in range(groups.bit_length() - 1)):
        pairs = [(i, i ^ step) for i in range(groups)]
        other = lax.ppermute(slot_sums, "head", pairs)
        slot_sums = jnp.where(
            (h // step) % 2 == 0,
            jnp.concatenate([slot_sums, other], axis=1),
            jnp.concatenate([other, slot_sums], axis=1),
        )
    if by_span:
        level_onehot = (
            jnp.arange(level_count, dtype=jnp.int32)[:, None] == noise_level[None, :]
        ).astype(f32)
        gate_grad = jnp.dot(level_onehot, slot_sums, precision=lax.Precision.HIGHEST)
    else:
        gate_grad = slot_sums

    def put(first, second, arrived, k, p):
        out = pl.BlockSpec(
            (rows, part_width),
            lambda i, place: (0, lax.rem(place[1] + k, groups) * parts + p),
        )
        anywhere = pl.BlockSpec(memory_space=pl.ANY)
        return pl.pallas_call(
            put_kernel,
            grid_spec=pltpu.PrefetchScalarGridSpec(
                num_scalar_prefetch=1,
                grid=(1,),
                in_specs=[whole((2, rows, part_width)), anywhere, anywhere],
                out_specs=[out, out],
            ),
            out_shape=[jax.ShapeDtypeStruct((rows, full_width), bf16)] * 2,
            input_output_aliases={2: 0, 3: 1},
            compiler_params=small,
            name="put",
        )(place, arrived, first, second)

    for p in range(parts):
        for k in range(1, groups):
            mixed, query_grad = put(mixed, query_grad, back_far[p][k - 1], k, p)
            key_grad, value_grad = put(key_grad, value_grad, grad_far[p][k - 1], k, p)
    return (mixed, query_grad, key_grad, value_grad, gate_grad)


def solution(mesh):
    sharded = P(("ctx", "head"), None)
    return jax.shard_map(
        per_device,
        mesh=mesh,
        in_specs=(sharded,) * 4 + (P(),) * 4,
        out_specs=(sharded,) * 4 + (P(),),
        check_vma=False,
    )
```

```python
import functools
import math

import jax
import jax.numpy as jnp
from jax import lax
from jax.experimental import pallas as pl
from jax.experimental.pallas import tpu as pltpu
from jax.sharding import PartitionSpec as P

DH = 128
HIDDEN = -1e30
LOG2E = 1.4426950408889634


def other_ctx(c, near):
    odd = lax.rem(c, 2)
    return c + 1 - 2 * odd if near else c - 1 + 2 * odd


def prep_kernel(
    place_ref, span_ref, noise_ref, mask_ref, table_ref, bias_ref, gate_ref, slot_ref, *, sizes
):
    ctx_count, groups, rows, span_total, level_count, by_span = sizes
    c, h = place_ref[0], place_ref[1]
    tokens = groups * rows
    total = ctx_count * tokens
    bf16, f32 = jnp.bfloat16, jnp.float32

    def block_of(ctx, k):
        return ctx * groups + lax.rem(h - k + groups, groups)

    def spans_of(ctx, k):
        at = jnp.clip(ctx, 0, ctx_count - 1)
        return span_ref[pl.ds(block_of(at, k), 1), :]

    def as_column(row):
        return jnp.broadcast_to(row.astype(f32), (rows, rows)).T[:, :1].astype(jnp.int32)

    across = lax.broadcasted_iota(jnp.int32, (1, rows), 1)
    down = lax.broadcasted_iota(jnp.int32, (rows, 1), 0)
    span_lane = lax.broadcasted_iota(jnp.int32, (rows, span_total), 1)
    span_down = lax.broadcasted_iota(jnp.int32, (span_total, rows), 0)
    level_lane = lax.broadcasted_iota(jnp.int32, (rows, level_count), 1)
    query_span = [spans_of(c, k) for k in range(groups)]
    query_pos = [block_of(c, k) * rows + across for k in range(groups)]
    mask_low = mask_ref[...].astype(bf16)
    allowed_q = [
        lax.dot_general(
            mask_low,
            (span_down == row).astype(bf16),
            (((0,), (0,)), ((), ())),
            preferred_element_type=f32,
        ).astype(bf16)
        for row in query_span
    ]
    noise = noise_ref[...].astype(f32)
    for i, ctx in enumerate((c, other_ctx(c, True), other_ctx(c, False))):
        for k in range(groups):
            key_span = as_column(spans_of(ctx, k))
            key_pos = block_of(ctx, k) * rows + down
            valid = (key_pos >= 0) & (key_pos < total)
            onehot = key_span == span_lane
            at = slice((i * groups + k) * rows, (i * groups + k + 1) * rows)
            for p in range(groups):
                allowed = jnp.dot(
                    onehot.astype(bf16), allowed_q[p], preferred_element_type=f32
                )
                visible = (
                    (allowed > 0.5)
                    & (key_span <= query_span[p])
                    & (query_pos[p] - key_pos < tokens)
                    & valid
                )
                bias_ref[at, p * rows : (p + 1) * rows] = jnp.where(visible, 0.0, HIDDEN)
            if i > 0:
                continue
            level = jnp.sum(jnp.where(onehot, noise, 0.0), axis=1, keepdims=True)
            level_onehot = (level.astype(jnp.int32) == level_lane).astype(f32)
            gate_ref[at, :] = jnp.dot(
                level_onehot,
                table_ref[...],
                precision=lax.Precision.HIGHEST,
                preferred_element_type=f32,
            )
            if by_span:
                slot_ref[:, at] = (span_down == query_span[k]).astype(bf16)
            else:
                slot_ref[:, at] = level_onehot.T.astype(bf16)


def attention_kernel(
    place_ref,
    qo_own_ref, kv_own_ref, qo_ref, kv_ref,
    near_own_ref, near_far_ref, side_own_ref, side_far_ref,
    gate_ref, bias_ref, slot_ref,
    *rest, rows, tokens, q_size, heads,
):
    (
        back_ref, side_grad_far_ref, mixed_ref, dq_ref, own_ref, far_ref,
        near_grad_own_ref, near_grad_far_ref, side_grad_own_ref, sums_ref,
    ) = rest[-10:]
    scale = 1.0 / math.sqrt(DH)
    bf16, f32 = jnp.bfloat16, jnp.float32
    tile = 32

    def dot(left, right, left_dim, right_dim):
        return lax.dot_general(
            left, right, (((left_dim,), (right_dim,)), ((), ())), preferred_element_type=f32
        )

    def load(j):
        at = slice(j * DH, (j + 1) * DH)
        keys, values = [], []
        for ref in (
            kv_own_ref, kv_ref, near_own_ref, near_far_ref, side_own_ref, side_far_ref
        ):
            keys.append(ref[0, :, at])
            values.append(ref[1, :, at])
        keys, values = jnp.concatenate(keys, axis=0), jnp.concatenate(values, axis=0)
        queries = jnp.concatenate([qo_own_ref[0, :, at], qo_ref[0, :, at]], axis=0)
        cotangent = jnp.concatenate([qo_own_ref[1, :, at], qo_ref[1, :, at]], axis=0)
        blocks = []
        for start in range(0, tokens, q_size):
            span = slice(start, start + q_size)
            q, o = queries[span], cotangent[span].astype(f32)
            gate = gate_ref[span, at]
            g = (gate * o).astype(bf16)
            blocks.append((q, o, gate, g, dot(keys, q, 1, 1), dot(values, g, 1, 1)))
        return keys, values, blocks

    def work(j, keys, values, blocks):
        at = slice(j * DH, (j + 1) * DH)
        keys_t, values_t = keys.T, values.T
        key_grad = value_grad = sums = None
        for number, (q, o, gate, g, scores, prob_grad) in enumerate(blocks):
            start = number * q_size
            span = slice(start, start + q_size)
            count = scores.shape[0]
            tiles = [slice(r, r + tile) for r in range(0, count, tile)]
            raised, top = [], None
            for t in tiles:
                part = scores[t] * (scale * LOG2E) + bias_ref[t, span]
                raised.append(part)
                high = jnp.max(part.reshape(tile // 8, 8, q_size), axis=0)
                top = high if top is None else jnp.maximum(top, high)
            top = jnp.max(top, axis=0, keepdims=True)
            total = None
            for i in range(len(tiles)):
                raised[i] = jnp.exp2(raised[i] - top)
                part = jnp.sum(raised[i].reshape(tile // 8, 8, q_size), axis=0)
                total = part if total is None else total + part
            inverse = 1.0 / jnp.sum(total, axis=0, keepdims=True)
            low = jnp.concatenate([(part * inverse).astype(bf16) for part in raised], axis=0)
            attended_t = dot(values_t, low, 1, 0).astype(bf16)
            row_dot = jnp.sum(g.T.astype(f32) * attended_t.astype(f32), axis=0, keepdims=True)
            attended = attended_t.T.astype(f32)
            score_grad = jnp.concatenate(
                [
                    (part * ((prob_grad[t] - row_dot) * inverse)).astype(bf16)
                    for part, t in zip(raised, tiles)
                ],
                axis=0,
            )
            query_grad = (dot(keys_t, score_grad, 1, 0) * scale).astype(bf16).T
            mixed = (gate * attended).astype(bf16)
            if start == 0:
                mixed_ref[:, at] = mixed[:rows]
                dq_ref[:, at] = query_grad[:rows]
                back_ref[0, : q_size - rows, at] = mixed[rows:]
                back_ref[1, : q_size - rows, at] = query_grad[rows:]
            else:
                back_ref[0, start - rows : start - rows + q_size, at] = mixed
                back_ref[1, start - rows : start - rows + q_size, at] = query_grad
            dk, dv = dot(score_grad, q, 1, 0), dot(low, g, 1, 0)
            product = o * attended
            high = product.astype(bf16)
            rest = (product - high.astype(f32)).astype(bf16)
            both = dot(slot_ref[:, span], jnp.concatenate([high, rest], axis=1), 1, 0)
            part = both[:, :DH] + both[:, DH:]
            key_grad = dk if key_grad is None else key_grad + dk
            value_grad = dv if value_grad is None else value_grad + dv
            sums = part if sums is None else sums + part
        sums_ref[:, at] = sums
        for i, grad in ((0, key_grad * scale), (1, value_grad)):
            own_ref[i, :, at] = grad[:rows]
            far_ref[i, :, at] = grad[rows:tokens]
            low = grad[tokens:].astype(bf16)
            near_grad_own_ref[i, :, at] = low[:rows]
            near_grad_far_ref[i, :, at] = low[rows:tokens]
            side_grad_own_ref[i, :, at] = low[tokens : tokens + rows]
            side_grad_far_ref[i, :, at] = low[tokens + rows :]

    ready = load(0)
    for j in range(heads):
        following = load(j + 1) if j + 1 < heads else None
        work(j, *ready)
        ready = following


def far_sum_kernel(part_ref, near_ref, side_ref, out_ref):
    total = part_ref[...] + near_ref[...].astype(jnp.float32) + side_ref[...].astype(jnp.float32)
    out_ref[...] = total.astype(out_ref.dtype)


def own_sum_kernel(place_ref, part_ref, near_ref, side_ref, key_ref, value_ref):
    total = part_ref[...] + near_ref[...].astype(jnp.float32) + side_ref[...].astype(jnp.float32)
    key_ref[...] = total[0].astype(key_ref.dtype)
    value_ref[...] = total[1].astype(value_ref.dtype)


def put_kernel(place_ref, part_ref, first_in, second_in, first_ref, second_ref, sems, *, at):
    shift, groups, parts, p = at
    width = part_ref.shape[2]
    start = (lax.rem(place_ref[1] + shift, groups) * parts + p) * width
    cols = pl.ds(pl.multiple_of(start, DH), width)
    copies = [
        pltpu.make_async_copy(part_ref.at[i], ref.at[:, cols], sems.at[i])
        for i, ref in enumerate((first_ref, second_ref))
    ]
    for copy in copies:
        copy.start()
    for copy in copies:
        copy.wait()


def pack_kernel(place_ref, first_ref, second_ref, own_ref, far_ref, sems, *, at):
    groups, parts, p = at
    rows, width = own_ref.shape[1:]
    copies = []
    for k in range(groups):
        start = (lax.rem(place_ref[1] + k, groups) * parts + p) * width
        cols = pl.ds(pl.multiple_of(start, DH), width)
        for i, ref in enumerate((first_ref, second_ref)):
            to = own_ref.at[i] if k == 0 else far_ref.at[i, pl.ds((k - 1) * rows, rows)]
            copies.append(pltpu.make_async_copy(ref.at[:, cols], to, sems.at[2 * k + i]))
    for copy in copies:
        copy.start()
    for copy in copies:
        copy.wait()


def spread_kernel(noise_ref, sums_ref, out_ref):
    spans = noise_ref.shape[1]
    levels = lax.broadcasted_iota(jnp.int32, (out_ref.shape[0], spans), 0)
    out_ref[...] = jnp.dot(
        (levels == noise_ref[...]).astype(jnp.float32),
        sums_ref[...],
        precision=lax.Precision.HIGHEST,
        preferred_element_type=jnp.float32,
    )


def per_device(
    queries, key_rows, value_rows, out_cotangent, gate_table, span_ids, noise_level, block_mask
):
    groups = lax.axis_size("head")
    ctx_count = lax.axis_size("ctx")
    rows, full_width = queries.shape
    width = full_width // groups
    heads = width // DH
    tokens = rows * groups
    far_rows = tokens - rows
    parts = 2 if heads % 2 == 0 else 1
    part_width = width // parts
    part_heads = heads // parts
    span_total = noise_level.shape[0]
    level_count = gate_table.shape[0]
    by_span = span_total <= level_count // 2
    slots = span_total if by_span else level_count
    c = lax.axis_index("ctx")
    h = lax.axis_index("head")
    place = jnp.stack([c, h]).astype(jnp.int32)
    bf16, f32 = jnp.bfloat16, jnp.float32
    tie = lax.optimization_barrier

    near_pairs = [(i, i ^ 1) for i in range(ctx_count)]
    side_of = [i - 1 + 2 * (i % 2) for i in range(ctx_count)]
    side_pairs = [(i, j if 0 <= j < ctx_count else i) for i, j in enumerate(side_of)]

    whole = lambda shape: pl.BlockSpec(shape, lambda i, place: (0,) * len(shape))
    limit = (26 if tokens <= 256 else 56) * 1024 * 1024
    params = pltpu.CompilerParams(vmem_limit_bytes=limit)
    alone = pltpu.CompilerParams(vmem_limit_bytes=60 * 1024 * 1024)
    small = pltpu.CompilerParams(vmem_limit_bytes=(12 if tokens <= 256 else 36) * 1024 * 1024)

    def pack(first, second, p, params):
        return pl.pallas_call(
            functools.partial(pack_kernel, at=(groups, parts, p)),
            grid_spec=pltpu.PrefetchScalarGridSpec(
                num_scalar_prefetch=1,
                grid=(1,),
                in_specs=[pl.BlockSpec(memory_space=pltpu.HBM)] * 2,
                out_specs=[pl.BlockSpec(memory_space=pl.ANY)] * 2,
                scratch_shapes=[pltpu.SemaphoreType.DMA((2 * groups,))],
            ),
            out_shape=[
                jax.ShapeDtypeStruct((2, rows, part_width), bf16),
                jax.ShapeDtypeStruct((2, far_rows, part_width), bf16),
            ],
            compiler_params=params,
            name="pack",
        )(place, first, second)

    def to_peers(slab):
        arrived = []
        for k in range(1, groups):
            part = slab if groups == 2 else slab[:, (k - 1) * rows : k * rows]
            pairs = [(i, (i + k) % groups) for i in range(groups)]
            arrived.append(lax.ppermute(part, "head", pairs))
        return arrived[0] if groups == 2 else jnp.concatenate(arrived, axis=1)

    def from_peers(slab):
        arrived = []
        for k in range(1, groups):
            part = slab if groups == 2 else slab[:, (k - 1) * rows : k * rows]
            pairs = [(i, (i - k) % groups) for i in range(groups)]
            arrived.append(lax.ppermute(part, "head", pairs))
        return arrived

    kv_own, kv_far, qo_own, qo_far = [], [], [], []
    side_own, side_far, near_own, near_far = [], [], [], []
    for p in range(parts):
        own_kv, sent_kv = pack(key_rows, value_rows, p, small if p else alone)
        own_qo, sent_qo = pack(queries, out_cotangent, p, small)
        kv_own.append(own_kv)
        qo_own.append(own_qo)
        if p > 0:
            own_kv, sent_kv, *_ = tie((own_kv, sent_kv, qo_far[-1], side_far[-1]))
        side_own.append(lax.ppermute(own_kv, "ctx", side_pairs))
        kv_far.append(to_peers(sent_kv))
        near_own.append(lax.ppermute(own_kv, "ctx", near_pairs))
        sent_qo, *_ = tie((sent_qo, kv_far[p], side_own[p]))
        side_far.append(lax.ppermute(kv_far[p], "ctx", side_pairs))
        near_far.append(lax.ppermute(kv_far[p], "ctx", near_pairs))
        qo_far.append(to_peers(sent_qo))

    sizes = (ctx_count, groups, rows, span_total, level_count, by_span)
    whole = lambda shape: pl.BlockSpec(shape, lambda i, place: (0,) * len(shape))
    bias, gate, slot = pl.pallas_call(
        functools.partial(prep_kernel, sizes=sizes),
        grid_spec=pltpu.PrefetchScalarGridSpec(
            num_scalar_prefetch=1,
            grid=(1,),
            in_specs=[
                whole((ctx_count * groups, rows)),
                whole((1, span_total)),
                whole((span_total, span_total)),
                pl.BlockSpec((level_count, width), lambda i, place: (0, place[1])),
            ],
            out_specs=[
                whole((3 * tokens, tokens)),
                whole((tokens, width)),
                whole((slots, tokens)),
            ],
        ),
        out_shape=[
            jax.ShapeDtypeStruct((3 * tokens, tokens), f32),
            jax.ShapeDtypeStruct((tokens, width), f32),
            jax.ShapeDtypeStruct((slots, tokens), bf16),
        ],
        compiler_params=small,
        name="prep",
    )(
        place,
        span_ids.reshape(ctx_count * groups, rows),
        noise_level.reshape(1, span_total),
        block_mask,
        gate_table,
    )

    batch = next(n for n in (3, 2, 1) if part_heads % n == 0) if tokens <= 256 else 1
    steps = part_heads // batch
    block = batch * DH
    q_size = min(256, tokens)
    flops = 6 * 2 * tokens * 3 * tokens * DH * part_heads

    def attention(p, joint):
        pair = lambda count: pl.BlockSpec((2, count, block), lambda i, place: (0, 0, i))
        at_part = lambda count: pl.BlockSpec(
            (2, count, block), lambda i, place: (0, 0, p * steps + i)
        )
        at_head = pl.BlockSpec(
            (rows, block), lambda i, place: (0, (place[1] * parts + p) * steps + i)
        )
        column = lambda count: pl.BlockSpec((count, block), lambda i, place: (0, p * steps + i))
        struct = jax.ShapeDtypeStruct
        inputs = [
            qo_own[p], kv_own[p], qo_far[p], kv_far[p],
            near_own[p], near_far[p], side_own[p], side_far[p],
            gate, bias, slot,
        ]
        return pl.pallas_call(
            functools.partial(
                attention_kernel, rows=rows, tokens=tokens, q_size=q_size, heads=batch
            ),
            grid_spec=pltpu.PrefetchScalarGridSpec(
                num_scalar_prefetch=1,
                grid=(steps,),
                in_specs=[
                    pair(rows), pair(rows), pair(far_rows), pair(far_rows),
                    pair(rows), pair(far_rows), pair(rows), pair(far_rows),
                    column(tokens), whole((3 * tokens, tokens)), whole((slots, tokens)),
                ]
                + [pl.BlockSpec(memory_space=pl.ANY)] * len(joint),
                out_specs=[
                    pair(far_rows), pair(far_rows),
                    at_head, at_head, at_part(rows), at_part(far_rows),
                    at_part(rows), at_part(far_rows), at_part(rows), column(slots),
                ],
            ),
            out_shape=[
                struct((2, far_rows, part_width), bf16),
                struct((2, far_rows, part_width), bf16),
                struct((rows, full_width), bf16),
                struct((rows, full_width), bf16),
                struct((2, rows, width), f32),
                struct((2, far_rows, width), f32),
                struct((2, rows, width), bf16),
                struct((2, far_rows, width), bf16),
                struct((2, rows, width), bf16),
                struct((slots, width), f32),
            ],
            input_output_aliases={1 + len(inputs) + i: 2 + i for i in range(len(joint))},
            compiler_params=params,
            cost_estimate=pl.CostEstimate(
                flops=flops, bytes_accessed=16 * tokens * part_width, transcendentals=0
            ),
            name="attention",
        )(place, *inputs, *joint)

    joint, back_far, side_back_far = (), [], []
    for p in range(parts):
        back, side_grad_far, *joint = attention(p, joint)
        if p > 0:
            back, side_grad_far, joint, back_far, side_back_far = tie(
                (back, side_grad_far, joint, back_far, side_back_far)
            )
        side_back_far.append(lax.ppermute(side_grad_far, "ctx", side_pairs))
        back_far.append(from_peers(back))
    mixed, query_grad, own, far, near_grad_own, near_grad_far, side_grad_own, sums = joint

    near_back_far = lax.ppermute(near_grad_far, "ctx", near_pairs)
    near_back_own = lax.ppermute(near_grad_own, "ctx", near_pairs)
    side_grad_own, _ = tie((side_grad_own, side_back_far[-1]))
    side_back_own = lax.ppermute(side_grad_own, "ctx", side_pairs)
    grad_far, grad_sent = [], []
    for p in range(parts):
        at_part = pl.BlockSpec((2, far_rows, part_width), lambda i, p=p: (0, 0, p))
        alone = pl.BlockSpec((2, far_rows, part_width), lambda i: (0, 0, 0))
        far_grad = pl.pallas_call(
            far_sum_kernel,
            grid=(1,),
            in_specs=[at_part, at_part, alone],
            out_specs=alone,
            out_shape=jax.ShapeDtypeStruct((2, far_rows, part_width), bf16),
            compiler_params=small,
            name="far_sum",
        )(far, near_back_far, side_back_far[p])
        grad_sent.append(far_grad)
        grad_far.append(from_peers(far_grad))
    key_grad, value_grad = pl.pallas_call(
        own_sum_kernel,
        grid_spec=pltpu.PrefetchScalarGridSpec(
            num_scalar_prefetch=1,
            grid=(parts,),
            in_specs=[pl.BlockSpec((2, rows, part_width), lambda i, place: (0, 0, i))] * 3,
            out_specs=[
                pl.BlockSpec((rows, part_width), lambda i, place: (0, place[1] * parts + i))
            ]
            * 2,
        ),
        out_shape=[jax.ShapeDtypeStruct((rows, full_width), bf16)] * 2,
        compiler_params=small,
        name="own_sum",
    )(place, own, near_back_own, side_back_own)

    def reduced(order, sums):
        for step in order:
            pairs = [(i, i ^ step) for i in range(ctx_count)]
            sums = sums + lax.ppermute(sums, "ctx", pairs)
        for step in (1 << n for n in range(groups.bit_length() - 1)):
            pairs = [(i, i ^ step) for i in range(groups)]
            other = lax.ppermute(sums, "head", pairs)
            sums = jnp.where(
                (h // step) % 2 == 0,
                jnp.concatenate([sums, other], axis=1),
                jnp.concatenate([other, sums], axis=1),
            )
        return sums

    doubling = [1 << n for n in range(ctx_count.bit_length() - 1)]
    turned = doubling[:1] + doubling[2:] + doubling[1:2]
    sums, _ = tie((sums, grad_sent))
    slot_sums = lax.cond(
        noise_level[0] >= 0,
        functools.partial(reduced, turned),
        functools.partial(reduced, doubling),
        sums,
    )
    if by_span:
        gate_grad = pl.pallas_call(
            spread_kernel,
            grid=(groups,),
            in_specs=[
                pl.BlockSpec((1, span_total), lambda i: (0, 0)),
                pl.BlockSpec((slots, width), lambda i: (0, i)),
            ],
            out_specs=pl.BlockSpec((level_count, width), lambda i: (0, i)),
            out_shape=jax.ShapeDtypeStruct((level_count, full_width), f32),
            compiler_params=small,
            name="spread",
        )(noise_level.reshape(1, span_total), slot_sums)
    else:
        gate_grad = slot_sums

    def put(first, second, arrived, k, p):
        anywhere = pl.BlockSpec(memory_space=pl.ANY)
        return pl.pallas_call(
            functools.partial(put_kernel, at=(k, groups, parts, p)),
            grid_spec=pltpu.PrefetchScalarGridSpec(
                num_scalar_prefetch=1,
                grid=(1,),
                in_specs=[anywhere] * 3,
                out_specs=[anywhere] * 2,
                scratch_shapes=[pltpu.SemaphoreType.DMA((2,))],
            ),
            out_shape=[jax.ShapeDtypeStruct((rows, full_width), bf16)] * 2,
            input_output_aliases={2: 0, 3: 1},
            compiler_params=small,
            name="put",
        )(place, arrived, first, second)

    for p in range(parts):
        for k in range(1, groups):
            mixed, query_grad = put(mixed, query_grad, back_far[p][k - 1], k, p)
            key_grad, value_grad = put(key_grad, value_grad, grad_far[p][k - 1], k, p)
    return (mixed, query_grad, key_grad, value_grad, gate_grad)


def solution(mesh):
    sharded = P(("ctx", "head"), None)
    return jax.shard_map(
        per_device,
        mesh=mesh,
        in_specs=(sharded,) * 4 + (P(),) * 4,
        out_specs=(sharded,) * 4 + (P(),),
        check_vma=False,
    )
```

```python
import functools
import math

import jax
import jax.numpy as jnp
from jax import lax
from jax.experimental import pallas as pl
from jax.experimental.pallas import tpu as pltpu
from jax.sharding import PartitionSpec as P

DH = 128
HIDDEN = -1e30
LOG2E = 1.4426950408889634


def other_ctx(c, near):
    odd = lax.rem(c, 2)
    return c + 1 - 2 * odd if near else c - 1 + 2 * odd


def prep_kernel(
    place_ref, span_ref, noise_ref, mask_ref, table_ref, bias_ref, gate_ref, slot_ref, *, sizes
):
    ctx_count, groups, rows, span_total, level_count, by_span = sizes
    c, h = place_ref[0], place_ref[1]
    tokens = groups * rows
    total = ctx_count * tokens
    bf16, f32 = jnp.bfloat16, jnp.float32

    def block_of(ctx, k):
        return ctx * groups + lax.rem(h - k + groups, groups)

    def spans_of(ctx, k):
        at = jnp.clip(ctx, 0, ctx_count - 1)
        return span_ref[pl.ds(block_of(at, k), 1), :]

    def as_column(row):
        return jnp.broadcast_to(row.astype(f32), (rows, rows)).T[:, :1].astype(jnp.int32)

    across = lax.broadcasted_iota(jnp.int32, (1, rows), 1)
    down = lax.broadcasted_iota(jnp.int32, (rows, 1), 0)
    span_lane = lax.broadcasted_iota(jnp.int32, (rows, span_total), 1)
    span_down = lax.broadcasted_iota(jnp.int32, (span_total, rows), 0)
    level_lane = lax.broadcasted_iota(jnp.int32, (rows, level_count), 1)
    query_span = [spans_of(c, k) for k in range(groups)]
    query_pos = [block_of(c, k) * rows + across for k in range(groups)]
    mask_low = mask_ref[...].astype(bf16)
    allowed_q = [
        lax.dot_general(
            mask_low,
            (span_down == row).astype(bf16),
            (((0,), (0,)), ((), ())),
            preferred_element_type=f32,
        ).astype(bf16)
        for row in query_span
    ]
    noise = noise_ref[...].astype(f32)
    for i, ctx in enumerate((c, other_ctx(c, True), other_ctx(c, False))):
        for k in range(groups):
            key_span = as_column(spans_of(ctx, k))
            key_pos = block_of(ctx, k) * rows + down
            valid = (key_pos >= 0) & (key_pos < total)
            onehot = key_span == span_lane
            at = slice((i * groups + k) * rows, (i * groups + k + 1) * rows)
            for p in range(groups):
                allowed = jnp.dot(
                    onehot.astype(bf16), allowed_q[p], preferred_element_type=f32
                )
                visible = (
                    (allowed > 0.5)
                    & (key_span <= query_span[p])
                    & (query_pos[p] - key_pos < tokens)
                    & valid
                )
                bias_ref[at, p * rows : (p + 1) * rows] = jnp.where(visible, 0.0, HIDDEN)
            if i > 0:
                continue
            level = jnp.sum(jnp.where(onehot, noise, 0.0), axis=1, keepdims=True)
            level_onehot = (level.astype(jnp.int32) == level_lane).astype(f32)
            gate_ref[at, :] = jnp.dot(
                level_onehot,
                table_ref[...],
                precision=lax.Precision.HIGHEST,
                preferred_element_type=f32,
            )
            if by_span:
                slot_ref[:, at] = (span_down == query_span[k]).astype(bf16)
            else:
                slot_ref[:, at] = level_onehot.T.astype(bf16)


def attention_kernel(
    place_ref,
    qo_own_ref, kv_own_ref, qo_ref, kv_ref,
    near_own_ref, near_far_ref, side_own_ref, side_far_ref,
    gate_ref, bias_ref, slot_ref,
    *rest, rows, tokens, q_size, heads,
):
    (
        back_ref, side_grad_far_ref, mixed_ref, dq_ref, own_ref, far_ref,
        near_grad_own_ref, near_grad_far_ref, side_grad_own_ref, sums_ref,
    ) = rest[-10:]
    scale = 1.0 / math.sqrt(DH)
    bf16, f32 = jnp.bfloat16, jnp.float32
    tile = 32

    def dot(left, right, left_dim, right_dim):
        return lax.dot_general(
            left, right, (((left_dim,), (right_dim,)), ((), ())), preferred_element_type=f32
        )

    def load(j):
        at = slice(j * DH, (j + 1) * DH)
        keys, values = [], []
        for ref in (
            kv_own_ref, kv_ref, near_own_ref, near_far_ref, side_own_ref, side_far_ref
        ):
            keys.append(ref[0, :, at])
            values.append(ref[1, :, at])
        keys, values = jnp.concatenate(keys, axis=0), jnp.concatenate(values, axis=0)
        queries = jnp.concatenate([qo_own_ref[0, :, at], qo_ref[0, :, at]], axis=0)
        cotangent = jnp.concatenate([qo_own_ref[1, :, at], qo_ref[1, :, at]], axis=0)
        blocks = []
        for start in range(0, tokens, q_size):
            span = slice(start, start + q_size)
            q, o = queries[span], cotangent[span].astype(f32)
            gate = gate_ref[span, at]
            g = (gate * o).astype(bf16)
            blocks.append((q, o, gate, g, dot(keys, q, 1, 1), dot(values, g, 1, 1)))
        return keys, values, blocks

    def work(j, keys, values, blocks):
        at = slice(j * DH, (j + 1) * DH)
        keys_t, values_t = keys.T, values.T
        key_grad = value_grad = sums = None
        for number, (q, o, gate, g, scores, prob_grad) in enumerate(blocks):
            start = number * q_size
            span = slice(start, start + q_size)
            count = scores.shape[0]
            tiles = [slice(r, r + tile) for r in range(0, count, tile)]
            raised, top = [], None
            for t in tiles:
                part = scores[t] * (scale * LOG2E) + bias_ref[t, span]
                raised.append(part)
                high = jnp.max(part.reshape(tile // 8, 8, q_size), axis=0)
                top = high if top is None else jnp.maximum(top, high)
            top = jnp.max(top, axis=0, keepdims=True)
            total = None
            for i in range(len(tiles)):
                raised[i] = jnp.exp2(raised[i] - top)
                part = jnp.sum(raised[i].reshape(tile // 8, 8, q_size), axis=0)
                total = part if total is None else total + part
            inverse = 1.0 / jnp.sum(total, axis=0, keepdims=True)
            low = jnp.concatenate([(part * inverse).astype(bf16) for part in raised], axis=0)
            attended_t = dot(values_t, low, 1, 0).astype(bf16)
            row_dot = jnp.sum(g.T.astype(f32) * attended_t.astype(f32), axis=0, keepdims=True)
            attended = attended_t.T.astype(f32)
            score_grad = jnp.concatenate(
                [
                    (part * ((prob_grad[t] - row_dot) * inverse)).astype(bf16)
                    for part, t in zip(raised, tiles)
                ],
                axis=0,
            )
            query_grad = (dot(keys_t, score_grad, 1, 0) * scale).astype(bf16).T
            mixed = (gate * attended).astype(bf16)
            if start == 0:
                mixed_ref[:, at] = mixed[:rows]
                dq_ref[:, at] = query_grad[:rows]
                back_ref[0, : q_size - rows, at] = mixed[rows:]
                back_ref[1, : q_size - rows, at] = query_grad[rows:]
            else:
                back_ref[0, start - rows : start - rows + q_size, at] = mixed
                back_ref[1, start - rows : start - rows + q_size, at] = query_grad
            dk, dv = dot(score_grad, q, 1, 0), dot(low, g, 1, 0)
            product = o * attended
            high = product.astype(bf16)
            rest = (product - high.astype(f32)).astype(bf16)
            both = dot(slot_ref[:, span], jnp.concatenate([high, rest], axis=1), 1, 0)
            part = both[:, :DH] + both[:, DH:]
            key_grad = dk if key_grad is None else key_grad + dk
            value_grad = dv if value_grad is None else value_grad + dv
            sums = part if sums is None else sums + part
        sums_ref[:, at] = sums
        for i, grad in ((0, key_grad * scale), (1, value_grad)):
            own_ref[i, :, at] = grad[:rows]
            far_ref[i, :, at] = grad[rows:tokens]
            low = grad[tokens:].astype(bf16)
            near_grad_own_ref[i, :, at] = low[:rows]
            near_grad_far_ref[i, :, at] = low[rows:tokens]
            side_grad_own_ref[i, :, at] = low[tokens : tokens + rows]
            side_grad_far_ref[i, :, at] = low[tokens + rows :]

    ready = load(0)
    for j in range(heads):
        following = load(j + 1) if j + 1 < heads else None
        work(j, *ready)
        ready = following


def far_sum_kernel(part_ref, near_ref, side_ref, out_ref):
    total = part_ref[...] + near_ref[...].astype(jnp.float32) + side_ref[...].astype(jnp.float32)
    out_ref[...] = total.astype(out_ref.dtype)


def own_sum_kernel(place_ref, part_ref, near_ref, side_ref, key_ref, value_ref):
    total = part_ref[...] + near_ref[...].astype(jnp.float32) + side_ref[...].astype(jnp.float32)
    key_ref[...] = total[0].astype(key_ref.dtype)
    value_ref[...] = total[1].astype(value_ref.dtype)


def put_kernel(place_ref, part_ref, first_in, second_in, first_ref, second_ref, sems, *, at):
    shift, groups, parts, p = at
    width = part_ref.shape[2]
    start = (lax.rem(place_ref[1] + shift, groups) * parts + p) * width
    cols = pl.ds(pl.multiple_of(start, DH), width)
    copies = [
        pltpu.make_async_copy(part_ref.at[i], ref.at[:, cols], sems.at[i])
        for i, ref in enumerate((first_ref, second_ref))
    ]
    for copy in copies:
        copy.start()
    for copy in copies:
        copy.wait()


def pack_kernel(place_ref, *refs, parts):
    ins, own_ref, far_refs = refs[: -1 - parts], refs[-1 - parts], refs[-parts:]
    rows = own_ref.shape[1]
    own_ref[0], own_ref[1] = ins[0][...], ins[1][...]
    for p, ref in enumerate(far_refs):
        width = ref.shape[2]
        cols = slice(p * width, (p + 1) * width)
        for k in range(ref.shape[1] // rows):
            at = slice(k * rows, (k + 1) * rows)
            ref[0, at], ref[1, at] = ins[2 + 2 * k][:, cols], ins[3 + 2 * k][:, cols]


def spread_kernel(place_ref, noise_ref, *refs, by_span):
    *slabs, out_ref = refs
    for j, ref in enumerate(slabs):

        @pl.when(pl.program_id(0) == j)
        def _(ref=ref):
            sums = ref[...]
            if not by_span:
                out_ref[...] = sums
                return
            levels = lax.broadcasted_iota(jnp.int32, (out_ref.shape[0], noise_ref.shape[1]), 0)
            onehot = (levels == noise_ref[...]).astype(jnp.bfloat16)
            total = None
            for _ in range(3):
                piece = sums.astype(jnp.bfloat16)
                sums = sums - piece.astype(jnp.float32)
                part = jnp.dot(onehot, piece, preferred_element_type=jnp.float32)
                total = part if total is None else total + part
            out_ref[...] = total


def per_device(
    queries, key_rows, value_rows, out_cotangent, gate_table, span_ids, noise_level, block_mask
):
    groups = lax.axis_size("head")
    ctx_count = lax.axis_size("ctx")
    rows, full_width = queries.shape
    width = full_width // groups
    heads = width // DH
    tokens = rows * groups
    far_rows = tokens - rows
    parts = 2 if heads % 2 == 0 else 1
    part_width = width // parts
    part_heads = heads // parts
    span_total = noise_level.shape[0]
    level_count = gate_table.shape[0]
    by_span = span_total <= level_count // 2
    slots = span_total if by_span else level_count
    c = lax.axis_index("ctx")
    h = lax.axis_index("head")
    place = jnp.stack([c, h]).astype(jnp.int32)
    bf16, f32 = jnp.bfloat16, jnp.float32
    tie = lax.optimization_barrier

    near_pairs = [(i, i ^ 1) for i in range(ctx_count)]
    side_of = [i - 1 + 2 * (i % 2) for i in range(ctx_count)]
    side_pairs = [(i, j if 0 <= j < ctx_count else i) for i, j in enumerate(side_of)]

    whole = lambda shape: pl.BlockSpec(shape, lambda i, place: (0,) * len(shape))
    limit = (26 if tokens <= 256 else 56) * 1024 * 1024
    params = pltpu.CompilerParams(vmem_limit_bytes=limit)
    alone = pltpu.CompilerParams(vmem_limit_bytes=60 * 1024 * 1024)
    small = pltpu.CompilerParams(vmem_limit_bytes=(12 if tokens <= 256 else 36) * 1024 * 1024)

    def pack(first, second, params):
        def at_group(k):
            return pl.BlockSpec(
                (rows, width), lambda i, place: (0, lax.rem(place[1] + k, groups))
            )

        far_shape = (2, far_rows, part_width)
        return pl.pallas_call(
            functools.partial(pack_kernel, parts=parts),
            grid_spec=pltpu.PrefetchScalarGridSpec(
                num_scalar_prefetch=1,
                grid=(1,),
                in_specs=[at_group(k) for k in range(groups) for _ in range(2)],
                out_specs=[whole((2, rows, width))] + [whole(far_shape)] * parts,
            ),
            out_shape=[jax.ShapeDtypeStruct((2, rows, width), bf16)]
            + [jax.ShapeDtypeStruct(far_shape, bf16)] * parts,
            compiler_params=params,
            name="pack",
        )(place, *[first, second] * groups)

    def to_peers(slab):
        arrived = []
        for k in range(1, groups):
            part = slab if groups == 2 else slab[:, (k - 1) * rows : k * rows]
            pairs = [(i, (i + k) % groups) for i in range(groups)]
            arrived.append(lax.ppermute(part, "head", pairs))
        return arrived[0] if groups == 2 else jnp.concatenate(arrived, axis=1)

    def from_peers(slab):
        arrived = []
        for k in range(1, groups):
            part = slab if groups == 2 else slab[:, (k - 1) * rows : k * rows]
            pairs = [(i, (i - k) % groups) for i in range(groups)]
            arrived.append(lax.ppermute(part, "head", pairs))
        return arrived

    kv_own, *kv_sent = pack(key_rows, value_rows, alone)
    qo_own, *qo_sent = pack(queries, out_cotangent, small)
    side_own = lax.ppermute(kv_own, "ctx", side_pairs)
    near_own = lax.ppermute(kv_own, "ctx", near_pairs)
    kv_far = [to_peers(slab) for slab in kv_sent]
    side_far = [lax.ppermute(slab, "ctx", side_pairs) for slab in kv_far]
    near_far = [lax.ppermute(slab, "ctx", near_pairs) for slab in kv_far]
    qo_far = [to_peers(tie((slab, far))[0]) for slab, far in zip(qo_sent, kv_far)]

    sizes = (ctx_count, groups, rows, span_total, level_count, by_span)
    whole = lambda shape: pl.BlockSpec(shape, lambda i, place: (0,) * len(shape))
    bias, gate, slot = pl.pallas_call(
        functools.partial(prep_kernel, sizes=sizes),
        grid_spec=pltpu.PrefetchScalarGridSpec(
            num_scalar_prefetch=1,
            grid=(1,),
            in_specs=[
                whole((ctx_count * groups, rows)),
                whole((1, span_total)),
                whole((span_total, span_total)),
                pl.BlockSpec((level_count, width), lambda i, place: (0, place[1])),
            ],
            out_specs=[
                whole((3 * tokens, tokens)),
                whole((tokens, width)),
                whole((slots, tokens)),
            ],
        ),
        out_shape=[
            jax.ShapeDtypeStruct((3 * tokens, tokens), f32),
            jax.ShapeDtypeStruct((tokens, width), f32),
            jax.ShapeDtypeStruct((slots, tokens), bf16),
        ],
        compiler_params=small,
        name="prep",
    )(
        place,
        span_ids.reshape(ctx_count * groups, rows),
        noise_level.reshape(1, span_total),
        block_mask,
        gate_table,
    )

    batch = next(n for n in (3, 2, 1) if part_heads % n == 0) if tokens <= 256 else 1
    steps = part_heads // batch
    block = batch * DH
    q_size = min(256, tokens)
    flops = 6 * 2 * tokens * 3 * tokens * DH * part_heads

    def attention(p, joint):
        pair = lambda count: pl.BlockSpec((2, count, block), lambda i, place: (0, 0, i))
        at_part = lambda count: pl.BlockSpec(
            (2, count, block), lambda i, place: (0, 0, p * steps + i)
        )
        at_head = pl.BlockSpec(
            (rows, block), lambda i, place: (0, (place[1] * parts + p) * steps + i)
        )
        column = lambda count: pl.BlockSpec((count, block), lambda i, place: (0, p * steps + i))
        struct = jax.ShapeDtypeStruct
        inputs = [
            qo_own, kv_own, qo_far[p], kv_far[p],
            near_own, near_far[p], side_own, side_far[p],
            gate, bias, slot,
        ]
        return pl.pallas_call(
            functools.partial(
                attention_kernel, rows=rows, tokens=tokens, q_size=q_size, heads=batch
            ),
            grid_spec=pltpu.PrefetchScalarGridSpec(
                num_scalar_prefetch=1,
                grid=(steps,),
                in_specs=[
                    at_part(rows), at_part(rows), pair(far_rows), pair(far_rows),
                    at_part(rows), pair(far_rows), at_part(rows), pair(far_rows),
                    column(tokens), whole((3 * tokens, tokens)), whole((slots, tokens)),
                ]
                + [pl.BlockSpec(memory_space=pl.ANY)] * len(joint),
                out_specs=[
                    pair(far_rows), pair(far_rows),
                    at_head, at_head, at_part(rows), at_part(far_rows),
                    at_part(rows), at_part(far_rows), at_part(rows), column(slots),
                ],
            ),
            out_shape=[
                struct((2, far_rows, part_width), bf16),
                struct((2, far_rows, part_width), bf16),
                struct((rows, full_width), bf16),
                struct((rows, full_width), bf16),
                struct((2, rows, width), f32),
                struct((2, far_rows, width), f32),
                struct((2, rows, width), bf16),
                struct((2, far_rows, width), bf16),
                struct((2, rows, width), bf16),
                struct((slots, width), f32),
            ],
            input_output_aliases={1 + len(inputs) + i: 2 + i for i in range(len(joint))},
            compiler_params=params,
            cost_estimate=pl.CostEstimate(
                flops=flops, bytes_accessed=16 * tokens * part_width, transcendentals=0
            ),
            name="attention",
        )(place, *inputs, *joint)

    joint, back_far, side_back_far = (), [], []
    for p in range(parts):
        back, side_grad_far, *joint = attention(p, joint)
        if p > 0:
            back, side_grad_far, joint, back_far, side_back_far = tie(
                (back, side_grad_far, joint, back_far, side_back_far)
            )
        side_back_far.append(lax.ppermute(side_grad_far, "ctx", side_pairs))
        back_far.append(from_peers(back))
    mixed, query_grad, own, far, near_grad_own, near_grad_far, side_grad_own, sums = joint

    near_back_far = lax.ppermute(near_grad_far, "ctx", near_pairs)
    near_back_own = lax.ppermute(near_grad_own, "ctx", near_pairs)
    side_back_own = lax.ppermute(side_grad_own, "ctx", side_pairs)

    def doubled(steps, sums):
        for step in steps:
            pairs = [(i, i ^ step) for i in range(ctx_count)]
            sums = sums + lax.ppermute(sums, "ctx", pairs)
        return sums

    doubling = [1 << n for n in range(ctx_count.bit_length() - 1)]
    first, last = [doubling[0], *doubling[2:3]], [*doubling[3:]]
    sums = lax.cond(
        noise_level[0] >= 0,
        functools.partial(doubled, first),
        functools.partial(doubled, first[::-1]),
        sums,
    )
    side_back_far, back_far, sums = tie((side_back_far, back_far, sums))
    grad_far, grad_sent = [], []
    for p in range(parts):
        at_part = pl.BlockSpec((2, far_rows, part_width), lambda i, p=p: (0, 0, p))
        alone = pl.BlockSpec((2, far_rows, part_width), lambda i: (0, 0, 0))
        far_grad = pl.pallas_call(
            far_sum_kernel,
            grid=(1,),
            in_specs=[at_part, at_part, alone],
            out_specs=alone,
            out_shape=jax.ShapeDtypeStruct((2, far_rows, part_width), bf16),
            compiler_params=small,
            name="far_sum",
        )(far, near_back_far, side_back_far[p])
        grad_sent.append(far_grad)
        grad_far.append(from_peers(far_grad))
    key_grad, value_grad = pl.pallas_call(
        own_sum_kernel,
        grid_spec=pltpu.PrefetchScalarGridSpec(
            num_scalar_prefetch=1,
            grid=(parts,),
            in_specs=[pl.BlockSpec((2, rows, part_width), lambda i, place: (0, 0, i))] * 3,
            out_specs=[
                pl.BlockSpec((rows, part_width), lambda i, place: (0, place[1] * parts + i))
            ]
            * 2,
        ),
        out_shape=[jax.ShapeDtypeStruct((rows, full_width), bf16)] * 2,
        compiler_params=small,
        name="own_sum",
    )(place, own, near_back_own, side_back_own)

    def to_all(first, last, sums):
        slabs = [doubled(first, sums)]
        for step in (1 << n for n in range(groups.bit_length() - 1)):
            pairs = [(i, i ^ step) for i in range(groups)]
            slabs = slabs + [lax.ppermute(slab, "head", pairs) for slab in slabs]
        return [doubled(last, slab) for slab in slabs]

    x_step = doubling[1:2]
    sums, _ = tie((sums, grad_sent))
    slabs = lax.cond(
        noise_level[0] >= 0,
        functools.partial(to_all, last + x_step, []),
        functools.partial(to_all, x_step + last, []),
        sums,
    )
    gate_grad = pl.pallas_call(
        functools.partial(spread_kernel, by_span=by_span),
        grid_spec=pltpu.PrefetchScalarGridSpec(
            num_scalar_prefetch=1,
            grid=(groups,),
            in_specs=[whole((1, span_total))] + [whole((slots, width))] * groups,
            out_specs=pl.BlockSpec(
                (level_count, width), lambda i, place: (0, lax.bitwise_xor(place[1], i))
            ),
        ),
        out_shape=jax.ShapeDtypeStruct((level_count, full_width), f32),
        compiler_params=small,
        name="spread",
    )(place, noise_level.reshape(1, span_total), *slabs)

    def put(first, second, arrived, k, p):
        anywhere = pl.BlockSpec(memory_space=pl.ANY)
        return pl.pallas_call(
            functools.partial(put_kernel, at=(k, groups, parts, p)),
            grid_spec=pltpu.PrefetchScalarGridSpec(
                num_scalar_prefetch=1,
                grid=(1,),
                in_specs=[whole((2, rows, part_width)), anywhere, anywhere],
                out_specs=[anywhere] * 2,
                scratch_shapes=[pltpu.SemaphoreType.DMA((2,))],
            ),
            out_shape=[jax.ShapeDtypeStruct((rows, full_width), bf16)] * 2,
            input_output_aliases={2: 0, 3: 1},
            compiler_params=small,
            name="put",
        )(place, arrived, first, second)

    for p in range(parts):
        for k in range(1, groups):
            mixed, query_grad = put(mixed, query_grad, back_far[p][k - 1], k, p)
            key_grad, value_grad = put(key_grad, value_grad, grad_far[p][k - 1], k, p)
    return (mixed, query_grad, key_grad, value_grad, gate_grad)


def solution(mesh):
    sharded = P(("ctx", "head"), None)
    return jax.shard_map(
        per_device,
        mesh=mesh,
        in_specs=(sharded,) * 4 + (P(),) * 4,
        out_specs=(sharded,) * 4 + (P(),),
        check_vma=False,
    )
```

```python
import functools
import math

import jax
import jax.numpy as jnp
from jax import lax
from jax.experimental import pallas as pl
from jax.experimental.pallas import tpu as pltpu
from jax.sharding import PartitionSpec as P

DH = 128
HIDDEN = -1e30
LOG2E = 1.4426950408889634


def other_ctx(c, near):
    odd = lax.rem(c, 2)
    return c + 1 - 2 * odd if near else c - 1 + 2 * odd


def prep_kernel(
    place_ref, span_ref, noise_ref, mask_ref, table_ref, bias_ref, gate_ref, slot_ref, *, sizes
):
    ctx_count, groups, rows, span_total, level_count, by_span = sizes
    c, h = lax.div(place_ref[0], groups), lax.rem(place_ref[0], groups)
    tokens = groups * rows
    total = ctx_count * tokens
    bf16, f32 = jnp.bfloat16, jnp.float32

    def block_of(ctx, k):
        return ctx * groups + lax.rem(h - k + groups, groups)

    def spans_of(ctx, k):
        at = jnp.clip(ctx, 0, ctx_count - 1)
        return span_ref[pl.ds(block_of(at, k), 1), :]

    def as_column(row):
        return jnp.broadcast_to(row.astype(f32), (rows, rows)).T[:, :1].astype(jnp.int32)

    across = lax.broadcasted_iota(jnp.int32, (1, rows), 1)
    down = lax.broadcasted_iota(jnp.int32, (rows, 1), 0)
    span_lane = lax.broadcasted_iota(jnp.int32, (rows, span_total), 1)
    span_down = lax.broadcasted_iota(jnp.int32, (span_total, rows), 0)
    level_lane = lax.broadcasted_iota(jnp.int32, (rows, level_count), 1)
    query_span = [spans_of(c, k) for k in range(groups)]
    query_pos = [block_of(c, k) * rows + across for k in range(groups)]
    mask_low = mask_ref[...].astype(bf16)
    allowed_q = [
        lax.dot_general(
            mask_low,
            (span_down == row).astype(bf16),
            (((0,), (0,)), ((), ())),
            preferred_element_type=f32,
        ).astype(bf16)
        for row in query_span
    ]
    noise = noise_ref[...].astype(f32)
    for i, ctx in enumerate((c, other_ctx(c, True), other_ctx(c, False))):
        for k in range(groups):
            key_span = as_column(spans_of(ctx, k))
            key_pos = block_of(ctx, k) * rows + down
            valid = (key_pos >= 0) & (key_pos < total)
            onehot = key_span == span_lane
            at = slice((i * groups + k) * rows, (i * groups + k + 1) * rows)
            for p in range(groups):
                allowed = jnp.dot(
                    onehot.astype(bf16), allowed_q[p], preferred_element_type=f32
                )
                visible = (
                    (allowed > 0.5)
                    & (key_span <= query_span[p])
                    & (query_pos[p] - key_pos < tokens)
                    & valid
                )
                bias_ref[at, p * rows : (p + 1) * rows] = jnp.where(visible, 0.0, HIDDEN)
            if i > 0:
                continue
            level = jnp.sum(jnp.where(onehot, noise, 0.0), axis=1, keepdims=True)
            level_onehot = (level.astype(jnp.int32) == level_lane).astype(f32)
            gate_ref[at, :] = jnp.dot(
                level_onehot,
                table_ref[...],
                precision=lax.Precision.HIGHEST,
                preferred_element_type=f32,
            )
            if by_span:
                slot_ref[:, at] = (span_down == query_span[k]).astype(bf16)
            else:
                slot_ref[:, at] = level_onehot.T.astype(bf16)


def attention_kernel(
    place_ref,
    qo_own_ref, kv_own_ref, qo_ref, kv_ref,
    near_own_ref, near_far_ref, side_own_ref, side_far_ref,
    gate_ref, bias_ref, slot_ref,
    *rest, rows, tokens, q_size, heads,
):
    (
        back_ref, side_grad_far_ref, mixed_ref, dq_ref, own_ref, far_ref,
        near_grad_own_ref, near_grad_far_ref, side_grad_own_ref, sums_ref,
    ) = rest[-10:]
    scale = 1.0 / math.sqrt(DH)
    bf16, f32 = jnp.bfloat16, jnp.float32
    tile = 32

    def dot(left, right, left_dim, right_dim):
        return lax.dot_general(
            left, right, (((left_dim,), (right_dim,)), ((), ())), preferred_element_type=f32
        )

    def load(j):
        at = slice(j * DH, (j + 1) * DH)
        keys, values = [], []
        for ref in (
            kv_own_ref, kv_ref, near_own_ref, near_far_ref, side_own_ref, side_far_ref
        ):
            keys.append(ref[0, :, at])
            values.append(ref[1, :, at])
        keys, values = jnp.concatenate(keys, axis=0), jnp.concatenate(values, axis=0)
        queries = jnp.concatenate([qo_own_ref[0, :, at], qo_ref[0, :, at]], axis=0)
        cotangent = jnp.concatenate([qo_own_ref[1, :, at], qo_ref[1, :, at]], axis=0)
        blocks = []
        for start in range(0, tokens, q_size):
            span = slice(start, start + q_size)
            q, o = queries[span], cotangent[span].astype(f32)
            gate = gate_ref[span, at]
            g = (gate * o).astype(bf16)
            blocks.append((q, o, gate, g, dot(keys, q, 1, 1), dot(values, g, 1, 1)))
        return keys, values, blocks

    def work(j, keys, values, blocks):
        at = slice(j * DH, (j + 1) * DH)
        keys_t, values_t = keys.T, values.T
        key_grad = value_grad = sums = None
        for number, (q, o, gate, g, scores, prob_grad) in enumerate(blocks):
            start = number * q_size
            span = slice(start, start + q_size)
            count = scores.shape[0]
            tiles = [slice(r, r + tile) for r in range(0, count, tile)]
            raised, top = [], None
            for t in tiles:
                part = scores[t] * (scale * LOG2E) + bias_ref[t, span]
                raised.append(part)
                high = jnp.max(part.reshape(tile // 8, 8, q_size), axis=0)
                top = high if top is None else jnp.maximum(top, high)
            top = jnp.max(top, axis=0, keepdims=True)
            total = None
            for i in range(len(tiles)):
                raised[i] = jnp.exp2(raised[i] - top)
                part = jnp.sum(raised[i].reshape(tile // 8, 8, q_size), axis=0)
                total = part if total is None else total + part
            inverse = 1.0 / jnp.sum(total, axis=0, keepdims=True)
            low = jnp.concatenate([(part * inverse).astype(bf16) for part in raised], axis=0)
            attended_t = dot(values_t, low, 1, 0).astype(bf16)
            row_dot = jnp.sum(g.T.astype(f32) * attended_t.astype(f32), axis=0, keepdims=True)
            attended = attended_t.T.astype(f32)
            score_grad = jnp.concatenate(
                [
                    (part * ((prob_grad[t] - row_dot) * inverse)).astype(bf16)
                    for part, t in zip(raised, tiles)
                ],
                axis=0,
            )
            query_grad = (dot(keys_t, score_grad, 1, 0) * scale).astype(bf16).T
            mixed = (gate * attended).astype(bf16)
            if start == 0:
                mixed_ref[:, at] = mixed[:rows]
                dq_ref[:, at] = query_grad[:rows]
                back_ref[0, : q_size - rows, at] = mixed[rows:]
                back_ref[1, : q_size - rows, at] = query_grad[rows:]
            else:
                back_ref[0, start - rows : start - rows + q_size, at] = mixed
                back_ref[1, start - rows : start - rows + q_size, at] = query_grad
            dk, dv = dot(score_grad, q, 1, 0), dot(low, g, 1, 0)
            product = o * attended
            high = product.astype(bf16)
            rest = (product - high.astype(f32)).astype(bf16)
            both = dot(slot_ref[:, span], jnp.concatenate([high, rest], axis=1), 1, 0)
            part = both[:, :DH] + both[:, DH:]
            key_grad = dk if key_grad is None else key_grad + dk
            value_grad = dv if value_grad is None else value_grad + dv
            sums = part if sums is None else sums + part
        sums_ref[:, at] = sums
        for i, grad in ((0, key_grad * scale), (1, value_grad)):
            own_ref[i, :, at] = grad[:rows]
            far_ref[i, :, at] = grad[rows:tokens]
            low = grad[tokens:].astype(bf16)
            near_grad_own_ref[i, :, at] = low[:rows]
            near_grad_far_ref[i, :, at] = low[rows:tokens]
            side_grad_own_ref[i, :, at] = low[tokens : tokens + rows]
            side_grad_far_ref[i, :, at] = low[tokens + rows :]

    ready = load(0)
    for j in range(heads):
        following = load(j + 1) if j + 1 < heads else None
        work(j, *ready)
        ready = following


def pack_kernel(place_ref, first_ref, second_ref, own_ref, *rest, groups):
    *far_refs, sems = rest
    rows, width = own_ref.shape[1:]
    copies = []

    def copy(ref, start, to):
        cols = pl.ds(pl.multiple_of(start, DH), to.shape[1])
        copies.append(pltpu.make_async_copy(ref.at[:, cols], to, sems.at[len(copies)]))
        copies[-1].start()

    for k in (*range(1, groups), 0):
        start = lax.rem(place_ref[0] + k, groups) * width
        for i, ref in enumerate((first_ref, second_ref)):
            if k == 0:
                copy(ref, start, own_ref.at[i])
                continue
            for p, far_ref in enumerate(far_refs):
                at = pl.ds((k - 1) * rows, rows)
                copy(ref, start + p * far_ref.shape[2], far_ref.at[i, at])
    for one in copies:
        one.wait()


def far_sum_kernel(part_ref, near_ref, *refs):
    *side_refs, out_ref = refs
    for p, ref in enumerate(side_refs):
        width = ref.shape[2]
        cols = slice(p * width, (p + 1) * width)
        total = part_ref[:, :, cols] + near_ref[:, :, cols].astype(jnp.float32)
        out_ref[:, :, cols] = (total + ref[...].astype(jnp.float32)).astype(out_ref.dtype)


def finish_kernel(place_ref, part_ref, near_ref, side_ref, *refs, groups, parts):
    count = (groups - 1) * (parts + 1)
    slabs, outs, (total_ref, sems) = refs[:count], refs[count + 2 : count + 6], refs[count + 6 :]
    width = part_ref.shape[2]
    copies = []

    def copy(slab, first, second, start):
        cols = pl.ds(pl.multiple_of(start, DH), slab.shape[2])
        for i, ref in enumerate((first, second)):
            copies.append(pltpu.make_async_copy(slab.at[i], ref.at[:, cols], sems.at[len(copies)]))
            copies[-1].start()

    for k in range(1, groups):
        start = lax.rem(place_ref[0] + k, groups) * width
        for p in range(parts):
            slab = slabs[p * (groups - 1) + k - 1]
            copy(slab, outs[0], outs[1], start + p * slab.shape[2])
        copy(slabs[parts * (groups - 1) + k - 1], outs[2], outs[3], start)
    total = part_ref[...] + near_ref[...].astype(jnp.float32) + side_ref[...].astype(jnp.float32)
    total_ref[...] = total.astype(total_ref.dtype)
    copy(total_ref, outs[2], outs[3], lax.rem(place_ref[0], groups) * width)
    for one in copies:
        one.wait()


def spread_kernel(place_ref, noise_ref, *refs, by_span, groups):
    *slabs, out_ref = refs
    levels = lax.broadcasted_iota(jnp.int32, (out_ref.shape[0], noise_ref.shape[1]), 0)
    onehot = (levels == noise_ref[...]).astype(jnp.bfloat16)
    for j, ref in enumerate(slabs):
        sums = ref[...]
        width = sums.shape[1]
        if by_span:
            total = None
            for _ in range(3):
                piece = sums.astype(jnp.bfloat16)
                sums = sums - piece.astype(jnp.float32)
                part = jnp.dot(onehot, piece, preferred_element_type=jnp.float32)
                total = part if total is None else total + part
            sums = total
        start = lax.bitwise_xor(lax.rem(place_ref[0], groups), j) * width
        out_ref[:, pl.ds(pl.multiple_of(start, DH), width)] = sums


def per_device(
    queries, key_rows, value_rows, out_cotangent, gate_table, span_ids, noise_level, block_mask
):
    groups = lax.axis_size("head")
    ctx_count = lax.axis_size("ctx")
    rows, full_width = queries.shape
    width = full_width // groups
    heads = width // DH
    tokens = rows * groups
    far_rows = tokens - rows
    parts = 2 if heads % 2 == 0 else 1
    part_width = width // parts
    part_heads = heads // parts
    span_total = noise_level.shape[0]
    level_count = gate_table.shape[0]
    by_span = span_total <= level_count // 2
    slots = span_total if by_span else level_count
    c = lax.axis_index("ctx")
    h = lax.axis_index("head")
    place = (c * groups + h).astype(jnp.int32).reshape(1)
    head_at = lambda place: lax.rem(place[0], groups)
    bf16, f32 = jnp.bfloat16, jnp.float32
    tie = lax.optimization_barrier

    near_pairs = [(i, i ^ 1) for i in range(ctx_count)]
    side_of = [i - 1 + 2 * (i % 2) for i in range(ctx_count)]
    side_pairs = [(i, j if 0 <= j < ctx_count else i) for i, j in enumerate(side_of)]

    whole = lambda shape: pl.BlockSpec(shape, lambda i, place: (0,) * len(shape))
    limit = (26 if tokens <= 256 else 56) * 1024 * 1024
    params = pltpu.CompilerParams(vmem_limit_bytes=limit)
    alone = pltpu.CompilerParams(vmem_limit_bytes=56 * 1024 * 1024)
    cheap = pl.CostEstimate(flops=1, bytes_accessed=1, transcendentals=0)
    in_vmem = pl.BlockSpec(memory_space=pltpu.VMEM)
    anywhere = pl.BlockSpec(memory_space=pl.ANY)
    small = pltpu.CompilerParams(vmem_limit_bytes=(12 if tokens <= 256 else 36) * 1024 * 1024)

    def pack(first, second, params):
        far_shape = (2, far_rows, part_width)
        return pl.pallas_call(
            functools.partial(pack_kernel, groups=groups),
            grid_spec=pltpu.PrefetchScalarGridSpec(
                num_scalar_prefetch=1,
                in_specs=[anywhere] * 2,
                out_specs=[in_vmem] * (1 + parts),
                scratch_shapes=[pltpu.SemaphoreType.DMA((2 + 2 * (groups - 1) * parts,))],
            ),
            out_shape=[jax.ShapeDtypeStruct((2, rows, width), bf16)]
            + [jax.ShapeDtypeStruct(far_shape, bf16)] * parts,
            compiler_params=params,
            cost_estimate=cheap,
            name="pack",
        )(place, first, second)

    def to_peers(slab):
        arrived = []
        for k in range(1, groups):
            part = slab if groups == 2 else slab[:, (k - 1) * rows : k * rows]
            pairs = [(i, (i + k) % groups) for i in range(groups)]
            arrived.append(lax.ppermute(part, "head", pairs))
        return arrived[0] if groups == 2 else jnp.concatenate(arrived, axis=1)

    def from_peers(slab):
        arrived = []
        for k in range(1, groups):
            part = slab if groups == 2 else slab[:, (k - 1) * rows : k * rows]
            pairs = [(i, (i - k) % groups) for i in range(groups)]
            arrived.append(lax.ppermute(part, "head", pairs))
        return arrived

    kv_own, *kv_sent = pack(key_rows, value_rows, alone)
    qo_own, *qo_sent = pack(queries, out_cotangent, small)
    side_own = lax.ppermute(kv_own, "ctx", side_pairs)
    near_own = lax.ppermute(kv_own, "ctx", near_pairs)
    kv_far = [to_peers(slab) for slab in kv_sent]
    side_far = [lax.ppermute(slab, "ctx", side_pairs) for slab in kv_far]
    near_far = [lax.ppermute(slab, "ctx", near_pairs) for slab in kv_far]
    qo_far = [to_peers(tie((slab, far))[0]) for slab, far in zip(qo_sent, kv_far)]

    sizes = (ctx_count, groups, rows, span_total, level_count, by_span)
    whole = lambda shape: pl.BlockSpec(shape, lambda i, place: (0,) * len(shape))
    bias, gate, slot = pl.pallas_call(
        functools.partial(prep_kernel, sizes=sizes),
        grid_spec=pltpu.PrefetchScalarGridSpec(
            num_scalar_prefetch=1,
            grid=(1,),
            in_specs=[
                whole((ctx_count * groups, rows)),
                whole((1, span_total)),
                whole((span_total, span_total)),
                pl.BlockSpec((level_count, width), lambda i, place: (0, head_at(place))),
            ],
            out_specs=[
                whole((3 * tokens, tokens)),
                whole((tokens, width)),
                whole((slots, tokens)),
            ],
        ),
        out_shape=[
            jax.ShapeDtypeStruct((3 * tokens, tokens), f32),
            jax.ShapeDtypeStruct((tokens, width), f32),
            jax.ShapeDtypeStruct((slots, tokens), bf16),
        ],
        compiler_params=small,
        cost_estimate=cheap,
        name="prep",
    )(
        place,
        span_ids.reshape(ctx_count * groups, rows),
        noise_level.reshape(1, span_total),
        block_mask,
        gate_table,
    )

    batch = next(n for n in (3, 2, 1) if part_heads % n == 0) if tokens <= 256 else 1
    steps = part_heads // batch
    block = batch * DH
    q_size = min(256, tokens)

    def attention(p, joint):
        pair = lambda count: pl.BlockSpec((2, count, block), lambda i, place: (0, 0, i))
        at_part = lambda count: pl.BlockSpec(
            (2, count, block), lambda i, place: (0, 0, p * steps + i)
        )
        at_head = pl.BlockSpec(
            (rows, block), lambda i, place: (0, (head_at(place) * parts + p) * steps + i)
        )
        column = lambda count: pl.BlockSpec((count, block), lambda i, place: (0, p * steps + i))
        struct = jax.ShapeDtypeStruct
        inputs = [
            qo_own, kv_own, qo_far[p], kv_far[p],
            near_own, near_far[p], side_own, side_far[p],
            gate, bias, slot,
        ]
        return pl.pallas_call(
            functools.partial(
                attention_kernel, rows=rows, tokens=tokens, q_size=q_size, heads=batch
            ),
            grid_spec=pltpu.PrefetchScalarGridSpec(
                num_scalar_prefetch=1,
                grid=(steps,),
                in_specs=[
                    at_part(rows), at_part(rows), pair(far_rows), pair(far_rows),
                    at_part(rows), pair(far_rows), at_part(rows), pair(far_rows),
                    column(tokens), whole((3 * tokens, tokens)), whole((slots, tokens)),
                ]
                + [pl.BlockSpec(memory_space=pl.ANY)] * len(joint),
                out_specs=[
                    pair(far_rows), pair(far_rows),
                    at_head, at_head, at_part(rows), at_part(far_rows),
                    at_part(rows), at_part(far_rows), at_part(rows), column(slots),
                ],
            ),
            out_shape=[
                struct((2, far_rows, part_width), bf16),
                struct((2, far_rows, part_width), bf16),
                struct((rows, full_width), bf16),
                struct((rows, full_width), bf16),
                struct((2, rows, width), f32),
                struct((2, far_rows, width), f32),
                struct((2, rows, width), bf16),
                struct((2, far_rows, width), bf16),
                struct((2, rows, width), bf16),
                struct((slots, width), f32),
            ],
            input_output_aliases={1 + len(inputs) + i: 2 + i for i in range(len(joint))},
            compiler_params=params,
            cost_estimate=cheap,
            name="attention",
        )(place, *inputs, *joint)

    joint, back_far, side_back_far = (), [], []
    for p in range(parts):
        back, side_grad_far, *joint = attention(p, joint)
        if p > 0:
            back, side_grad_far, joint, back_far, side_back_far = tie(
                (back, side_grad_far, joint, back_far, side_back_far)
            )
        side_back_far.append(lax.ppermute(side_grad_far, "ctx", side_pairs))
        back_far.append(from_peers(back))
    mixed, query_grad, own, far, near_grad_own, near_grad_far, side_grad_own, sums = joint

    near_back_far = lax.ppermute(near_grad_far, "ctx", near_pairs)
    near_back_own = lax.ppermute(near_grad_own, "ctx", near_pairs)
    side_back_own = lax.ppermute(side_grad_own, "ctx", side_pairs)

    def shifted(array, step):
        return lax.ppermute(array, "ctx", [(i, i ^ step) for i in range(ctx_count)])

    def rounds(steps, sums):
        for one, two in zip(steps[::2], [*steps[1::2], None]):
            if two is None:
                sums = sums + shifted(sums, one)
                continue
            across = [shifted(sums, step) for step in (one, two, one ^ two)]
            sums = (sums + across[0]) + (across[1] + across[2])
        return sums

    bits = [1 << n for n in range(ctx_count.bit_length() - 1)]
    sums = rounds([bits[0], bits[2]], sums)
    side_back_far, back_far = tie((side_back_far, back_far))
    far_grad = pl.pallas_call(
        far_sum_kernel,
        in_specs=[in_vmem] * (2 + parts),
        out_specs=in_vmem,
        out_shape=jax.ShapeDtypeStruct((2, far_rows, width), bf16),
        compiler_params=small,
        cost_estimate=cheap,
        name="far_sum",
    )(far, near_back_far, *side_back_far)
    grad_far = from_peers(far_grad)

    def to_all(steps, sums):
        slabs = [rounds(steps, sums)]
        for step in (1 << n for n in range(groups.bit_length() - 1)):
            pairs = [(i, i ^ step) for i in range(groups)]
            slabs = slabs + [lax.ppermute(slab, "head", pairs) for slab in slabs]
        return slabs

    rest = [bits[1], *bits[3:]]
    sums, _ = tie((sums, far_grad))
    slabs = lax.cond(
        noise_level[0] >= 0,
        functools.partial(to_all, rest),
        functools.partial(to_all, rest[::-1]),
        sums,
    )
    slabs, grad_far, side_back_own = tie((slabs, grad_far, side_back_own))
    gate_grad = pl.pallas_call(
        functools.partial(spread_kernel, by_span=by_span, groups=groups),
        grid_spec=pltpu.PrefetchScalarGridSpec(
            num_scalar_prefetch=1,
            grid=(1,),
            in_specs=[whole((1, span_total))] + [whole((slots, width))] * groups,
            out_specs=whole((level_count, full_width)),
        ),
        out_shape=jax.ShapeDtypeStruct((level_count, full_width), f32),
        compiler_params=small,
        cost_estimate=cheap,
        name="spread",
    )(place, noise_level.reshape(1, span_total), *slabs)

    arrived = [slab for slabs in back_far for slab in slabs] + grad_far
    outputs = pl.pallas_call(
        functools.partial(finish_kernel, groups=groups, parts=parts),
        grid_spec=pltpu.PrefetchScalarGridSpec(
            num_scalar_prefetch=1,
            in_specs=[in_vmem] * (3 + len(arrived)) + [anywhere] * 2,
            out_specs=[anywhere] * 4,
            scratch_shapes=[
                pltpu.VMEM((2, rows, width), bf16),
                pltpu.SemaphoreType.DMA((2 * len(arrived) + 2,)),
            ],
        ),
        out_shape=[jax.ShapeDtypeStruct((rows, full_width), bf16)] * 4,
        input_output_aliases={4 + len(arrived): 0, 5 + len(arrived): 1},
        compiler_params=small,
        cost_estimate=cheap,
        name="finish",
    )(place, own, near_back_own, side_back_own, *arrived, mixed, query_grad)
    return (*outputs, gate_grad)


def solution(mesh):
    sharded = P(("ctx", "head"), None)
    return jax.shard_map(
        per_device,
        mesh=mesh,
        in_specs=(sharded,) * 4 + (P(),) * 4,
        out_specs=(sharded,) * 4 + (P(),),
        check_vma=False,
    )
```

```python
import functools
import math

import jax
import jax.numpy as jnp
from jax import lax
from jax.experimental import pallas as pl
from jax.experimental.pallas import tpu as pltpu
from jax.sharding import PartitionSpec as P

DH = 128
HIDDEN = -1e30
LOG2E = 1.4426950408889634


def other_ctx(c, near):
    odd = lax.rem(c, 2)
    return c + 1 - 2 * odd if near else c - 1 + 2 * odd


def prep_kernel(
    place_ref, span_ref, noise_ref, mask_ref, table_ref, bias_ref, gate_ref, slot_ref, *, sizes
):
    ctx_count, groups, rows, span_total, level_count, by_span = sizes
    c, h = lax.div(place_ref[0], groups), lax.rem(place_ref[0], groups)
    tokens = groups * rows
    total = ctx_count * tokens
    bf16, f32 = jnp.bfloat16, jnp.float32

    def block_of(ctx, k):
        return ctx * groups + lax.rem(h - k + groups, groups)

    def spans_of(ctx, k):
        at = jnp.clip(ctx, 0, ctx_count - 1)
        return span_ref[pl.ds(block_of(at, k), 1), :]

    def as_column(row):
        return jnp.broadcast_to(row.astype(f32), (rows, rows)).T[:, :1].astype(jnp.int32)

    across = lax.broadcasted_iota(jnp.int32, (1, rows), 1)
    down = lax.broadcasted_iota(jnp.int32, (rows, 1), 0)
    span_lane = lax.broadcasted_iota(jnp.int32, (rows, span_total), 1)
    span_down = lax.broadcasted_iota(jnp.int32, (span_total, rows), 0)
    level_lane = lax.broadcasted_iota(jnp.int32, (rows, level_count), 1)
    query_span = [spans_of(c, k) for k in range(groups)]
    query_pos = [block_of(c, k) * rows + across for k in range(groups)]
    mask_low = mask_ref[...].astype(bf16)
    allowed_q = [
        lax.dot_general(
            mask_low,
            (span_down == row).astype(bf16),
            (((0,), (0,)), ((), ())),
            preferred_element_type=f32,
        ).astype(bf16)
        for row in query_span
    ]
    noise = noise_ref[...].astype(f32)
    for i, ctx in enumerate((c, other_ctx(c, True), other_ctx(c, False))):
        for k in range(groups):
            key_span = as_column(spans_of(ctx, k))
            key_pos = block_of(ctx, k) * rows + down
            valid = (key_pos >= 0) & (key_pos < total)
            onehot = key_span == span_lane
            at = slice((i * groups + k) * rows, (i * groups + k + 1) * rows)
            for p in range(groups):
                allowed = jnp.dot(
                    onehot.astype(bf16), allowed_q[p], preferred_element_type=f32
                )
                visible = (
                    (allowed > 0.5)
                    & (key_span <= query_span[p])
                    & (query_pos[p] - key_pos < tokens)
                    & valid
                )
                bias_ref[at, p * rows : (p + 1) * rows] = jnp.where(visible, 0.0, HIDDEN)
            if i > 0:
                continue
            level = jnp.sum(jnp.where(onehot, noise, 0.0), axis=1, keepdims=True)
            level_onehot = (level.astype(jnp.int32) == level_lane).astype(f32)
            gate_ref[at, :] = jnp.dot(
                level_onehot,
                table_ref[...],
                precision=lax.Precision.HIGHEST,
                preferred_element_type=f32,
            )
            if by_span:
                slot_ref[:, at] = (span_down == query_span[k]).astype(bf16)
            else:
                slot_ref[:, at] = level_onehot.T.astype(bf16)


def attention_kernel(
    place_ref,
    qo_own_ref, kv_own_ref, qo_ref, kv_ref,
    near_own_ref, near_far_ref, side_own_ref, side_far_ref,
    gate_ref, bias_ref, slot_ref,
    *rest, rows, tokens, q_size, heads,
):
    (
        back_ref, side_grad_far_ref, mixed_ref, dq_ref, own_ref, far_ref,
        near_grad_own_ref, near_grad_far_ref, side_grad_own_ref, sums_ref,
    ) = rest[-10:]
    scale = 1.0 / math.sqrt(DH)
    bf16, f32 = jnp.bfloat16, jnp.float32
    tile = 32

    def dot(left, right, left_dim, right_dim):
        return lax.dot_general(
            left, right, (((left_dim,), (right_dim,)), ((), ())), preferred_element_type=f32
        )

    def load(j):
        at = slice(j * DH, (j + 1) * DH)
        keys, values = [], []
        for ref in (
            kv_own_ref, kv_ref, near_own_ref, near_far_ref, side_own_ref, side_far_ref
        ):
            keys.append(ref[0, :, at])
            values.append(ref[1, :, at])
        keys, values = jnp.concatenate(keys, axis=0), jnp.concatenate(values, axis=0)
        queries = jnp.concatenate([qo_own_ref[0, :, at], qo_ref[0, :, at]], axis=0)
        cotangent = jnp.concatenate([qo_own_ref[1, :, at], qo_ref[1, :, at]], axis=0)
        blocks = []
        for start in range(0, tokens, q_size):
            span = slice(start, start + q_size)
            q, o = queries[span], cotangent[span].astype(f32)
            gate = gate_ref[span, at]
            g = (gate * o).astype(bf16)
            blocks.append((q, o, gate, g, dot(keys, q, 1, 1), dot(values, g, 1, 1)))
        return keys, values, blocks

    def work(j, keys, values, blocks):
        at = slice(j * DH, (j + 1) * DH)
        keys_t, values_t = keys.T, values.T
        key_grad = value_grad = sums = None
        for number, (q, o, gate, g, scores, prob_grad) in enumerate(blocks):
            start = number * q_size
            span = slice(start, start + q_size)
            count = scores.shape[0]
            tiles = [slice(r, r + tile) for r in range(0, count, tile)]
            raised, top = [], None
            for t in tiles:
                part = scores[t] * (scale * LOG2E) + bias_ref[t, span]
                raised.append(part)
                high = jnp.max(part.reshape(tile // 8, 8, q_size), axis=0)
                top = high if top is None else jnp.maximum(top, high)
            top = jnp.max(top, axis=0, keepdims=True)
            total = None
            for i in range(len(tiles)):
                raised[i] = jnp.exp2(raised[i] - top)
                part = jnp.sum(raised[i].reshape(tile // 8, 8, q_size), axis=0)
                total = part if total is None else total + part
            inverse = 1.0 / jnp.sum(total, axis=0, keepdims=True)
            low = jnp.concatenate([(part * inverse).astype(bf16) for part in raised], axis=0)
            attended_t = dot(values_t, low, 1, 0).astype(bf16)
            row_dot = jnp.sum(g.T.astype(f32) * attended_t.astype(f32), axis=0, keepdims=True)
            attended = attended_t.T.astype(f32)
            score_grad = jnp.concatenate(
                [
                    (part * ((prob_grad[t] - row_dot) * inverse)).astype(bf16)
                    for part, t in zip(raised, tiles)
                ],
                axis=0,
            )
            query_grad = (dot(keys_t, score_grad, 1, 0) * scale).astype(bf16).T
            mixed = (gate * attended).astype(bf16)
            if start == 0:
                mixed_ref[:, at] = mixed[:rows]
                dq_ref[:, at] = query_grad[:rows]
                back_ref[0, : q_size - rows, at] = mixed[rows:]
                back_ref[1, : q_size - rows, at] = query_grad[rows:]
            else:
                back_ref[0, start - rows : start - rows + q_size, at] = mixed
                back_ref[1, start - rows : start - rows + q_size, at] = query_grad
            dk, dv = dot(score_grad, q, 1, 0), dot(low, g, 1, 0)
            product = o * attended
            high = product.astype(bf16)
            rest = (product - high.astype(f32)).astype(bf16)
            both = dot(slot_ref[:, span], jnp.concatenate([high, rest], axis=1), 1, 0)
            part = both[:, :DH] + both[:, DH:]
            key_grad = dk if key_grad is None else key_grad + dk
            value_grad = dv if value_grad is None else value_grad + dv
            sums = part if sums is None else sums + part
        sums_ref[:, at] = sums
        for i, grad in ((0, key_grad * scale), (1, value_grad)):
            own_ref[i, :, at] = grad[:rows]
            far_ref[i, :, at] = grad[rows:tokens]
            low = grad[tokens:].astype(bf16)
            near_grad_own_ref[i, :, at] = low[:rows]
            near_grad_far_ref[i, :, at] = low[rows:tokens]
            side_grad_own_ref[i, :, at] = low[tokens : tokens + rows]
            side_grad_far_ref[i, :, at] = low[tokens + rows :]

    ready = load(0)
    for j in range(heads):
        following = load(j + 1) if j + 1 < heads else None
        work(j, *ready)
        ready = following


def pack_kernel(place_ref, first_ref, second_ref, own_ref, *rest, groups):
    *far_refs, sems = rest
    rows, width = own_ref.shape[1:]
    copies = []

    def copy(ref, start, to):
        cols = pl.ds(pl.multiple_of(start, DH), to.shape[1])
        copies.append(pltpu.make_async_copy(ref.at[:, cols], to, sems.at[len(copies)]))
        copies[-1].start()

    for k in (*range(1, groups), 0):
        start = lax.rem(place_ref[0] + k, groups) * width
        for i, ref in enumerate((first_ref, second_ref)):
            if k == 0:
                copy(ref, start, own_ref.at[i])
                continue
            for p, far_ref in enumerate(far_refs):
                at = pl.ds((k - 1) * rows, rows)
                copy(ref, start + p * far_ref.shape[2], far_ref.at[i, at])
    for one in copies:
        one.wait()


def far_sum_kernel(part_ref, near_ref, *refs):
    *side_refs, out_ref = refs
    for p, ref in enumerate(side_refs):
        width = ref.shape[2]
        cols = slice(p * width, (p + 1) * width)
        total = part_ref[:, :, cols] + near_ref[:, :, cols].astype(jnp.float32)
        out_ref[:, :, cols] = (total + ref[...].astype(jnp.float32)).astype(out_ref.dtype)


def finish_kernel(place_ref, noise_ref, part_ref, near_ref, side_ref, *refs, groups, parts, by_span):
    count = (groups - 1) * (parts + 1)
    slot_refs, refs = refs[:groups], refs[groups:]
    slabs, outs = refs[:count], refs[count + 2 : count + 7]
    total_ref, pieces_ref, gate_ref, sems = refs[count + 7 :]
    width = part_ref.shape[2]
    copies = []

    def copy(slab, first, second, start):
        cols = pl.ds(pl.multiple_of(start, DH), slab.shape[2])
        for i, ref in enumerate((first, second)):
            copies.append(pltpu.make_async_copy(slab.at[i], ref.at[:, cols], sems.at[len(copies)]))
            copies[-1].start()

    for k in range(1, groups):
        start = lax.rem(place_ref[0] + k, groups) * width
        for p in range(parts):
            slab = slabs[p * (groups - 1) + k - 1]
            copy(slab, outs[0], outs[1], start + p * slab.shape[2])
        copy(slabs[parts * (groups - 1) + k - 1], outs[2], outs[3], start)
    total = part_ref[...] + near_ref[...].astype(jnp.float32) + side_ref[...].astype(jnp.float32)
    total_ref[...] = total.astype(total_ref.dtype)
    copy(total_ref, outs[2], outs[3], lax.rem(place_ref[0], groups) * width)
    slots = pieces_ref.shape[0] // 3
    levels = lax.broadcasted_iota(jnp.int32, (gate_ref.shape[0], noise_ref.shape[1]), 0)
    onehot = (levels == noise_ref[...]).astype(jnp.bfloat16)
    if by_span:
        pieces_ref[...] = jnp.zeros_like(pieces_ref)
    for j, ref in enumerate(slot_refs):
        sums = ref[...]
        if by_span:
            for n in range(3):
                piece = sums.astype(jnp.bfloat16)
                sums = sums - piece.astype(jnp.float32)
                pieces_ref[n * slots : n * slots + sums.shape[0]] = piece
            sums = jnp.dot(onehot, pieces_ref[...], preferred_element_type=jnp.float32)
        start = lax.bitwise_xor(lax.rem(place_ref[0], groups), j) * width
        cols = pl.ds(pl.multiple_of(start, DH), width)
        gate_ref[:, cols] = sums
        copies.append(
            pltpu.make_async_copy(gate_ref.at[:, cols], outs[4].at[:, cols], sems.at[len(copies)])
        )
        copies[-1].start()
    for one in copies:
        one.wait()


def per_device(
    queries, key_rows, value_rows, out_cotangent, gate_table, span_ids, noise_level, block_mask
):
    groups = lax.axis_size("head")
    ctx_count = lax.axis_size("ctx")
    rows, full_width = queries.shape
    width = full_width // groups
    heads = width // DH
    tokens = rows * groups
    far_rows = tokens - rows
    parts = 2 if heads % 2 == 0 else 1
    part_width = width // parts
    part_heads = heads // parts
    span_total = noise_level.shape[0]
    level_count = gate_table.shape[0]
    by_span = span_total <= level_count // 2
    slots = span_total if by_span else level_count
    c = lax.axis_index("ctx")
    h = lax.axis_index("head")
    place = (c * groups + h).astype(jnp.int32).reshape(1)
    head_at = lambda place: lax.rem(place[0], groups)
    bf16, f32 = jnp.bfloat16, jnp.float32
    tie = lax.optimization_barrier

    near_pairs = [(i, i ^ 1) for i in range(ctx_count)]
    side_of = [i - 1 + 2 * (i % 2) for i in range(ctx_count)]
    side_pairs = [(i, j if 0 <= j < ctx_count else i) for i, j in enumerate(side_of)]

    whole = lambda shape: pl.BlockSpec(shape, lambda i, place: (0,) * len(shape))
    limit = (26 if tokens <= 256 else 56) * 1024 * 1024
    params = pltpu.CompilerParams(vmem_limit_bytes=limit)
    alone = pltpu.CompilerParams(vmem_limit_bytes=56 * 1024 * 1024)
    cheap = pl.CostEstimate(flops=1, bytes_accessed=1, transcendentals=0)
    in_vmem = pl.BlockSpec(memory_space=pltpu.VMEM)
    anywhere = pl.BlockSpec(memory_space=pl.ANY)
    small = pltpu.CompilerParams(vmem_limit_bytes=(12 if tokens <= 256 else 36) * 1024 * 1024)

    def pack(first, second, params):
        far_shape = (2, far_rows, part_width)
        return pl.pallas_call(
            functools.partial(pack_kernel, groups=groups),
            grid_spec=pltpu.PrefetchScalarGridSpec(
                num_scalar_prefetch=1,
                in_specs=[anywhere] * 2,
                out_specs=[in_vmem] * (1 + parts),
                scratch_shapes=[pltpu.SemaphoreType.DMA((2 + 2 * (groups - 1) * parts,))],
            ),
            out_shape=[jax.ShapeDtypeStruct((2, rows, width), bf16)]
            + [jax.ShapeDtypeStruct(far_shape, bf16)] * parts,
            compiler_params=params,
            cost_estimate=cheap,
            name="pack",
        )(place, first, second)

    def to_peers(slab):
        arrived = []
        for k in range(1, groups):
            part = slab if groups == 2 else slab[:, (k - 1) * rows : k * rows]
            pairs = [(i, (i + k) % groups) for i in range(groups)]
            arrived.append(lax.ppermute(part, "head", pairs))
        return arrived[0] if groups == 2 else jnp.concatenate(arrived, axis=1)

    def from_peers(slab):
        arrived = []
        for k in range(1, groups):
            part = slab if groups == 2 else slab[:, (k - 1) * rows : k * rows]
            pairs = [(i, (i - k) % groups) for i in range(groups)]
            arrived.append(lax.ppermute(part, "head", pairs))
        return arrived

    kv_own, *kv_sent = pack(key_rows, value_rows, alone)
    qo_own, *qo_sent = pack(queries, out_cotangent, small)
    side_own = lax.ppermute(kv_own, "ctx", side_pairs)
    near_own = lax.ppermute(kv_own, "ctx", near_pairs)
    kv_far = [to_peers(slab) for slab in kv_sent]
    side_far = [lax.ppermute(slab, "ctx", side_pairs) for slab in kv_far]
    near_far = [lax.ppermute(slab, "ctx", near_pairs) for slab in kv_far]
    qo_far = [to_peers(tie((slab, far))[0]) for slab, far in zip(qo_sent, kv_far)]

    sizes = (ctx_count, groups, rows, span_total, level_count, by_span)
    whole = lambda shape: pl.BlockSpec(shape, lambda i, place: (0,) * len(shape))
    bias, gate, slot = pl.pallas_call(
        functools.partial(prep_kernel, sizes=sizes),
        grid_spec=pltpu.PrefetchScalarGridSpec(
            num_scalar_prefetch=1,
            grid=(1,),
            in_specs=[
                whole((ctx_count * groups, rows)),
                whole((1, span_total)),
                whole((span_total, span_total)),
                pl.BlockSpec((level_count, width), lambda i, place: (0, head_at(place))),
            ],
            out_specs=[
                whole((3 * tokens, tokens)),
                whole((tokens, width)),
                whole((slots, tokens)),
            ],
        ),
        out_shape=[
            jax.ShapeDtypeStruct((3 * tokens, tokens), f32),
            jax.ShapeDtypeStruct((tokens, width), f32),
            jax.ShapeDtypeStruct((slots, tokens), bf16),
        ],
        compiler_params=small,
        cost_estimate=cheap,
        name="prep",
    )(
        place,
        span_ids.reshape(ctx_count * groups, rows),
        noise_level.reshape(1, span_total),
        block_mask,
        gate_table,
    )

    batch = next(n for n in (3, 2, 1) if part_heads % n == 0) if tokens <= 256 else 1
    steps = part_heads // batch
    block = batch * DH
    q_size = min(256, tokens)

    def attention(p, joint):
        pair = lambda count: pl.BlockSpec((2, count, block), lambda i, place: (0, 0, i))
        at_part = lambda count: pl.BlockSpec(
            (2, count, block), lambda i, place: (0, 0, p * steps + i)
        )
        at_head = pl.BlockSpec(
            (rows, block), lambda i, place: (0, (head_at(place) * parts + p) * steps + i)
        )
        column = lambda count: pl.BlockSpec((count, block), lambda i, place: (0, p * steps + i))
        struct = jax.ShapeDtypeStruct
        inputs = [
            qo_own, kv_own, qo_far[p], kv_far[p],
            near_own, near_far[p], side_own, side_far[p],
            gate, bias, slot,
        ]
        return pl.pallas_call(
            functools.partial(
                attention_kernel, rows=rows, tokens=tokens, q_size=q_size, heads=batch
            ),
            grid_spec=pltpu.PrefetchScalarGridSpec(
                num_scalar_prefetch=1,
                grid=(steps,),
                in_specs=[
                    at_part(rows), at_part(rows), pair(far_rows), pair(far_rows),
                    at_part(rows), pair(far_rows), at_part(rows), pair(far_rows),
                    column(tokens), whole((3 * tokens, tokens)), whole((slots, tokens)),
                ]
                + [pl.BlockSpec(memory_space=pl.ANY)] * len(joint),
                out_specs=[
                    pair(far_rows), pair(far_rows),
                    at_head, at_head, at_part(rows), at_part(far_rows),
                    at_part(rows), at_part(far_rows), at_part(rows), column(slots),
                ],
            ),
            out_shape=[
                struct((2, far_rows, part_width), bf16),
                struct((2, far_rows, part_width), bf16),
                struct((rows, full_width), bf16),
                struct((rows, full_width), bf16),
                struct((2, rows, width), f32),
                struct((2, far_rows, width), f32),
                struct((2, rows, width), bf16),
                struct((2, far_rows, width), bf16),
                struct((2, rows, width), bf16),
                struct((slots, width), f32),
            ],
            input_output_aliases={1 + len(inputs) + i: 2 + i for i in range(len(joint))},
            compiler_params=params,
            cost_estimate=cheap,
            name="attention",
        )(place, *inputs, *joint)

    joint, back_far, side_back_far = (), [], []
    for p in range(parts):
        back, side_grad_far, *joint = attention(p, joint)
        if p > 0:
            back, side_grad_far, joint, back_far, side_back_far = tie(
                (back, side_grad_far, joint, back_far, side_back_far)
            )
        side_back_far.append(lax.ppermute(side_grad_far, "ctx", side_pairs))
        back_far.append(from_peers(back))
    mixed, query_grad, own, far, near_grad_own, near_grad_far, side_grad_own, sums = joint

    near_back_far = lax.ppermute(near_grad_far, "ctx", near_pairs)
    near_back_own = lax.ppermute(near_grad_own, "ctx", near_pairs)
    side_back_own = lax.ppermute(side_grad_own, "ctx", side_pairs)

    def shifted(array, step):
        return lax.ppermute(array, "ctx", [(i, i ^ step) for i in range(ctx_count)])

    def rounds(steps, sums):
        for one, two in zip(steps[::2], [*steps[1::2], None]):
            if two is None:
                sums = sums + shifted(sums, one)
                continue
            across = [shifted(sums, step) for step in (one, two, one ^ two)]
            sums = (sums + across[0]) + (across[1] + across[2])
        return sums

    bits = [1 << n for n in range(ctx_count.bit_length() - 1)]
    side_back_far, back_far = tie((side_back_far, back_far))
    sums = rounds(bits[:2], sums)
    far_grad = pl.pallas_call(
        far_sum_kernel,
        in_specs=[in_vmem] * (2 + parts),
        out_specs=in_vmem,
        out_shape=jax.ShapeDtypeStruct((2, far_rows, width), bf16),
        compiler_params=small,
        cost_estimate=cheap,
        name="far_sum",
    )(far, near_back_far, *side_back_far)
    grad_far = from_peers(far_grad)

    def to_all(steps, sums):
        slabs = [rounds(steps, sums)]
        for step in (1 << n for n in range(groups.bit_length() - 1)):
            pairs = [(i, i ^ step) for i in range(groups)]
            slabs = slabs + [lax.ppermute(slab, "head", pairs) for slab in slabs]
        return slabs

    rest = bits[2:]
    sums, _ = tie((sums, far_grad))
    slabs = lax.cond(
        noise_level[0] >= 0,
        functools.partial(to_all, rest),
        functools.partial(to_all, rest[::-1]),
        sums,
    )
    slabs, grad_far, side_back_own = tie((slabs, grad_far, side_back_own))
    arrived = [slab for slabs in back_far for slab in slabs] + grad_far
    padded = -(-slots // 16) * 16
    noise_row = jnp.pad(noise_level, (0, padded - slots), constant_values=-1) if by_span else noise_level
    noise_row = jnp.tile(noise_row, 3 if by_span else 1).reshape(1, -1)
    operands = (noise_row, own, near_back_own, side_back_own, *slabs, *arrived)
    return tuple(
        pl.pallas_call(
            functools.partial(finish_kernel, groups=groups, parts=parts, by_span=by_span),
            grid_spec=pltpu.PrefetchScalarGridSpec(
                num_scalar_prefetch=1,
                in_specs=[in_vmem] * len(operands) + [anywhere] * 2,
                out_specs=[anywhere] * 5,
                scratch_shapes=[
                    pltpu.VMEM((2, rows, width), bf16),
                    pltpu.VMEM((3 * padded, width), bf16),
                    pltpu.VMEM((level_count, full_width), f32),
                    pltpu.SemaphoreType.DMA((2 * len(arrived) + 2 + groups,)),
                ],
            ),
            out_shape=[jax.ShapeDtypeStruct((rows, full_width), bf16)] * 4
            + [jax.ShapeDtypeStruct((level_count, full_width), f32)],
            input_output_aliases={1 + len(operands): 0, 2 + len(operands): 1},
            compiler_params=small,
            cost_estimate=cheap,
            name="finish",
        )(place, *operands, mixed, query_grad)
    )


def solution(mesh):
    sharded = P(("ctx", "head"), None)
    return jax.shard_map(
        per_device,
        mesh=mesh,
        in_specs=(sharded,) * 4 + (P(),) * 4,
        out_specs=(sharded,) * 4 + (P(),),
        check_vma=False,
    )
```

```python
import functools
import math

import jax
import jax.numpy as jnp
from jax import lax
from jax.experimental import pallas as pl
from jax.experimental.pallas import tpu as pltpu
from jax.sharding import PartitionSpec as P

DH = 128
HIDDEN = -1e30
LOG2E = 1.4426950408889634


def other_ctx(c, near):
    odd = lax.rem(c, 2)
    return c + 1 - 2 * odd if near else c - 1 + 2 * odd


def prep_kernel(
    place_ref, span_ref, noise_ref, mask_ref, table_ref, bias_ref, gate_ref, slot_ref, *, sizes
):
    ctx_count, groups, rows, span_total, level_count, by_span = sizes
    c, h = lax.div(place_ref[0], groups), lax.rem(place_ref[0], groups)
    tokens = groups * rows
    total = ctx_count * tokens
    bf16, f32 = jnp.bfloat16, jnp.float32

    def block_of(ctx, k):
        return ctx * groups + lax.rem(h - k + groups, groups)

    def spans_of(ctx, k):
        at = jnp.clip(ctx, 0, ctx_count - 1)
        return span_ref[pl.ds(block_of(at, k), 1), :]

    def as_column(row):
        return jnp.broadcast_to(row.astype(f32), (rows, rows)).T[:, :1].astype(jnp.int32)

    across = lax.broadcasted_iota(jnp.int32, (1, rows), 1)
    down = lax.broadcasted_iota(jnp.int32, (rows, 1), 0)
    span_lane = lax.broadcasted_iota(jnp.int32, (rows, span_total), 1)
    span_down = lax.broadcasted_iota(jnp.int32, (span_total, rows), 0)
    level_lane = lax.broadcasted_iota(jnp.int32, (rows, level_count), 1)
    query_span = [spans_of(c, k) for k in range(groups)]
    query_pos = [block_of(c, k) * rows + across for k in range(groups)]
    mask_low = mask_ref[...].astype(bf16)
    allowed_q = [
        lax.dot_general(
            mask_low,
            (span_down == row).astype(bf16),
            (((0,), (0,)), ((), ())),
            preferred_element_type=f32,
        ).astype(bf16)
        for row in query_span
    ]
    noise = noise_ref[...].astype(f32)
    for i, ctx in enumerate((c, other_ctx(c, True), other_ctx(c, False))):
        for k in range(groups):
            key_span = as_column(spans_of(ctx, k))
            key_pos = block_of(ctx, k) * rows + down
            valid = (key_pos >= 0) & (key_pos < total)
            onehot = key_span == span_lane
            at = slice((i * groups + k) * rows, (i * groups + k + 1) * rows)
            for p in range(groups):
                allowed = jnp.dot(
                    onehot.astype(bf16), allowed_q[p], preferred_element_type=f32
                )
                visible = (
                    (allowed > 0.5)
                    & (key_span <= query_span[p])
                    & (query_pos[p] - key_pos < tokens)
                    & valid
                )
                bias_ref[at, p * rows : (p + 1) * rows] = jnp.where(visible, 0.0, HIDDEN)
            if i > 0:
                continue
            level = jnp.sum(jnp.where(onehot, noise, 0.0), axis=1, keepdims=True)
            level_onehot = (level.astype(jnp.int32) == level_lane).astype(f32)
            gate_ref[at, :] = jnp.dot(
                level_onehot,
                table_ref[...],
                precision=lax.Precision.HIGHEST,
                preferred_element_type=f32,
            )
            if by_span:
                slot_ref[:, at] = (span_down == query_span[k]).astype(bf16)
            else:
                slot_ref[:, at] = level_onehot.T.astype(bf16)


def attention_kernel(
    place_ref,
    qo_own_ref, kv_own_ref, qo_ref, kv_ref,
    near_own_ref, near_far_ref, side_own_ref, side_far_ref,
    gate_ref, bias_ref, slot_ref,
    *rest, rows, tokens, q_size, heads,
):
    (
        back_ref, side_grad_far_ref, mixed_ref, dq_ref, own_ref, far_ref,
        near_grad_ref, side_grad_own_ref, sums_ref,
    ) = rest[-9:]
    scale = 1.0 / math.sqrt(DH)
    bf16, f32 = jnp.bfloat16, jnp.float32
    tile = 32

    def dot(left, right, left_dim, right_dim):
        return lax.dot_general(
            left, right, (((left_dim,), (right_dim,)), ((), ())), preferred_element_type=f32
        )

    def load(j):
        at = slice(j * DH, (j + 1) * DH)
        keys, values = [], []
        for ref in (
            kv_own_ref, kv_ref, near_own_ref, near_far_ref, side_own_ref, side_far_ref
        ):
            keys.append(ref[0, :, at])
            values.append(ref[1, :, at])
        keys, values = jnp.concatenate(keys, axis=0), jnp.concatenate(values, axis=0)
        queries = jnp.concatenate([qo_own_ref[0, :, at], qo_ref[0, :, at]], axis=0)
        cotangent = jnp.concatenate([qo_own_ref[1, :, at], qo_ref[1, :, at]], axis=0)
        blocks = []
        for start in range(0, tokens, q_size):
            span = slice(start, start + q_size)
            q, o = queries[span], cotangent[span].astype(f32)
            gate = gate_ref[span, at]
            g = (gate * o).astype(bf16)
            blocks.append((q, o, gate, g, dot(keys, q, 1, 1), dot(values, g, 1, 1)))
        return keys, values, blocks

    def work(j, keys, values, blocks):
        at = slice(j * DH, (j + 1) * DH)
        keys_t, values_t = keys.T, values.T
        key_grad = value_grad = sums = None
        for number, (q, o, gate, g, scores, prob_grad) in enumerate(blocks):
            start = number * q_size
            span = slice(start, start + q_size)
            count = scores.shape[0]
            tiles = [slice(r, r + tile) for r in range(0, count, tile)]
            raised, top = [], None
            for t in tiles:
                part = scores[t] * (scale * LOG2E) + bias_ref[t, span]
                raised.append(part)
                high = jnp.max(part.reshape(tile // 8, 8, q_size), axis=0)
                top = high if top is None else jnp.maximum(top, high)
            top = jnp.max(top, axis=0, keepdims=True)
            total = None
            for i in range(len(tiles)):
                raised[i] = jnp.exp2(raised[i] - top)
                part = jnp.sum(raised[i].reshape(tile // 8, 8, q_size), axis=0)
                total = part if total is None else total + part
            inverse = 1.0 / jnp.sum(total, axis=0, keepdims=True)
            low = jnp.concatenate([(part * inverse).astype(bf16) for part in raised], axis=0)
            attended_t = dot(values_t, low, 1, 0).astype(bf16)
            row_dot = jnp.sum(g.T.astype(f32) * attended_t.astype(f32), axis=0, keepdims=True)
            attended = attended_t.T.astype(f32)
            score_grad = jnp.concatenate(
                [
                    (part * ((prob_grad[t] - row_dot) * inverse)).astype(bf16)
                    for part, t in zip(raised, tiles)
                ],
                axis=0,
            )
            query_grad = (dot(keys_t, score_grad, 1, 0) * scale).astype(bf16).T
            mixed = (gate * attended).astype(bf16)
            if start == 0:
                mixed_ref[:, at] = mixed[:rows]
                dq_ref[:, at] = query_grad[:rows]
                back_ref[0, : q_size - rows, at] = mixed[rows:]
                back_ref[1, : q_size - rows, at] = query_grad[rows:]
            else:
                back_ref[0, start - rows : start - rows + q_size, at] = mixed
                back_ref[1, start - rows : start - rows + q_size, at] = query_grad
            dk, dv = dot(score_grad, q, 1, 0), dot(low, g, 1, 0)
            product = o * attended
            high = product.astype(bf16)
            rest = (product - high.astype(f32)).astype(bf16)
            both = dot(slot_ref[:, span], jnp.concatenate([high, rest], axis=1), 1, 0)
            part = both[:, :DH] + both[:, DH:]
            key_grad = dk if key_grad is None else key_grad + dk
            value_grad = dv if value_grad is None else value_grad + dv
            sums = part if sums is None else sums + part
        sums_ref[:, at] = sums.astype(bf16)
        for i, grad in ((0, key_grad * scale), (1, value_grad)):
            own_ref[i, :, at] = grad[:rows]
            far_ref[i, :, at] = grad[rows:tokens]
            low = grad[tokens:].astype(bf16)
            near_grad_ref[i, :, at] = low[:tokens]
            side_grad_own_ref[i, :, at] = low[tokens : tokens + rows]
            side_grad_far_ref[i, :, at] = low[tokens + rows :]

    ready = load(0)
    for j in range(heads):
        following = load(j + 1) if j + 1 < heads else None
        work(j, *ready)
        ready = following


def pack_kernel(place_ref, first_ref, second_ref, own_ref, *rest, groups):
    *far_refs, sems = rest
    rows, width = own_ref.shape[1:]
    copies = []

    def copy(ref, start, to):
        cols = pl.ds(pl.multiple_of(start, DH), to.shape[1])
        copies.append(pltpu.make_async_copy(ref.at[:, cols], to, sems.at[len(copies)]))
        copies[-1].start()

    for k in (*range(1, groups), 0):
        start = lax.rem(place_ref[0] + k, groups) * width
        for i, ref in enumerate((first_ref, second_ref)):
            if k == 0:
                copy(ref, start, own_ref.at[i])
                continue
            for p, far_ref in enumerate(far_refs):
                at = pl.ds((k - 1) * rows, rows)
                copy(ref, start + p * far_ref.shape[2], far_ref.at[i, at])
    for one in copies:
        one.wait()


def far_sum_kernel(part_ref, near_ref, *refs):
    *side_refs, out_ref = refs
    far = slice(near_ref.shape[1] - part_ref.shape[1], None)
    for p, ref in enumerate(side_refs):
        width = ref.shape[2]
        cols = slice(p * width, (p + 1) * width)
        total = part_ref[:, :, cols] + near_ref[:, far, cols].astype(jnp.float32)
        out_ref[:, :, cols] = (total + ref[...].astype(jnp.float32)).astype(out_ref.dtype)


def finish_kernel(place_ref, noise_ref, part_ref, near_ref, side_ref, *refs, groups, parts, by_span):
    count = (groups - 1) * (parts + 1)
    slot_refs, refs = refs[:groups], refs[groups:]
    slabs, outs = refs[:count], refs[count + 2 : count + 7]
    total_ref, gate_ref, sems = refs[count + 7 :]
    width = part_ref.shape[2]
    copies = []

    def copy(slab, first, second, start):
        cols = pl.ds(pl.multiple_of(start, DH), slab.shape[2])
        for i, ref in enumerate((first, second)):
            copies.append(pltpu.make_async_copy(slab.at[i], ref.at[:, cols], sems.at[len(copies)]))
            copies[-1].start()

    for k in range(1, groups):
        start = lax.rem(place_ref[0] + k, groups) * width
        for p in range(parts):
            slab = slabs[p * (groups - 1) + k - 1]
            copy(slab, outs[0], outs[1], start + p * slab.shape[2])
        copy(slabs[parts * (groups - 1) + k - 1], outs[2], outs[3], start)
    near = near_ref[:, : part_ref.shape[1]].astype(jnp.float32)
    total = part_ref[...] + near + side_ref[...].astype(jnp.float32)
    total_ref[...] = total.astype(total_ref.dtype)
    copy(total_ref, outs[2], outs[3], lax.rem(place_ref[0], groups) * width)
    levels = lax.broadcasted_iota(jnp.int32, (gate_ref.shape[0], noise_ref.shape[1]), 0)
    onehot = (levels == noise_ref[...]).astype(jnp.bfloat16)
    for j, ref in enumerate(slot_refs):
        sums = ref[...]
        if by_span:
            sums = jnp.dot(onehot, sums, preferred_element_type=jnp.float32)
        else:
            sums = sums.astype(jnp.float32)
        start = lax.bitwise_xor(lax.rem(place_ref[0], groups), j) * width
        cols = pl.ds(pl.multiple_of(start, DH), width)
        gate_ref[:, cols] = sums
        copies.append(
            pltpu.make_async_copy(gate_ref.at[:, cols], outs[4].at[:, cols], sems.at[len(copies)])
        )
        copies[-1].start()
    for one in copies:
        one.wait()


def per_device(
    queries, key_rows, value_rows, out_cotangent, gate_table, span_ids, noise_level, block_mask
):
    groups = lax.axis_size("head")
    ctx_count = lax.axis_size("ctx")
    rows, full_width = queries.shape
    width = full_width // groups
    heads = width // DH
    tokens = rows * groups
    far_rows = tokens - rows
    parts = 2 if heads % 2 == 0 else 1
    part_width = width // parts
    part_heads = heads // parts
    span_total = noise_level.shape[0]
    level_count = gate_table.shape[0]
    by_span = span_total <= level_count // 2
    slots = span_total if by_span else level_count
    c = lax.axis_index("ctx")
    h = lax.axis_index("head")
    place = (c * groups + h).astype(jnp.int32).reshape(1)
    head_at = lambda place: lax.rem(place[0], groups)
    bf16, f32 = jnp.bfloat16, jnp.float32
    tie = lax.optimization_barrier

    near_pairs = [(i, i ^ 1) for i in range(ctx_count)]
    side_of = [i - 1 + 2 * (i % 2) for i in range(ctx_count)]
    side_pairs = [(i, j if 0 <= j < ctx_count else i) for i, j in enumerate(side_of)]

    whole = lambda shape: pl.BlockSpec(shape, lambda i, place: (0,) * len(shape))
    limit = (26 if tokens <= 256 else 56) * 1024 * 1024
    params = pltpu.CompilerParams(vmem_limit_bytes=limit)
    alone = pltpu.CompilerParams(vmem_limit_bytes=56 * 1024 * 1024)
    cheap = pl.CostEstimate(flops=1, bytes_accessed=1, transcendentals=0)
    in_vmem = pl.BlockSpec(memory_space=pltpu.VMEM)
    anywhere = pl.BlockSpec(memory_space=pl.ANY)
    small = pltpu.CompilerParams(vmem_limit_bytes=(12 if tokens <= 256 else 36) * 1024 * 1024)

    def pack(first, second, params):
        far_shape = (2, far_rows, part_width)
        return pl.pallas_call(
            functools.partial(pack_kernel, groups=groups),
            grid_spec=pltpu.PrefetchScalarGridSpec(
                num_scalar_prefetch=1,
                in_specs=[anywhere] * 2,
                out_specs=[in_vmem] * (1 + parts),
                scratch_shapes=[pltpu.SemaphoreType.DMA((2 + 2 * (groups - 1) * parts,))],
            ),
            out_shape=[jax.ShapeDtypeStruct((2, rows, width), bf16)]
            + [jax.ShapeDtypeStruct(far_shape, bf16)] * parts,
            compiler_params=params,
            cost_estimate=cheap,
            name="pack",
        )(place, first, second)

    def to_peers(slab):
        arrived = []
        for k in range(1, groups):
            part = slab if groups == 2 else slab[:, (k - 1) * rows : k * rows]
            pairs = [(i, (i + k) % groups) for i in range(groups)]
            arrived.append(lax.ppermute(part, "head", pairs))
        return arrived[0] if groups == 2 else jnp.concatenate(arrived, axis=1)

    def from_peers(slab):
        arrived = []
        for k in range(1, groups):
            part = slab if groups == 2 else slab[:, (k - 1) * rows : k * rows]
            pairs = [(i, (i - k) % groups) for i in range(groups)]
            arrived.append(lax.ppermute(part, "head", pairs))
        return arrived

    kv_own, *kv_sent = pack(key_rows, value_rows, alone)
    qo_own, *qo_sent = pack(queries, out_cotangent, small)
    side_own = lax.ppermute(kv_own, "ctx", side_pairs)
    near_own = lax.ppermute(kv_own, "ctx", near_pairs)
    kv_far = [to_peers(slab) for slab in kv_sent]
    side_far = [lax.ppermute(slab, "ctx", side_pairs) for slab in kv_far]
    near_far = [lax.ppermute(slab, "ctx", near_pairs) for slab in kv_far]
    qo_far = [to_peers(tie((slab, far))[0]) for slab, far in zip(qo_sent, kv_far)]

    sizes = (ctx_count, groups, rows, span_total, level_count, by_span)
    whole = lambda shape: pl.BlockSpec(shape, lambda i, place: (0,) * len(shape))
    bias, gate, slot = pl.pallas_call(
        functools.partial(prep_kernel, sizes=sizes),
        grid_spec=pltpu.PrefetchScalarGridSpec(
            num_scalar_prefetch=1,
            grid=(1,),
            in_specs=[
                whole((ctx_count * groups, rows)),
                whole((1, span_total)),
                whole((span_total, span_total)),
                pl.BlockSpec((level_count, width), lambda i, place: (0, head_at(place))),
            ],
            out_specs=[
                whole((3 * tokens, tokens)),
                whole((tokens, width)),
                whole((slots, tokens)),
            ],
        ),
        out_shape=[
            jax.ShapeDtypeStruct((3 * tokens, tokens), f32),
            jax.ShapeDtypeStruct((tokens, width), f32),
            jax.ShapeDtypeStruct((slots, tokens), bf16),
        ],
        compiler_params=small,
        cost_estimate=cheap,
        name="prep",
    )(
        place,
        span_ids.reshape(ctx_count * groups, rows),
        noise_level.reshape(1, span_total),
        block_mask,
        gate_table,
    )

    batch = next(n for n in (3, 2, 1) if part_heads % n == 0) if tokens <= 256 else 1
    steps = part_heads // batch
    block = batch * DH
    q_size = min(256, tokens)

    def attention(p, joint):
        pair = lambda count: pl.BlockSpec((2, count, block), lambda i, place: (0, 0, i))
        at_part = lambda count: pl.BlockSpec(
            (2, count, block), lambda i, place: (0, 0, p * steps + i)
        )
        at_head = pl.BlockSpec(
            (rows, block), lambda i, place: (0, (head_at(place) * parts + p) * steps + i)
        )
        column = lambda count: pl.BlockSpec((count, block), lambda i, place: (0, p * steps + i))
        struct = jax.ShapeDtypeStruct
        inputs = [
            qo_own, kv_own, qo_far[p], kv_far[p],
            near_own, near_far[p], side_own, side_far[p],
            gate, bias, slot,
        ]
        return pl.pallas_call(
            functools.partial(
                attention_kernel, rows=rows, tokens=tokens, q_size=q_size, heads=batch
            ),
            grid_spec=pltpu.PrefetchScalarGridSpec(
                num_scalar_prefetch=1,
                grid=(steps,),
                in_specs=[
                    at_part(rows), at_part(rows), pair(far_rows), pair(far_rows),
                    at_part(rows), pair(far_rows), at_part(rows), pair(far_rows),
                    column(tokens), whole((3 * tokens, tokens)), whole((slots, tokens)),
                ]
                + [pl.BlockSpec(memory_space=pl.ANY)] * len(joint),
                out_specs=[
                    pair(far_rows), pair(far_rows),
                    at_head, at_head, at_part(rows), at_part(far_rows),
                    at_part(tokens), at_part(rows), column(slots),
                ],
            ),
            out_shape=[
                struct((2, far_rows, part_width), bf16),
                struct((2, far_rows, part_width), bf16),
                struct((rows, full_width), bf16),
                struct((rows, full_width), bf16),
                struct((2, rows, width), f32),
                struct((2, far_rows, width), f32),
                struct((2, tokens, width), bf16),
                struct((2, rows, width), bf16),
                struct((slots, width), bf16),
            ],
            input_output_aliases={1 + len(inputs) + i: 2 + i for i in range(len(joint))},
            compiler_params=params,
            cost_estimate=cheap,
            name="attention",
        )(place, *inputs, *joint)

    joint, back_far, side_back_far = (), [], []
    for p in range(parts):
        back, side_grad_far, *joint = attention(p, joint)
        if p > 0:
            back, side_grad_far, joint, back_far, side_back_far = tie(
                (back, side_grad_far, joint, back_far, side_back_far)
            )
        side_back_far.append(lax.ppermute(side_grad_far, "ctx", side_pairs))
        back_far.append(from_peers(back))
    mixed, query_grad, own, far, near_grad, side_grad_own, sums = joint

    near_back = lax.ppermute(near_grad, "ctx", near_pairs)

    def shifted(array, step):
        return lax.ppermute(array, "ctx", [(i, i ^ step) for i in range(ctx_count)])

    def rounds(steps, sums):
        for one, two in zip(steps[::2], [*steps[1::2], None]):
            if two is None:
                sums = sums + shifted(sums, one)
                continue
            across = [shifted(sums, step) for step in (one, two, one ^ two)]
            sums = (sums + across[0]) + (across[1] + across[2])
        return sums

    bits = [1 << n for n in range(ctx_count.bit_length() - 1)]
    side_back_far, back_far = tie((side_back_far, back_far))
    side_grad_own, _ = tie((side_grad_own, side_back_far))
    side_back_own = lax.ppermute(side_grad_own, "ctx", side_pairs)
    sums = rounds(bits[:1], rounds(bits[2:], sums))
    side_back_far, sums = tie((side_back_far, sums))
    far_grad = pl.pallas_call(
        far_sum_kernel,
        in_specs=[in_vmem] * (2 + parts),
        out_specs=in_vmem,
        out_shape=jax.ShapeDtypeStruct((2, far_rows, width), bf16),
        compiler_params=small,
        cost_estimate=cheap,
        name="far_sum",
    )(far, near_back, *side_back_far)
    grad_far = from_peers(far_grad)

    def to_all(before, after, sums):
        slabs = [rounds(before, sums)]
        for step in (1 << n for n in range(groups.bit_length() - 1)):
            pairs = [(i, i ^ step) for i in range(groups)]
            slabs = slabs + [lax.ppermute(slab, "head", pairs) for slab in slabs]
        return [rounds(after, slab) for slab in slabs]

    sums, _ = tie((sums, far_grad))
    slabs = lax.cond(
        noise_level[0] >= 0,
        functools.partial(to_all, bits[1:2], []),
        functools.partial(to_all, [], bits[1:2]),
        sums,
    )
    slabs, grad_far, side_back_own = tie((slabs, grad_far, side_back_own))
    arrived = [slab for slabs in back_far for slab in slabs] + grad_far
    noise_row = noise_level.reshape(1, span_total)
    operands = (noise_row, own, near_back, side_back_own, *slabs, *arrived)
    return tuple(
        pl.pallas_call(
            functools.partial(finish_kernel, groups=groups, parts=parts, by_span=by_span),
            grid_spec=pltpu.PrefetchScalarGridSpec(
                num_scalar_prefetch=1,
                in_specs=[in_vmem] * len(operands) + [anywhere] * 2,
                out_specs=[anywhere] * 5,
                scratch_shapes=[
                    pltpu.VMEM((2, rows, width), bf16),
                    pltpu.VMEM((level_count, full_width), f32),
                    pltpu.SemaphoreType.DMA((2 * len(arrived) + 2 + groups,)),
                ],
            ),
            out_shape=[jax.ShapeDtypeStruct((rows, full_width), bf16)] * 4
            + [jax.ShapeDtypeStruct((level_count, full_width), f32)],
            input_output_aliases={1 + len(operands): 0, 2 + len(operands): 1},
            compiler_params=small,
            cost_estimate=cheap,
            name="finish",
        )(place, *operands, mixed, query_grad)
    )


def solution(mesh):
    sharded = P(("ctx", "head"), None)
    return jax.shard_map(
        per_device,
        mesh=mesh,
        in_specs=(sharded,) * 4 + (P(),) * 4,
        out_specs=(sharded,) * 4 + (P(),),
        check_vma=False,
    )
```

```python
import functools
import math

import jax
import jax.numpy as jnp
from jax import lax
from jax.experimental import pallas as pl
from jax.experimental.pallas import tpu as pltpu
from jax.sharding import PartitionSpec as P

DH = 128
HIDDEN = -1e30
LOG2E = 1.4426950408889634


def other_ctx(c, near):
    odd = lax.rem(c, 2)
    return c + 1 - 2 * odd if near else c - 1 + 2 * odd


def prep_kernel(
    place_ref, span_ref, noise_ref, mask_ref, table_ref, bias_ref, gate_ref, slot_ref, *, sizes
):
    ctx_count, groups, rows, span_total, level_count, by_span = sizes
    c, h = lax.div(place_ref[0], groups), lax.rem(place_ref[0], groups)
    tokens = groups * rows
    total = ctx_count * tokens
    bf16, f32 = jnp.bfloat16, jnp.float32

    def block_of(ctx, k):
        return ctx * groups + lax.rem(h - k + groups, groups)

    def spans_of(ctx, k):
        at = jnp.clip(ctx, 0, ctx_count - 1)
        return span_ref[pl.ds(block_of(at, k), 1), :]

    def as_column(row):
        return jnp.broadcast_to(row.astype(f32), (rows, rows)).T[:, :1].astype(jnp.int32)

    across = lax.broadcasted_iota(jnp.int32, (1, rows), 1)
    down = lax.broadcasted_iota(jnp.int32, (rows, 1), 0)
    span_lane = lax.broadcasted_iota(jnp.int32, (rows, span_total), 1)
    span_down = lax.broadcasted_iota(jnp.int32, (span_total, rows), 0)
    level_lane = lax.broadcasted_iota(jnp.int32, (rows, level_count), 1)
    query_span = [spans_of(c, k) for k in range(groups)]
    query_pos = [block_of(c, k) * rows + across for k in range(groups)]
    mask_low = mask_ref[...].astype(bf16)
    allowed_q = [
        lax.dot_general(
            mask_low,
            (span_down == row).astype(bf16),
            (((0,), (0,)), ((), ())),
            preferred_element_type=f32,
        ).astype(bf16)
        for row in query_span
    ]
    noise = noise_ref[...].astype(f32)
    for i, ctx in enumerate((c, other_ctx(c, True), other_ctx(c, False))):
        for k in range(groups):
            key_span = as_column(spans_of(ctx, k))
            key_pos = block_of(ctx, k) * rows + down
            valid = (key_pos >= 0) & (key_pos < total)
            onehot = key_span == span_lane
            at = slice((i * groups + k) * rows, (i * groups + k + 1) * rows)
            for p in range(groups):
                allowed = jnp.dot(
                    onehot.astype(bf16), allowed_q[p], preferred_element_type=f32
                )
                visible = (
                    (allowed > 0.5)
                    & (key_span <= query_span[p])
                    & (query_pos[p] - key_pos < tokens)
                    & valid
                )
                bias_ref[at, p * rows : (p + 1) * rows] = jnp.where(visible, 0.0, HIDDEN)
            if i > 0:
                continue
            level = jnp.sum(jnp.where(onehot, noise, 0.0), axis=1, keepdims=True)
            level_onehot = (level.astype(jnp.int32) == level_lane).astype(f32)
            gate_ref[at, :] = jnp.dot(
                level_onehot,
                table_ref[...],
                precision=lax.Precision.HIGHEST,
                preferred_element_type=f32,
            )
            if by_span:
                slot_ref[:, at] = (span_down == query_span[k]).astype(bf16)
            else:
                slot_ref[:, at] = level_onehot.T.astype(bf16)


def attention_kernel(
    place_ref,
    qo_own_ref, kv_own_ref, qo_ref, kv_ref,
    near_own_ref, near_far_ref, side_own_ref, side_far_ref,
    gate_ref, bias_ref, slot_ref,
    *rest, rows, tokens, q_size, heads, apart,
):
    back_ref, own_ref, far_ref, near_grad_ref, *side_grad_refs = rest[-8 - apart : -3]
    mixed_ref, dq_ref, sums_ref = rest[-3:]
    scale = 1.0 / math.sqrt(DH)
    bf16, f32 = jnp.bfloat16, jnp.float32
    tile = 32

    def dot(left, right, left_dim, right_dim):
        return lax.dot_general(
            left, right, (((left_dim,), (right_dim,)), ((), ())), preferred_element_type=f32
        )

    def load(j):
        at = slice(j * DH, (j + 1) * DH)
        keys, values = [], []
        for ref in (
            kv_own_ref, kv_ref, near_own_ref, near_far_ref, side_own_ref, side_far_ref
        ):
            keys.append(ref[0, :, at])
            values.append(ref[1, :, at])
        keys, values = jnp.concatenate(keys, axis=0), jnp.concatenate(values, axis=0)
        queries = jnp.concatenate([qo_own_ref[0, :, at], qo_ref[0, :, at]], axis=0)
        cotangent = jnp.concatenate([qo_own_ref[1, :, at], qo_ref[1, :, at]], axis=0)
        blocks = []
        for start in range(0, tokens, q_size):
            span = slice(start, start + q_size)
            q, o = queries[span], cotangent[span].astype(f32)
            gate = gate_ref[span, at]
            g = (gate * o).astype(bf16)
            blocks.append((q, o, gate, g, dot(keys, q, 1, 1), dot(values, g, 1, 1)))
        return keys, values, blocks

    def work(j, keys, values, blocks):
        at = slice(j * DH, (j + 1) * DH)
        keys_t, values_t = keys.T, values.T
        key_grad = value_grad = sums = None
        for number, (q, o, gate, g, scores, prob_grad) in enumerate(blocks):
            start = number * q_size
            span = slice(start, start + q_size)
            count = scores.shape[0]
            tiles = [slice(r, r + tile) for r in range(0, count, tile)]
            raised, top = [], None
            for t in tiles:
                part = scores[t] * (scale * LOG2E) + bias_ref[t, span]
                raised.append(part)
                high = jnp.max(part.reshape(tile // 8, 8, q_size), axis=0)
                top = high if top is None else jnp.maximum(top, high)
            top = jnp.max(top, axis=0, keepdims=True)
            total = None
            for i in range(len(tiles)):
                raised[i] = jnp.exp2(raised[i] - top)
                part = jnp.sum(raised[i].reshape(tile // 8, 8, q_size), axis=0)
                total = part if total is None else total + part
            inverse = 1.0 / jnp.sum(total, axis=0, keepdims=True)
            low = jnp.concatenate([(part * inverse).astype(bf16) for part in raised], axis=0)
            attended_t = dot(values_t, low, 1, 0).astype(bf16)
            row_dot = jnp.sum(g.T.astype(f32) * attended_t.astype(f32), axis=0, keepdims=True)
            attended = attended_t.T.astype(f32)
            score_grad = jnp.concatenate(
                [
                    (part * ((prob_grad[t] - row_dot) * inverse)).astype(bf16)
                    for part, t in zip(raised, tiles)
                ],
                axis=0,
            )
            query_grad = (dot(keys_t, score_grad, 1, 0) * scale).astype(bf16).T
            mixed = (gate * attended).astype(bf16)
            if start == 0:
                mixed_ref[:, at] = mixed[:rows]
                dq_ref[:, at] = query_grad[:rows]
                back_ref[0, : q_size - rows, at] = mixed[rows:]
                back_ref[1, : q_size - rows, at] = query_grad[rows:]
            else:
                back_ref[0, start - rows : start - rows + q_size, at] = mixed
                back_ref[1, start - rows : start - rows + q_size, at] = query_grad
            dk, dv = dot(score_grad, q, 1, 0), dot(low, g, 1, 0)
            product = o * attended
            high = product.astype(bf16)
            rest = (product - high.astype(f32)).astype(bf16)
            both = dot(slot_ref[:, span], jnp.concatenate([high, rest], axis=1), 1, 0)
            part = both[:, :DH] + both[:, DH:]
            key_grad = dk if key_grad is None else key_grad + dk
            value_grad = dv if value_grad is None else value_grad + dv
            sums = part if sums is None else sums + part
        sums_ref[:, at] = sums.astype(bf16)
        for i, grad in ((0, key_grad * scale), (1, value_grad)):
            own_ref[i, :, at] = grad[:rows]
            far_ref[i, :, at] = grad[rows:tokens]
            low = grad[tokens:].astype(bf16)
            near_grad_ref[i, :, at] = low[:tokens]
            if apart:
                side_grad_refs[0][i, :, at] = low[tokens : tokens + rows]
                side_grad_refs[1][i, :, at] = low[tokens + rows :]
            else:
                side_grad_refs[0][i, :, at] = low[tokens:]

    ready = load(0)
    for j in range(heads):
        following = load(j + 1) if j + 1 < heads else None
        work(j, *ready)
        ready = following


def pack_kernel(place_ref, first_ref, second_ref, own_ref, *rest, groups):
    *far_refs, sems = rest
    rows, width = own_ref.shape[1:]
    copies = []

    def copy(ref, start, to):
        cols = pl.ds(pl.multiple_of(start, DH), to.shape[1])
        copies.append(pltpu.make_async_copy(ref.at[:, cols], to, sems.at[len(copies)]))
        copies[-1].start()

    for k in (*range(1, groups), 0):
        start = lax.rem(place_ref[0] + k, groups) * width
        for i, ref in enumerate((first_ref, second_ref)):
            if k == 0:
                copy(ref, start, own_ref.at[i])
                continue
            for p, far_ref in enumerate(far_refs):
                at = pl.ds((k - 1) * rows, rows)
                copy(ref, start + p * far_ref.shape[2], far_ref.at[i, at])
    for one in copies:
        one.wait()


def far_sum_kernel(part_ref, near_ref, side_ref, out_ref):
    far = slice(near_ref.shape[1] - part_ref.shape[1], None)
    total = part_ref[...] + near_ref[:, far].astype(jnp.float32)
    side = side_ref[:, side_ref.shape[1] - part_ref.shape[1] :].astype(jnp.float32)
    out_ref[...] = (total + side).astype(out_ref.dtype)


def finish_kernel(place_ref, noise_ref, *refs, groups, parts):
    part_refs, near_refs, side_refs = (refs[n * parts : (n + 1) * parts] for n in range(3))
    refs = refs[3 * parts :]
    slot_refs, refs = refs[:groups], refs[groups:]
    count = 2 * (groups - 1) * parts
    slabs, outs = refs[:count], refs[count + 2 : count + 7]
    total_ref, gate_ref, sems = refs[count + 7 :]
    part_width = part_refs[0].shape[2]
    width = part_width * parts
    copies = []

    def send(source, to):
        copies.append(pltpu.make_async_copy(source, to, sems.at[len(copies)]))
        copies[-1].start()

    def place_slab(slab, first, second, k, p):
        start = lax.rem(place_ref[0] + k, groups) * width + p * part_width
        cols = pl.ds(pl.multiple_of(start, DH), part_width)
        for i, ref in enumerate((first, second)):
            send(slab.at[i], ref.at[:, cols])

    slabs = iter(slabs)
    for first, second in (outs[:2], outs[2:4]):
        for p in range(parts):
            for k in range(1, groups):
                place_slab(next(slabs), first, second, k, p)
    for p in range(parts):
        near, side = (
            ref[p][:, : total_ref.shape[2]].astype(jnp.float32) for ref in (near_refs, side_refs)
        )
        total = part_refs[p][...] + near + side
        total_ref[p] = total.astype(total_ref.dtype)
        place_slab(total_ref.at[p], outs[2], outs[3], 0, p)
    by_span = noise_ref.shape[1] == slot_refs[0].shape[0]
    levels = lax.broadcasted_iota(jnp.int32, (gate_ref.shape[0], noise_ref.shape[1]), 0)
    onehot = (levels == noise_ref[...]).astype(jnp.bfloat16)
    for j, ref in enumerate(slot_refs):
        if by_span:
            sums = jnp.dot(onehot, ref[...], preferred_element_type=jnp.float32)
        else:
            sums = ref[...].astype(jnp.float32)
        start = lax.bitwise_xor(lax.rem(place_ref[0], groups), j) * width
        cols = pl.ds(pl.multiple_of(start, DH), width)
        gate_ref[:, cols] = sums
        send(gate_ref.at[:, cols], outs[4].at[:, cols])
    for one in copies:
        one.wait()


def per_device(
    queries, key_rows, value_rows, out_cotangent, gate_table, span_ids, noise_level, block_mask
):
    groups = lax.axis_size("head")
    ctx_count = lax.axis_size("ctx")
    rows, full_width = queries.shape
    width = full_width // groups
    heads = width // DH
    tokens = rows * groups
    far_rows = tokens - rows
    parts = 2 if heads % 2 == 0 else 1
    part_width = width // parts
    part_heads = heads // parts
    span_total = noise_level.shape[0]
    level_count = gate_table.shape[0]
    by_span = span_total <= level_count // 2
    slots = span_total if by_span else level_count
    c = lax.axis_index("ctx")
    h = lax.axis_index("head")
    place = (c * groups + h).astype(jnp.int32).reshape(1)
    head_at = lambda place: lax.rem(place[0], groups)
    bf16, f32 = jnp.bfloat16, jnp.float32
    tie = lax.optimization_barrier

    near_pairs = [(i, i ^ 1) for i in range(ctx_count)]
    side_of = [i - 1 + 2 * (i % 2) for i in range(ctx_count)]
    side_pairs = [(i, j if 0 <= j < ctx_count else i) for i, j in enumerate(side_of)]

    whole = lambda shape: pl.BlockSpec(shape, lambda i, place: (0,) * len(shape))
    limit = (26 if tokens <= 256 else 56) * 1024 * 1024
    params = pltpu.CompilerParams(vmem_limit_bytes=limit)
    alone = pltpu.CompilerParams(vmem_limit_bytes=56 * 1024 * 1024)
    cheap = pl.CostEstimate(flops=1, bytes_accessed=1, transcendentals=0)
    in_vmem = pl.BlockSpec(memory_space=pltpu.VMEM)
    anywhere = pl.BlockSpec(memory_space=pl.ANY)
    small = pltpu.CompilerParams(vmem_limit_bytes=(12 if tokens <= 256 else 36) * 1024 * 1024)

    def pack(first, second, params):
        far_shape = (2, far_rows, part_width)
        return pl.pallas_call(
            functools.partial(pack_kernel, groups=groups),
            grid_spec=pltpu.PrefetchScalarGridSpec(
                num_scalar_prefetch=1,
                in_specs=[anywhere] * 2,
                out_specs=[in_vmem] * (1 + parts),
                scratch_shapes=[pltpu.SemaphoreType.DMA((2 + 2 * (groups - 1) * parts,))],
            ),
            out_shape=[jax.ShapeDtypeStruct((2, rows, width), bf16)]
            + [jax.ShapeDtypeStruct(far_shape, bf16)] * parts,
            compiler_params=params,
            cost_estimate=cheap,
            name="pack",
        )(place, first, second)

    def to_peers(slab):
        arrived = []
        for k in range(1, groups):
            part = slab if groups == 2 else slab[:, (k - 1) * rows : k * rows]
            pairs = [(i, (i + k) % groups) for i in range(groups)]
            arrived.append(lax.ppermute(part, "head", pairs))
        return arrived[0] if groups == 2 else jnp.concatenate(arrived, axis=1)

    def from_peers(slab):
        arrived = []
        for k in range(1, groups):
            part = slab if groups == 2 else slab[:, (k - 1) * rows : k * rows]
            pairs = [(i, (i - k) % groups) for i in range(groups)]
            arrived.append(lax.ppermute(part, "head", pairs))
        return arrived

    kv_own, *kv_sent = pack(key_rows, value_rows, alone)
    qo_own, *qo_sent = pack(queries, out_cotangent, small)
    side_own = lax.ppermute(kv_own, "ctx", side_pairs)
    near_own = lax.ppermute(kv_own, "ctx", near_pairs)
    kv_far = [to_peers(slab) for slab in kv_sent]
    side_far = [lax.ppermute(slab, "ctx", side_pairs) for slab in kv_far]
    near_far = [lax.ppermute(slab, "ctx", near_pairs) for slab in kv_far]
    qo_far = [to_peers(tie((slab, far))[0]) for slab, far in zip(qo_sent, kv_far)]

    sizes = (ctx_count, groups, rows, span_total, level_count, by_span)
    whole = lambda shape: pl.BlockSpec(shape, lambda i, place: (0,) * len(shape))
    bias, gate, slot = pl.pallas_call(
        functools.partial(prep_kernel, sizes=sizes),
        grid_spec=pltpu.PrefetchScalarGridSpec(
            num_scalar_prefetch=1,
            grid=(1,),
            in_specs=[
                whole((ctx_count * groups, rows)),
                whole((1, span_total)),
                whole((span_total, span_total)),
                pl.BlockSpec((level_count, width), lambda i, place: (0, head_at(place))),
            ],
            out_specs=[
                whole((3 * tokens, tokens)),
                whole((tokens, width)),
                whole((slots, tokens)),
            ],
        ),
        out_shape=[
            jax.ShapeDtypeStruct((3 * tokens, tokens), f32),
            jax.ShapeDtypeStruct((tokens, width), f32),
            jax.ShapeDtypeStruct((slots, tokens), bf16),
        ],
        compiler_params=small,
        cost_estimate=cheap,
        name="prep",
    )(
        place,
        span_ids.reshape(ctx_count * groups, rows),
        noise_level.reshape(1, span_total),
        block_mask,
        gate_table,
    )

    batch = next(n for n in (3, 2, 1) if part_heads % n == 0) if tokens <= 256 else 1
    steps = part_heads // batch
    block = batch * DH
    q_size = min(256, tokens)

    def attention(p, joint):
        pair = lambda count: pl.BlockSpec((2, count, block), lambda i, place: (0, 0, i))
        at_part = lambda count: pl.BlockSpec(
            (2, count, block), lambda i, place: (0, 0, p * steps + i)
        )
        at_head = pl.BlockSpec(
            (rows, block), lambda i, place: (0, (head_at(place) * parts + p) * steps + i)
        )
        column = lambda count: pl.BlockSpec((count, block), lambda i, place: (0, p * steps + i))
        struct = jax.ShapeDtypeStruct
        side_counts = (rows, far_rows) if p + 1 == parts else (tokens,)
        inputs = [
            qo_own, kv_own, qo_far[p], kv_far[p],
            near_own, near_far[p], side_own, side_far[p],
            gate, bias, slot,
        ]
        return pl.pallas_call(
            functools.partial(
                attention_kernel,
                rows=rows, tokens=tokens, q_size=q_size, heads=batch, apart=p + 1 == parts,
            ),
            grid_spec=pltpu.PrefetchScalarGridSpec(
                num_scalar_prefetch=1,
                grid=(steps,),
                in_specs=[
                    at_part(rows), at_part(rows), pair(far_rows), pair(far_rows),
                    at_part(rows), pair(far_rows), at_part(rows), pair(far_rows),
                    column(tokens), whole((3 * tokens, tokens)), whole((slots, tokens)),
                ]
                + [pl.BlockSpec(memory_space=pl.ANY)] * len(joint),
                out_specs=[
                    pair(far_rows), pair(rows), pair(far_rows), pair(tokens),
                    *[pair(count) for count in side_counts],
                    at_head, at_head, column(slots),
                ],
            ),
            out_shape=[
                struct((2, far_rows, part_width), bf16),
                struct((2, rows, part_width), f32),
                struct((2, far_rows, part_width), f32),
                struct((2, tokens, part_width), bf16),
                *[struct((2, count, part_width), bf16) for count in side_counts],
                struct((rows, full_width), bf16),
                struct((rows, full_width), bf16),
                struct((slots, width), bf16),
            ],
            input_output_aliases={1 + len(inputs) + i: 4 + len(side_counts) + i for i in range(len(joint))},
            compiler_params=params,
            cost_estimate=cheap,
            name="attention",
        )(place, *inputs, *joint)

    def summed(p):
        far_grad = pl.pallas_call(
            far_sum_kernel,
            in_specs=[in_vmem] * 3,
            out_specs=in_vmem,
            out_shape=jax.ShapeDtypeStruct((2, far_rows, part_width), bf16),
            compiler_params=small,
            cost_estimate=cheap,
            name="far_sum",
        )(far[p], near_back[p], side_back_far[p])
        far_sent.append(far_grad)
        grad_far.append(from_peers(far_grad))

    joint, own, far = (), [], []
    back_far, side_back_far, near_back, side_back_own, far_sent, grad_far = [], [], [], [], [], []
    for p in range(parts):
        back, own_part, far_part, near_grad, *rest = attention(p, joint)
        side_grads, joint = rest[:-3], rest[-3:]
        if p + 1 < parts:
            side_grads, *_ = tie((side_grads, side_far[p + 1], near_far[p + 1], qo_far[p + 1]))
        if p > 0:
            side_grads, side_back_far, back_far = tie(
                (side_grads, side_back_far, back_far)
            )
            summed(p - 1)
            *side_grads, _ = tie((*side_grads, far_sent[-1]))
        own.append(own_part)
        far.append(far_part)
        side_back_far.append(lax.ppermute(side_grads[-1], "ctx", side_pairs))
        near_back.append(lax.ppermute(near_grad, "ctx", near_pairs))
        back_far.append(from_peers(back))
        if p + 1 < parts:
            side_back_own.append(side_back_far[p])
            continue
        side_grad_own, _ = tie((side_grads[0], side_back_far[p]))
        side_back_own.append(lax.ppermute(side_grad_own, "ctx", side_pairs))
    mixed, query_grad, sums = joint

    def shifted(array, step):
        return lax.ppermute(array, "ctx", [(i, i ^ step) for i in range(ctx_count)])

    def rounds(steps, sums):
        for one, two in zip(steps[::2], [*steps[1::2], None]):
            if two is None:
                sums = sums + shifted(sums, one)
                continue
            across = [shifted(sums, step) for step in (one, two, one ^ two)]
            sums = (sums + across[0]) + (across[1] + across[2])
        return sums

    bits = [1 << n for n in range(ctx_count.bit_length() - 1)]
    sums = rounds(bits[:1], rounds(bits[2:], sums))
    side_back_far, sums, back_far, grad_far = tie((side_back_far, sums, back_far, grad_far))
    summed(parts - 1)

    def to_all(before, after, sums):
        slabs = [rounds(before, sums)]
        for step in (1 << n for n in range(groups.bit_length() - 1)):
            pairs = [(i, i ^ step) for i in range(groups)]
            slabs = slabs + [lax.ppermute(slab, "head", pairs) for slab in slabs]
        return [rounds(after, slab) for slab in slabs]

    sums, _ = tie((sums, far_sent[-1]))
    slabs = lax.cond(
        noise_level[0] >= 0,
        functools.partial(to_all, bits[1:2], []),
        functools.partial(to_all, [], bits[1:2]),
        sums,
    )
    slabs, grad_far, side_back_own[-1] = tie((slabs, grad_far, side_back_own[-1]))
    arrived = [slab for part in back_far + grad_far for slab in part]
    noise_row = noise_level.reshape(1, span_total)
    operands = (noise_row, *own, *near_back, *side_back_own, *slabs, *arrived)
    return tuple(
        pl.pallas_call(
            functools.partial(finish_kernel, groups=groups, parts=parts),
            grid_spec=pltpu.PrefetchScalarGridSpec(
                num_scalar_prefetch=1,
                in_specs=[in_vmem] * len(operands) + [anywhere] * 2,
                out_specs=[anywhere] * 5,
                scratch_shapes=[
                    pltpu.VMEM((parts, 2, rows, part_width), bf16),
                    pltpu.VMEM((level_count, full_width), f32),
                    pltpu.SemaphoreType.DMA((2 * len(arrived) + 2 * parts + groups,)),
                ],
            ),
            out_shape=[jax.ShapeDtypeStruct((rows, full_width), bf16)] * 4
            + [jax.ShapeDtypeStruct((level_count, full_width), f32)],
            input_output_aliases={1 + len(operands): 0, 2 + len(operands): 1},
            compiler_params=small,
            cost_estimate=cheap,
            name="finish",
        )(place, *operands, mixed, query_grad)
    )


def solution(mesh):
    sharded = P(("ctx", "head"), None)
    return jax.shard_map(
        per_device,
        mesh=mesh,
        in_specs=(sharded,) * 4 + (P(),) * 4,
        out_specs=(sharded,) * 4 + (P(),),
        check_vma=False,
    )
```

```python
import functools
import math

import jax
import jax.numpy as jnp
from jax import lax
from jax.experimental import pallas as pl
from jax.experimental.pallas import tpu as pltpu
from jax.sharding import PartitionSpec as P

DH = 128
HIDDEN = -1e30
LOG2E = 1.4426950408889634


def other_ctx(c, near):
    odd = lax.rem(c, 2)
    return c + 1 - 2 * odd if near else c - 1 + 2 * odd


def prep_kernel(
    place_ref, span_ref, noise_ref, mask_ref, table_ref, bias_ref, gate_ref, slot_ref, *, sizes
):
    ctx_count, groups, rows, span_total, level_count, by_span = sizes
    c, h = lax.div(place_ref[0], groups), lax.rem(place_ref[0], groups)
    tokens = groups * rows
    total = ctx_count * tokens
    bf16, f32 = jnp.bfloat16, jnp.float32

    def block_of(ctx, k):
        return ctx * groups + lax.rem(h - k + groups, groups)

    def spans_of(ctx, k):
        at = jnp.clip(ctx, 0, ctx_count - 1)
        return span_ref[pl.ds(block_of(at, k), 1), :]

    def as_column(row):
        return jnp.broadcast_to(row.astype(f32), (rows, rows)).T[:, :1].astype(jnp.int32)

    across = lax.broadcasted_iota(jnp.int32, (1, rows), 1)
    down = lax.broadcasted_iota(jnp.int32, (rows, 1), 0)
    span_lane = lax.broadcasted_iota(jnp.int32, (rows, span_total), 1)
    span_down = lax.broadcasted_iota(jnp.int32, (span_total, rows), 0)
    level_lane = lax.broadcasted_iota(jnp.int32, (rows, level_count), 1)
    query_span = [spans_of(c, k) for k in range(groups)]
    query_pos = [block_of(c, k) * rows + across for k in range(groups)]
    mask_low = mask_ref[...].astype(bf16)
    allowed_q = [
        lax.dot_general(
            mask_low,
            (span_down == row).astype(bf16),
            (((0,), (0,)), ((), ())),
            preferred_element_type=f32,
        ).astype(bf16)
        for row in query_span
    ]
    noise = noise_ref[...].astype(f32)
    for i, ctx in enumerate((c, other_ctx(c, True), other_ctx(c, False))):
        for k in range(groups):
            key_span = as_column(spans_of(ctx, k))
            key_pos = block_of(ctx, k) * rows + down
            valid = (key_pos >= 0) & (key_pos < total)
            onehot = key_span == span_lane
            at = slice((i * groups + k) * rows, (i * groups + k + 1) * rows)
            for p in range(groups):
                allowed = jnp.dot(
                    onehot.astype(bf16), allowed_q[p], preferred_element_type=f32
                )
                visible = (
                    (allowed > 0.5)
                    & (key_span <= query_span[p])
                    & (query_pos[p] - key_pos < tokens)
                    & valid
                )
                bias_ref[at, p * rows : (p + 1) * rows] = jnp.where(visible, 0.0, HIDDEN)
            if i > 0:
                continue
            level = jnp.sum(jnp.where(onehot, noise, 0.0), axis=1, keepdims=True)
            level_onehot = (level.astype(jnp.int32) == level_lane).astype(f32)
            gate_ref[at, :] = jnp.dot(
                level_onehot,
                table_ref[...],
                precision=lax.Precision.HIGHEST,
                preferred_element_type=f32,
            )
            if by_span:
                slot_ref[:, at] = (span_down == query_span[k]).astype(bf16)
            else:
                slot_ref[:, at] = level_onehot.T.astype(bf16)


def attention_kernel(
    place_ref,
    qo_own_ref, kv_own_ref, qo_ref, kv_ref,
    near_own_ref, near_far_ref, side_own_ref, side_far_ref,
    gate_ref, bias_ref, slot_ref,
    *rest, rows, tokens, q_size, heads, apart,
):
    back_ref, own_ref, far_ref, near_grad_ref, *side_grad_refs = rest[-8 - apart : -3]
    mixed_ref, dq_ref, sums_ref = rest[-3:]
    scale = 1.0 / math.sqrt(DH)
    bf16, f32 = jnp.bfloat16, jnp.float32
    tile = 32

    def dot(left, right, left_dim, right_dim):
        return lax.dot_general(
            left, right, (((left_dim,), (right_dim,)), ((), ())), preferred_element_type=f32
        )

    def load(j):
        at = slice(j * DH, (j + 1) * DH)
        keys, values = [], []
        for ref in (
            kv_own_ref, kv_ref, near_own_ref, near_far_ref, side_own_ref, side_far_ref
        ):
            keys.append(ref[0, :, at])
            values.append(ref[1, :, at])
        keys, values = jnp.concatenate(keys, axis=0), jnp.concatenate(values, axis=0)
        queries = jnp.concatenate([qo_own_ref[0, :, at], qo_ref[0, :, at]], axis=0)
        cotangent = jnp.concatenate([qo_own_ref[1, :, at], qo_ref[1, :, at]], axis=0)
        blocks = []
        for start in range(0, tokens, q_size):
            span = slice(start, start + q_size)
            q, o = queries[span], cotangent[span].astype(f32)
            gate = gate_ref[span, at]
            g = (gate * o).astype(bf16)
            blocks.append((q, o, gate, g, dot(keys, q, 1, 1), dot(values, g, 1, 1)))
        return keys, values, blocks

    def work(j, keys, values, blocks):
        at = slice(j * DH, (j + 1) * DH)
        keys_t, values_t = keys.T, values.T
        key_grad = value_grad = sums = None
        for number, (q, o, gate, g, scores, prob_grad) in enumerate(blocks):
            start = number * q_size
            span = slice(start, start + q_size)
            count = scores.shape[0]
            tiles = [slice(r, r + tile) for r in range(0, count, tile)]
            raised, top = [], None
            for t in tiles:
                part = scores[t] * (scale * LOG2E) + bias_ref[t, span]
                raised.append(part)
                high = jnp.max(part.reshape(tile // 8, 8, q_size), axis=0)
                top = high if top is None else jnp.maximum(top, high)
            top = jnp.max(top, axis=0, keepdims=True)
            total = None
            for i in range(len(tiles)):
                raised[i] = jnp.exp2(raised[i] - top)
                part = jnp.sum(raised[i].reshape(tile // 8, 8, q_size), axis=0)
                total = part if total is None else total + part
            inverse = 1.0 / jnp.sum(total, axis=0, keepdims=True)
            low = jnp.concatenate([(part * inverse).astype(bf16) for part in raised], axis=0)
            attended_t = dot(values_t, low, 1, 0).astype(bf16)
            row_dot = jnp.sum(g.T.astype(f32) * attended_t.astype(f32), axis=0, keepdims=True)
            attended = attended_t.T.astype(f32)
            score_grad = jnp.concatenate(
                [
                    (part * ((prob_grad[t] - row_dot) * inverse)).astype(bf16)
                    for part, t in zip(raised, tiles)
                ],
                axis=0,
            )
            query_grad = (dot(keys_t, score_grad, 1, 0) * scale).astype(bf16).T
            mixed = (gate * attended).astype(bf16)
            if start == 0:
                mixed_ref[:, at] = mixed[:rows]
                dq_ref[:, at] = query_grad[:rows]
                back_ref[0, : q_size - rows, at] = mixed[rows:]
                back_ref[1, : q_size - rows, at] = query_grad[rows:]
            else:
                back_ref[0, start - rows : start - rows + q_size, at] = mixed
                back_ref[1, start - rows : start - rows + q_size, at] = query_grad
            dk, dv = dot(score_grad, q, 1, 0), dot(low, g, 1, 0)
            product = o * attended
            high = product.astype(bf16)
            rest = (product - high.astype(f32)).astype(bf16)
            both = dot(slot_ref[:, span], jnp.concatenate([high, rest], axis=1), 1, 0)
            part = both[:, :DH] + both[:, DH:]
            key_grad = dk if key_grad is None else key_grad + dk
            value_grad = dv if value_grad is None else value_grad + dv
            sums = part if sums is None else sums + part
        sums_ref[:, at] = sums.astype(bf16)
        for i, grad in ((0, key_grad * scale), (1, value_grad)):
            own_ref[i, :, at] = grad[:rows]
            far_ref[i, :, at] = grad[rows:tokens]
            low = grad[tokens:].astype(bf16)
            near_grad_ref[i, :, at] = low[:tokens]
            if apart:
                side_grad_refs[0][i, :, at] = low[tokens : tokens + rows]
                side_grad_refs[1][i, :, at] = low[tokens + rows :]
            else:
                side_grad_refs[0][i, :, at] = low[tokens:]

    ready = load(0)
    for j in range(heads):
        following = load(j + 1) if j + 1 < heads else None
        work(j, *ready)
        ready = following


def pack_kernel(place_ref, first_ref, second_ref, own_ref, *rest, groups):
    *far_refs, sems = rest
    rows, width = own_ref.shape[1:]
    copies = []

    def copy(ref, start, to):
        cols = pl.ds(pl.multiple_of(start, DH), to.shape[1])
        copies.append(pltpu.make_async_copy(ref.at[:, cols], to, sems.at[len(copies)]))
        copies[-1].start()

    for k in (*range(1, groups), 0):
        start = lax.rem(place_ref[0] + k, groups) * width
        for i, ref in enumerate((first_ref, second_ref)):
            if k == 0:
                copy(ref, start, own_ref.at[i])
                continue
            for p, far_ref in enumerate(far_refs):
                at = pl.ds((k - 1) * rows, rows)
                copy(ref, start + p * far_ref.shape[2], far_ref.at[i, at])
    for one in copies:
        one.wait()


def far_sum_kernel(part_ref, near_ref, side_ref, out_ref):
    far = slice(near_ref.shape[1] - part_ref.shape[1], None)
    total = part_ref[...] + near_ref[:, far].astype(jnp.float32)
    side = side_ref[:, side_ref.shape[1] - part_ref.shape[1] :].astype(jnp.float32)
    out_ref[...] = (total + side).astype(out_ref.dtype)


def finish_kernel(place_ref, part_ref, near_ref, side_ref, *refs, groups, parts, p, gate):
    slabs, refs = refs[: 2 * (groups - 1)], refs[2 * (groups - 1) :]
    slot_refs = refs[1 : 1 + groups] if gate else ()
    scratch = 3 if gate else 2
    total_ref, *gate_scratch, sems = refs[-scratch:]
    outs = refs[-scratch - (5 if gate else 4) : -scratch]
    part_width = part_ref.shape[2]
    width = part_width * parts
    copies = []

    def send(source, to):
        copies.append(pltpu.make_async_copy(source, to, sems.at[len(copies)]))
        copies[-1].start()

    def place_slab(slab, first, second, k):
        start = lax.rem(place_ref[0] + k, groups) * width + p * part_width
        cols = pl.ds(pl.multiple_of(start, DH), part_width)
        for i, ref in enumerate((first, second)):
            send(slab.at[i], ref.at[:, cols])

    for k in range(1, groups):
        place_slab(slabs[k - 1], outs[0], outs[1], k)
        place_slab(slabs[groups + k - 2], outs[2], outs[3], k)
    near, side = (ref[:, : part_ref.shape[1]].astype(jnp.float32) for ref in (near_ref, side_ref))
    total_ref[...] = (part_ref[...] + near + side).astype(total_ref.dtype)
    place_slab(total_ref, outs[2], outs[3], 0)
    if gate:
        noise_ref, gate_ref = refs[0], gate_scratch[0]
        by_span = noise_ref.shape[1] == slot_refs[0].shape[0]
        levels = lax.broadcasted_iota(jnp.int32, (gate_ref.shape[0], noise_ref.shape[1]), 0)
        onehot = (levels == noise_ref[...]).astype(jnp.bfloat16)
        for j, ref in enumerate(slot_refs):
            if by_span:
                sums = jnp.dot(onehot, ref[...], preferred_element_type=jnp.float32)
            else:
                sums = ref[...].astype(jnp.float32)
            start = lax.bitwise_xor(lax.rem(place_ref[0], groups), j) * width
            cols = pl.ds(pl.multiple_of(start, DH), width)
            gate_ref[:, cols] = sums
            send(gate_ref.at[:, cols], outs[4].at[:, cols])
    for one in copies:
        one.wait()


def per_device(
    queries, key_rows, value_rows, out_cotangent, gate_table, span_ids, noise_level, block_mask
):
    groups = lax.axis_size("head")
    ctx_count = lax.axis_size("ctx")
    rows, full_width = queries.shape
    width = full_width // groups
    heads = width // DH
    tokens = rows * groups
    far_rows = tokens - rows
    parts = 2 if heads % 2 == 0 else 1
    part_width = width // parts
    part_heads = heads // parts
    span_total = noise_level.shape[0]
    level_count = gate_table.shape[0]
    by_span = span_total <= level_count // 2
    slots = span_total if by_span else level_count
    c = lax.axis_index("ctx")
    h = lax.axis_index("head")
    place = (c * groups + h).astype(jnp.int32).reshape(1)
    head_at = lambda place: lax.rem(place[0], groups)
    bf16, f32 = jnp.bfloat16, jnp.float32
    tie = lax.optimization_barrier

    near_pairs = [(i, i ^ 1) for i in range(ctx_count)]
    side_of = [i - 1 + 2 * (i % 2) for i in range(ctx_count)]
    side_pairs = [(i, j if 0 <= j < ctx_count else i) for i, j in enumerate(side_of)]

    whole = lambda shape: pl.BlockSpec(shape, lambda i, place: (0,) * len(shape))
    limit = (26 if tokens <= 256 else 56) * 1024 * 1024
    params = pltpu.CompilerParams(vmem_limit_bytes=limit)
    alone = pltpu.CompilerParams(vmem_limit_bytes=56 * 1024 * 1024)
    cheap = pl.CostEstimate(flops=1, bytes_accessed=1, transcendentals=0)
    in_vmem = pl.BlockSpec(memory_space=pltpu.VMEM)
    anywhere = pl.BlockSpec(memory_space=pl.ANY)
    small = pltpu.CompilerParams(vmem_limit_bytes=(12 if tokens <= 256 else 36) * 1024 * 1024)

    def pack(first, second, params):
        far_shape = (2, far_rows, part_width)
        return pl.pallas_call(
            functools.partial(pack_kernel, groups=groups),
            grid_spec=pltpu.PrefetchScalarGridSpec(
                num_scalar_prefetch=1,
                in_specs=[anywhere] * 2,
                out_specs=[in_vmem] * (1 + parts),
                scratch_shapes=[pltpu.SemaphoreType.DMA((2 + 2 * (groups - 1) * parts,))],
            ),
            out_shape=[jax.ShapeDtypeStruct((2, rows, width), bf16)]
            + [jax.ShapeDtypeStruct(far_shape, bf16)] * parts,
            compiler_params=params,
            cost_estimate=cheap,
            name="pack",
        )(place, first, second)

    def to_peers(slab):
        arrived = []
        for k in range(1, groups):
            part = slab if groups == 2 else slab[:, (k - 1) * rows : k * rows]
            pairs = [(i, (i + k) % groups) for i in range(groups)]
            arrived.append(lax.ppermute(part, "head", pairs))
        return arrived[0] if groups == 2 else jnp.concatenate(arrived, axis=1)

    def from_peers(slab):
        arrived = []
        for k in range(1, groups):
            part = slab if groups == 2 else slab[:, (k - 1) * rows : k * rows]
            pairs = [(i, (i - k) % groups) for i in range(groups)]
            arrived.append(lax.ppermute(part, "head", pairs))
        return arrived

    kv_own, *kv_sent = pack(key_rows, value_rows, alone)
    qo_own, *qo_sent = pack(queries, out_cotangent, small)
    side_own = lax.ppermute(kv_own, "ctx", side_pairs)
    near_own = lax.ppermute(kv_own, "ctx", near_pairs)
    kv_far = [to_peers(slab) for slab in kv_sent]
    side_far = [lax.ppermute(slab, "ctx", side_pairs) for slab in kv_far]
    near_far = [lax.ppermute(slab, "ctx", near_pairs) for slab in kv_far]
    qo_far = [
        to_peers(tie((slab, *done))[0])
        for slab, done in zip(qo_sent, (kv_far[:1], (*kv_far[1:], side_own, near_own)))
    ]

    sizes = (ctx_count, groups, rows, span_total, level_count, by_span)
    whole = lambda shape: pl.BlockSpec(shape, lambda i, place: (0,) * len(shape))
    bias, gate, slot = pl.pallas_call(
        functools.partial(prep_kernel, sizes=sizes),
        grid_spec=pltpu.PrefetchScalarGridSpec(
            num_scalar_prefetch=1,
            grid=(1,),
            in_specs=[
                whole((ctx_count * groups, rows)),
                whole((1, span_total)),
                whole((span_total, span_total)),
                pl.BlockSpec((level_count, width), lambda i, place: (0, head_at(place))),
            ],
            out_specs=[
                whole((3 * tokens, tokens)),
                whole((tokens, width)),
                whole((slots, tokens)),
            ],
        ),
        out_shape=[
            jax.ShapeDtypeStruct((3 * tokens, tokens), f32),
            jax.ShapeDtypeStruct((tokens, width), f32),
            jax.ShapeDtypeStruct((slots, tokens), bf16),
        ],
        compiler_params=small,
        cost_estimate=cheap,
        name="prep",
    )(
        place,
        span_ids.reshape(ctx_count * groups, rows),
        noise_level.reshape(1, span_total),
        block_mask,
        gate_table,
    )

    batch = next(n for n in (3, 2, 1) if part_heads % n == 0) if tokens <= 256 else 1
    steps = part_heads // batch
    block = batch * DH
    q_size = min(256, tokens)

    def attention(p, joint):
        pair = lambda count: pl.BlockSpec((2, count, block), lambda i, place: (0, 0, i))
        at_part = lambda count: pl.BlockSpec(
            (2, count, block), lambda i, place: (0, 0, p * steps + i)
        )
        at_head = pl.BlockSpec(
            (rows, block), lambda i, place: (0, (head_at(place) * parts + p) * steps + i)
        )
        column = lambda count: pl.BlockSpec((count, block), lambda i, place: (0, p * steps + i))
        struct = jax.ShapeDtypeStruct
        side_counts = (rows, far_rows) if p + 1 == parts else (tokens,)
        inputs = [
            qo_own, kv_own, qo_far[p], kv_far[p],
            near_own, near_far[p], side_own, side_far[p],
            gate, bias, slot,
        ]
        return pl.pallas_call(
            functools.partial(
                attention_kernel,
                rows=rows, tokens=tokens, q_size=q_size, heads=batch, apart=p + 1 == parts,
            ),
            grid_spec=pltpu.PrefetchScalarGridSpec(
                num_scalar_prefetch=1,
                grid=(steps,),
                in_specs=[
                    at_part(rows), at_part(rows), pair(far_rows), pair(far_rows),
                    at_part(rows), pair(far_rows), at_part(rows), pair(far_rows),
                    column(tokens), whole((3 * tokens, tokens)), whole((slots, tokens)),
                ]
                + [pl.BlockSpec(memory_space=pl.ANY)] * len(joint),
                out_specs=[
                    pair(far_rows), pair(rows), pair(far_rows), pair(tokens),
                    *[pair(count) for count in side_counts],
                    at_head, at_head, column(slots),
                ],
            ),
            out_shape=[
                struct((2, far_rows, part_width), bf16),
                struct((2, rows, part_width), f32),
                struct((2, far_rows, part_width), f32),
                struct((2, tokens, part_width), bf16),
                *[struct((2, count, part_width), bf16) for count in side_counts],
                struct((rows, full_width), bf16),
                struct((rows, full_width), bf16),
                struct((slots, width), bf16),
            ],
            input_output_aliases={1 + len(inputs) + i: 4 + len(side_counts) + i for i in range(len(joint))},
            compiler_params=params,
            cost_estimate=cheap,
            name="attention",
        )(place, *inputs, *joint)

    def summed(p):
        far_grad = pl.pallas_call(
            far_sum_kernel,
            in_specs=[in_vmem] * 3,
            out_specs=in_vmem,
            out_shape=jax.ShapeDtypeStruct((2, far_rows, part_width), bf16),
            compiler_params=small,
            cost_estimate=cheap,
            name="far_sum",
        )(far[p], near_back[p], side_back_far[p])
        far_sent.append(far_grad)
        grad_far.append(from_peers(far_grad))

    joint, own, far = (), [], []
    back_far, side_back_far, near_back, side_back_own, far_sent, grad_far = [], [], [], [], [], []
    for p in range(parts):
        back, own_part, far_part, near_grad, *rest = attention(p, joint)
        side_grads, joint = rest[:-3], rest[-3:]
        if p + 1 < parts:
            side_grads, *_ = tie((side_grads, side_far[p + 1], near_far[p + 1], qo_far[p + 1]))
        if p > 0:
            back, side_back_far, back_far = tie(
                (back, side_back_far, back_far)
            )
            summed(p - 1)
        own.append(own_part)
        far.append(far_part)
        side_back_far.append(lax.ppermute(side_grads[-1], "ctx", side_pairs))
        near_back.append(lax.ppermute(near_grad, "ctx", near_pairs))
        back_far.append(from_peers(back))
        if p + 1 < parts:
            side_back_own.append(side_back_far[p])
            continue
        side_grad_own, _ = tie((side_grads[0], side_back_far[p]))
        side_back_own.append(lax.ppermute(side_grad_own, "ctx", side_pairs))
    mixed, query_grad, sums = joint

    def shifted(array, step):
        return lax.ppermute(array, "ctx", [(i, i ^ step) for i in range(ctx_count)])

    def rounds(steps, sums):
        for one, two in zip(steps[::2], [*steps[1::2], None]):
            if two is None:
                sums = sums + shifted(sums, one)
                continue
            across = [shifted(sums, step) for step in (one, two, one ^ two)]
            sums = (sums + across[0]) + (across[1] + across[2])
        return sums

    bits = [1 << n for n in range(ctx_count.bit_length() - 1)]
    sums = rounds(bits[:1], rounds(bits[2:], sums))
    side_back_far, sums, back_far, grad_far = tie((side_back_far, sums, back_far, grad_far))
    summed(parts - 1)

    def to_all(before, after, sums):
        slabs = [rounds(before, sums)]
        for step in (1 << n for n in range(groups.bit_length() - 1)):
            pairs = [(i, i ^ step) for i in range(groups)]
            slabs = slabs + [lax.ppermute(slab, "head", pairs) for slab in slabs]
        return [rounds(after, slab) for slab in slabs]

    sums, _ = tie((sums, far_sent[-1]))
    slabs = to_all(bits[1:2], [], sums)
    results = [mixed, query_grad]
    struct = jax.ShapeDtypeStruct
    for p in range(parts):
        gate = p + 1 == parts
        operands = [own[p], near_back[p], side_back_own[p], *back_far[p], *grad_far[p]]
        if gate:
            operands += [noise_level.reshape(1, span_total), *slabs]
        scratch = [pltpu.VMEM((2, rows, part_width), bf16)]
        if gate:
            scratch.append(pltpu.VMEM((level_count, full_width), f32))
        scratch.append(pltpu.SemaphoreType.DMA((4 * groups - 2 + groups,)))
        results = pl.pallas_call(
            functools.partial(finish_kernel, groups=groups, parts=parts, p=p, gate=gate),
            grid_spec=pltpu.PrefetchScalarGridSpec(
                num_scalar_prefetch=1,
                in_specs=[in_vmem] * len(operands) + [anywhere] * len(results),
                out_specs=[anywhere] * (4 + gate),
                scratch_shapes=scratch,
            ),
            out_shape=[struct((rows, full_width), bf16)] * 4
            + [struct((level_count, full_width), f32)] * gate,
            input_output_aliases={1 + len(operands) + i: i for i in range(len(results))},
            compiler_params=small,
            cost_estimate=cheap,
            name="finish",
        )(place, *operands, *results)
    return tuple(results)


def solution(mesh):
    sharded = P(("ctx", "head"), None)
    return jax.shard_map(
        per_device,
        mesh=mesh,
        in_specs=(sharded,) * 4 + (P(),) * 4,
        out_specs=(sharded,) * 4 + (P(),),
        check_vma=False,
    )
```

```python
import functools
import math

import jax
import jax.numpy as jnp
from jax import lax
from jax.experimental import pallas as pl
from jax.experimental.pallas import tpu as pltpu
from jax.sharding import PartitionSpec as P

DH = 128
HIDDEN = -1e30
LOG2E = 1.4426950408889634


def other_ctx(c, near):
    odd = lax.rem(c, 2)
    return c + 1 - 2 * odd if near else c - 1 + 2 * odd


def prep_kernel(
    place_ref, span_ref, noise_ref, mask_ref, table_ref, bias_ref, gate_ref, slot_ref, *, sizes
):
    ctx_count, groups, rows, span_total, level_count, by_span = sizes
    c, h = lax.div(place_ref[0], groups), lax.rem(place_ref[0], groups)
    tokens = groups * rows
    total = ctx_count * tokens
    bf16, f32 = jnp.bfloat16, jnp.float32

    def block_of(ctx, k):
        return ctx * groups + lax.rem(h - k + groups, groups)

    def spans_of(ctx, k):
        at = jnp.clip(ctx, 0, ctx_count - 1)
        return span_ref[pl.ds(block_of(at, k), 1), :]

    def as_column(row):
        return jnp.broadcast_to(row.astype(f32), (rows, rows)).T[:, :1].astype(jnp.int32)

    across = lax.broadcasted_iota(jnp.int32, (1, rows), 1)
    down = lax.broadcasted_iota(jnp.int32, (rows, 1), 0)
    span_lane = lax.broadcasted_iota(jnp.int32, (rows, span_total), 1)
    span_down = lax.broadcasted_iota(jnp.int32, (span_total, rows), 0)
    level_lane = lax.broadcasted_iota(jnp.int32, (rows, level_count), 1)
    query_span = [spans_of(c, k) for k in range(groups)]
    query_pos = [block_of(c, k) * rows + across for k in range(groups)]
    mask_low = mask_ref[...].astype(bf16)
    allowed_q = [
        lax.dot_general(
            mask_low,
            (span_down == row).astype(bf16),
            (((0,), (0,)), ((), ())),
            preferred_element_type=f32,
        ).astype(bf16)
        for row in query_span
    ]
    noise = noise_ref[...].astype(f32)
    for i, ctx in enumerate((c, other_ctx(c, True), other_ctx(c, False))):
        for k in range(groups):
            key_span = as_column(spans_of(ctx, k))
            key_pos = block_of(ctx, k) * rows + down
            valid = (key_pos >= 0) & (key_pos < total)
            onehot = key_span == span_lane
            at = slice((i * groups + k) * rows, (i * groups + k + 1) * rows)
            for p in range(groups):
                allowed = jnp.dot(
                    onehot.astype(bf16), allowed_q[p], preferred_element_type=f32
                )
                visible = (
                    (allowed > 0.5)
                    & (key_span <= query_span[p])
                    & (query_pos[p] - key_pos < tokens)
                    & valid
                )
                bias_ref[at, p * rows : (p + 1) * rows] = jnp.where(visible, 0.0, HIDDEN)
            if i > 0:
                continue
            level = jnp.sum(jnp.where(onehot, noise, 0.0), axis=1, keepdims=True)
            level_onehot = (level.astype(jnp.int32) == level_lane).astype(f32)
            gate_ref[at, :] = jnp.dot(
                level_onehot,
                table_ref[...],
                precision=lax.Precision.HIGHEST,
                preferred_element_type=f32,
            )
            if by_span:
                slot_ref[:, at] = (span_down == query_span[k]).astype(bf16)
            else:
                slot_ref[:, at] = level_onehot.T.astype(bf16)


def attention_kernel(
    place_ref,
    qo_own_ref, kv_own_ref, qo_ref, kv_ref,
    near_own_ref, near_far_ref, side_own_ref, side_far_ref,
    gate_ref, bias_ref, slot_ref,
    *rest, rows, tokens, q_size, heads, apart,
):
    back_ref, own_ref, far_ref, near_grad_ref, *side_grad_refs = rest[-8 - apart : -3]
    mixed_ref, dq_ref, sums_ref = rest[-3:]
    scale = 1.0 / math.sqrt(DH)
    bf16, f32 = jnp.bfloat16, jnp.float32
    tile = 32

    def dot(left, right, left_dim, right_dim):
        return lax.dot_general(
            left, right, (((left_dim,), (right_dim,)), ((), ())), preferred_element_type=f32
        )

    def load(j):
        at = slice(j * DH, (j + 1) * DH)
        keys, values = [], []
        for ref in (
            kv_own_ref, kv_ref, near_own_ref, near_far_ref, side_own_ref, side_far_ref
        ):
            keys.append(ref[0, :, at])
            values.append(ref[1, :, at])
        keys, values = jnp.concatenate(keys, axis=0), jnp.concatenate(values, axis=0)
        queries = jnp.concatenate([qo_own_ref[0, :, at], qo_ref[0, :, at]], axis=0)
        cotangent = jnp.concatenate([qo_own_ref[1, :, at], qo_ref[1, :, at]], axis=0)
        blocks = []
        for start in range(0, tokens, q_size):
            span = slice(start, start + q_size)
            q, o = queries[span], cotangent[span].astype(f32)
            gate = gate_ref[span, at]
            g = (gate * o).astype(bf16)
            blocks.append((q, o, gate, g, dot(keys, q, 1, 1), dot(values, g, 1, 1)))
        return keys, values, blocks

    def work(j, keys, values, blocks):
        at = slice(j * DH, (j + 1) * DH)
        unit = lax.broadcasted_iota(jnp.int32, (DH, DH), 0) == lax.broadcasted_iota(
            jnp.int32, (DH, DH), 1
        )
        unit = unit.astype(bf16)
        keys_t, values_t = dot(unit, keys, 1, 1).astype(bf16), dot(unit, values, 1, 1).astype(bf16)
        key_grad = value_grad = sums = None
        for number, (q, o, gate, g, scores, prob_grad) in enumerate(blocks):
            start = number * q_size
            span = slice(start, start + q_size)
            count = scores.shape[0]
            tiles = [slice(r, r + tile) for r in range(0, count, tile)]
            raised, top = [], None
            for t in tiles:
                part = scores[t] * (scale * LOG2E) + bias_ref[t, span]
                raised.append(part)
                high = jnp.max(part.reshape(tile // 8, 8, q_size), axis=0)
                top = high if top is None else jnp.maximum(top, high)
            top = jnp.max(top, axis=0, keepdims=True)
            total = None
            for i in range(len(tiles)):
                raised[i] = jnp.exp2(raised[i] - top)
                part = jnp.sum(raised[i].reshape(tile // 8, 8, q_size), axis=0)
                total = part if total is None else total + part
            inverse = 1.0 / jnp.sum(total, axis=0, keepdims=True)
            low = jnp.concatenate([(part * inverse).astype(bf16) for part in raised], axis=0)
            attended_t = dot(values_t, low, 1, 0).astype(bf16)
            row_dot = jnp.sum(g.T.astype(f32) * attended_t.astype(f32), axis=0, keepdims=True)
            attended = attended_t.T.astype(f32)
            score_grad = jnp.concatenate(
                [
                    (part * ((prob_grad[t] - row_dot) * inverse)).astype(bf16)
                    for part, t in zip(raised, tiles)
                ],
                axis=0,
            )
            query_grad = (dot(keys_t, score_grad, 1, 0) * scale).astype(bf16).T
            mixed = (gate * attended).astype(bf16)
            if start == 0:
                mixed_ref[:, at] = mixed[:rows]
                dq_ref[:, at] = query_grad[:rows]
                back_ref[0, : q_size - rows, at] = mixed[rows:]
                back_ref[1, : q_size - rows, at] = query_grad[rows:]
            else:
                back_ref[0, start - rows : start - rows + q_size, at] = mixed
                back_ref[1, start - rows : start - rows + q_size, at] = query_grad
            dk, dv = dot(score_grad, q, 1, 0), dot(low, g, 1, 0)
            product = o * attended
            high = product.astype(bf16)
            rest = (product - high.astype(f32)).astype(bf16)
            both = dot(slot_ref[:, span], jnp.concatenate([high, rest], axis=1), 1, 0)
            part = both[:, :DH] + both[:, DH:]
            key_grad = dk if key_grad is None else key_grad + dk
            value_grad = dv if value_grad is None else value_grad + dv
            sums = part if sums is None else sums + part
        sums_ref[:, at] = sums.astype(bf16)
        for i, grad in ((0, key_grad * scale), (1, value_grad)):
            own_ref[i, :, at] = grad[:rows]
            far_ref[i, :, at] = grad[rows:tokens]
            low = grad[tokens:].astype(bf16)
            near_grad_ref[i, :, at] = low[:tokens]
            if apart:
                side_grad_refs[0][i, :, at] = low[tokens : tokens + rows]
                side_grad_refs[1][i, :, at] = low[tokens + rows :]
            else:
                side_grad_refs[0][i, :, at] = low[tokens:]

    ready = load(0)
    for j in range(heads):
        following = load(j + 1) if j + 1 < heads else None
        work(j, *ready)
        ready = following


def pack_kernel(place_ref, first_ref, second_ref, own_ref, *rest, groups):
    *far_refs, sems = rest
    rows, width = own_ref.shape[1:]
    copies = []

    def copy(ref, start, to):
        cols = pl.ds(pl.multiple_of(start, DH), to.shape[1])
        copies.append(pltpu.make_async_copy(ref.at[:, cols], to, sems.at[len(copies)]))
        copies[-1].start()

    for k in (*range(1, groups), 0):
        start = lax.rem(place_ref[0] + k, groups) * width
        for i, ref in enumerate((first_ref, second_ref)):
            if k == 0:
                copy(ref, start, own_ref.at[i])
                continue
            for p, far_ref in enumerate(far_refs):
                at = pl.ds((k - 1) * rows, rows)
                copy(ref, start + p * far_ref.shape[2], far_ref.at[i, at])
    for one in copies:
        one.wait()


def far_sum_kernel(part_ref, near_ref, side_ref, out_ref):
    far = slice(near_ref.shape[1] - part_ref.shape[1], None)
    total = part_ref[...] + near_ref[:, far].astype(jnp.float32)
    side = side_ref[:, side_ref.shape[1] - part_ref.shape[1] :].astype(jnp.float32)
    out_ref[...] = (total + side).astype(out_ref.dtype)


def finish_kernel(place_ref, part_ref, near_ref, side_ref, *refs, groups, parts, p, gate):
    slabs, refs = refs[: 2 * (groups - 1)], refs[2 * (groups - 1) :]
    slot_refs = refs[1 : 1 + groups] if gate else ()
    scratch = 3 if gate else 2
    total_ref, *gate_scratch, sems = refs[-scratch:]
    outs = refs[-scratch - (5 if gate else 4) : -scratch]
    part_width = part_ref.shape[2]
    width = part_width * parts
    copies = []

    def send(source, to):
        copies.append(pltpu.make_async_copy(source, to, sems.at[len(copies)]))
        copies[-1].start()

    def place_slab(slab, first, second, k):
        start = lax.rem(place_ref[0] + k, groups) * width + p * part_width
        cols = pl.ds(pl.multiple_of(start, DH), part_width)
        for i, ref in enumerate((first, second)):
            send(slab.at[i], ref.at[:, cols])

    for k in range(1, groups):
        place_slab(slabs[k - 1], outs[0], outs[1], k)
        place_slab(slabs[groups + k - 2], outs[2], outs[3], k)
    near, side = (ref[:, : part_ref.shape[1]].astype(jnp.float32) for ref in (near_ref, side_ref))
    total_ref[...] = (part_ref[...] + near + side).astype(total_ref.dtype)
    place_slab(total_ref, outs[2], outs[3], 0)
    if gate:
        noise_ref, gate_ref = refs[0], gate_scratch[0]
        by_span = noise_ref.shape[1] == slot_refs[0].shape[0]
        levels = lax.broadcasted_iota(jnp.int32, (gate_ref.shape[0], noise_ref.shape[1]), 0)
        onehot = (levels == noise_ref[...]).astype(jnp.bfloat16)
        for j, ref in enumerate(slot_refs):
            if by_span:
                sums = jnp.dot(onehot, ref[...], preferred_element_type=jnp.float32)
            else:
                sums = ref[...].astype(jnp.float32)
            start = lax.bitwise_xor(lax.rem(place_ref[0], groups), j) * width
            cols = pl.ds(pl.multiple_of(start, DH), width)
            gate_ref[:, cols] = sums
            send(gate_ref.at[:, cols], outs[4].at[:, cols])
    for one in copies:
        one.wait()


def per_device(
    queries, key_rows, value_rows, out_cotangent, gate_table, span_ids, noise_level, block_mask
):
    groups = lax.axis_size("head")
    ctx_count = lax.axis_size("ctx")
    rows, full_width = queries.shape
    width = full_width // groups
    heads = width // DH
    tokens = rows * groups
    far_rows = tokens - rows
    parts = 2 if heads % 2 == 0 else 1
    part_width = width // parts
    part_heads = heads // parts
    span_total = noise_level.shape[0]
    level_count = gate_table.shape[0]
    by_span = span_total <= level_count // 2
    slots = span_total if by_span else level_count
    c = lax.axis_index("ctx")
    h = lax.axis_index("head")
    place = (c * groups + h).astype(jnp.int32).reshape(1)
    head_at = lambda place: lax.rem(place[0], groups)
    bf16, f32 = jnp.bfloat16, jnp.float32
    tie = lax.optimization_barrier

    near_pairs = [(i, i ^ 1) for i in range(ctx_count)]
    side_of = [i - 1 + 2 * (i % 2) for i in range(ctx_count)]
    side_pairs = [(i, j if 0 <= j < ctx_count else i) for i, j in enumerate(side_of)]

    whole = lambda shape: pl.BlockSpec(shape, lambda i, place: (0,) * len(shape))
    limit = (26 if tokens <= 256 else 56) * 1024 * 1024
    params = pltpu.CompilerParams(vmem_limit_bytes=limit)
    alone = pltpu.CompilerParams(vmem_limit_bytes=56 * 1024 * 1024)
    cheap = pl.CostEstimate(flops=1, bytes_accessed=1, transcendentals=0)
    in_vmem = pl.BlockSpec(memory_space=pltpu.VMEM)
    anywhere = pl.BlockSpec(memory_space=pl.ANY)
    small = pltpu.CompilerParams(vmem_limit_bytes=(12 if tokens <= 256 else 36) * 1024 * 1024)

    def pack(first, second, params):
        far_shape = (2, far_rows, part_width)
        return pl.pallas_call(
            functools.partial(pack_kernel, groups=groups),
            grid_spec=pltpu.PrefetchScalarGridSpec(
                num_scalar_prefetch=1,
                in_specs=[anywhere] * 2,
                out_specs=[in_vmem] * (1 + parts),
                scratch_shapes=[pltpu.SemaphoreType.DMA((2 + 2 * (groups - 1) * parts,))],
            ),
            out_shape=[jax.ShapeDtypeStruct((2, rows, width), bf16)]
            + [jax.ShapeDtypeStruct(far_shape, bf16)] * parts,
            compiler_params=params,
            cost_estimate=cheap,
            name="pack",
        )(place, first, second)

    def to_peers(slab):
        arrived = []
        for k in range(1, groups):
            part = slab if groups == 2 else slab[:, (k - 1) * rows : k * rows]
            pairs = [(i, (i + k) % groups) for i in range(groups)]
            arrived.append(lax.ppermute(part, "head", pairs))
        return arrived[0] if groups == 2 else jnp.concatenate(arrived, axis=1)

    def from_peers(slab):
        arrived = []
        for k in range(1, groups):
            part = slab if groups == 2 else slab[:, (k - 1) * rows : k * rows]
            pairs = [(i, (i - k) % groups) for i in range(groups)]
            arrived.append(lax.ppermute(part, "head", pairs))
        return arrived

    kv_own, *kv_sent = pack(key_rows, value_rows, alone)
    qo_own, *qo_sent = pack(queries, out_cotangent, small)
    side_own = lax.ppermute(kv_own, "ctx", side_pairs)
    near_own = lax.ppermute(kv_own, "ctx", near_pairs)
    kv_far = [to_peers(slab) for slab in kv_sent]
    side_far = [lax.ppermute(slab, "ctx", side_pairs) for slab in kv_far]
    near_far = [lax.ppermute(slab, "ctx", near_pairs) for slab in kv_far]
    qo_far = [
        to_peers(tie((slab, *done))[0])
        for slab, done in zip(qo_sent, (kv_far[:1], (*kv_far[1:], side_own, near_own)))
    ]

    sizes = (ctx_count, groups, rows, span_total, level_count, by_span)
    whole = lambda shape: pl.BlockSpec(shape, lambda i, place: (0,) * len(shape))
    bias, gate, slot = pl.pallas_call(
        functools.partial(prep_kernel, sizes=sizes),
        grid_spec=pltpu.PrefetchScalarGridSpec(
            num_scalar_prefetch=1,
            grid=(1,),
            in_specs=[
                whole((ctx_count * groups, rows)),
                whole((1, span_total)),
                whole((span_total, span_total)),
                pl.BlockSpec((level_count, width), lambda i, place: (0, head_at(place))),
            ],
            out_specs=[
                whole((3 * tokens, tokens)),
                whole((tokens, width)),
                whole((slots, tokens)),
            ],
        ),
        out_shape=[
            jax.ShapeDtypeStruct((3 * tokens, tokens), f32),
            jax.ShapeDtypeStruct((tokens, width), f32),
            jax.ShapeDtypeStruct((slots, tokens), bf16),
        ],
        compiler_params=small,
        cost_estimate=cheap,
        name="prep",
    )(
        place,
        span_ids.reshape(ctx_count * groups, rows),
        noise_level.reshape(1, span_total),
        block_mask,
        gate_table,
    )

    batch = next(n for n in (3, 2, 1) if part_heads % n == 0) if tokens <= 256 else 1
    steps = part_heads // batch
    block = batch * DH
    q_size = min(256, tokens)

    def attention(p, joint):
        pair = lambda count: pl.BlockSpec((2, count, block), lambda i, place: (0, 0, i))
        at_part = lambda count: pl.BlockSpec(
            (2, count, block), lambda i, place: (0, 0, p * steps + i)
        )
        at_head = pl.BlockSpec(
            (rows, block), lambda i, place: (0, (head_at(place) * parts + p) * steps + i)
        )
        column = lambda count: pl.BlockSpec((count, block), lambda i, place: (0, p * steps + i))
        struct = jax.ShapeDtypeStruct
        side_counts = (rows, far_rows) if p + 1 == parts else (tokens,)
        inputs = [
            qo_own, kv_own, qo_far[p], kv_far[p],
            near_own, near_far[p], side_own, side_far[p],
            gate, bias, slot,
        ]
        return pl.pallas_call(
            functools.partial(
                attention_kernel,
                rows=rows, tokens=tokens, q_size=q_size, heads=batch, apart=p + 1 == parts,
            ),
            grid_spec=pltpu.PrefetchScalarGridSpec(
                num_scalar_prefetch=1,
                grid=(steps,),
                in_specs=[
                    at_part(rows), at_part(rows), pair(far_rows), pair(far_rows),
                    at_part(rows), pair(far_rows), at_part(rows), pair(far_rows),
                    column(tokens), whole((3 * tokens, tokens)), whole((slots, tokens)),
                ]
                + [pl.BlockSpec(memory_space=pl.ANY)] * len(joint),
                out_specs=[
                    pair(far_rows), pair(rows), pair(far_rows), pair(tokens),
                    *[pair(count) for count in side_counts],
                    at_head, at_head, column(slots),
                ],
            ),
            out_shape=[
                struct((2, far_rows, part_width), bf16),
                struct((2, rows, part_width), f32),
                struct((2, far_rows, part_width), f32),
                struct((2, tokens, part_width), bf16),
                *[struct((2, count, part_width), bf16) for count in side_counts],
                struct((rows, full_width), bf16),
                struct((rows, full_width), bf16),
                struct((slots, width), bf16),
            ],
            input_output_aliases={1 + len(inputs) + i: 4 + len(side_counts) + i for i in range(len(joint))},
            compiler_params=params,
            cost_estimate=cheap,
            name="attention",
        )(place, *inputs, *joint)

    def summed(p):
        far_grad = pl.pallas_call(
            far_sum_kernel,
            in_specs=[in_vmem] * 3,
            out_specs=in_vmem,
            out_shape=jax.ShapeDtypeStruct((2, far_rows, part_width), bf16),
            compiler_params=small,
            cost_estimate=cheap,
            name="far_sum",
        )(far[p], near_back[p], side_back_far[p])
        far_sent.append(far_grad)
        grad_far.append(from_peers(far_grad))

    joint, own, far = (), [], []
    back_far, side_back_far, near_back, side_back_own, far_sent, grad_far = [], [], [], [], [], []
    for p in range(parts):
        back, own_part, far_part, near_grad, *rest = attention(p, joint)
        side_grads, joint = rest[:-3], rest[-3:]
        if p + 1 < parts:
            side_grads, *_ = tie((side_grads, side_far[p + 1], near_far[p + 1], qo_far[p + 1]))
        if p > 0:
            side_grads, side_back_far, back_far = tie(
                (side_grads, side_back_far, back_far)
            )
        own.append(own_part)
        far.append(far_part)
        side_back_far.append(lax.ppermute(side_grads[-1], "ctx", side_pairs))
        near_back.append(lax.ppermute(near_grad, "ctx", near_pairs))
        back_far.append(from_peers(back))
        if p > 0:
            side_back_far[p - 1], _ = tie((side_back_far[p - 1], back_far[p]))
            summed(p - 1)
        if p + 1 < parts:
            side_back_own.append(side_back_far[p])
            continue
        side_grad_own, _ = tie((side_grads[0], side_back_far[p]))
        side_back_own.append(lax.ppermute(side_grad_own, "ctx", side_pairs))
    mixed, query_grad, sums = joint

    def shifted(array, step):
        return lax.ppermute(array, "ctx", [(i, i ^ step) for i in range(ctx_count)])

    def rounds(steps, sums):
        for one, two in zip(steps[::2], [*steps[1::2], None]):
            if two is None:
                sums = sums + shifted(sums, one)
                continue
            across = [shifted(sums, step) for step in (one, two, one ^ two)]
            sums = (sums + across[0]) + (across[1] + across[2])
        return sums

    bits = [1 << n for n in range(ctx_count.bit_length() - 1)]
    sums = rounds(bits[:1], rounds(bits[2:], sums))
    side_back_far, sums, back_far, grad_far = tie((side_back_far, sums, back_far, grad_far))
    summed(parts - 1)

    def to_all(before, after, sums):
        slabs = [rounds(before, sums)]
        for step in (1 << n for n in range(groups.bit_length() - 1)):
            pairs = [(i, i ^ step) for i in range(groups)]
            slabs = slabs + [lax.ppermute(slab, "head", pairs) for slab in slabs]
        return [rounds(after, slab) for slab in slabs]

    sums, _ = tie((sums, far_sent[-1]))
    slabs = to_all(bits[1:2], [], sums)
    results = [mixed, query_grad]
    struct = jax.ShapeDtypeStruct
    for p in range(parts):
        gate = p + 1 == parts
        operands = [own[p], near_back[p], side_back_own[p], *back_far[p], *grad_far[p]]
        if gate:
            operands += [noise_level.reshape(1, span_total), *slabs]
        scratch = [pltpu.VMEM((2, rows, part_width), bf16)]
        if gate:
            scratch.append(pltpu.VMEM((level_count, full_width), f32))
        scratch.append(pltpu.SemaphoreType.DMA((4 * groups - 2 + groups,)))
        results = pl.pallas_call(
            functools.partial(finish_kernel, groups=groups, parts=parts, p=p, gate=gate),
            grid_spec=pltpu.PrefetchScalarGridSpec(
                num_scalar_prefetch=1,
                in_specs=[in_vmem] * len(operands) + [anywhere] * len(results),
                out_specs=[anywhere] * (4 + gate),
                scratch_shapes=scratch,
            ),
            out_shape=[struct((rows, full_width), bf16)] * 4
            + [struct((level_count, full_width), f32)] * gate,
            input_output_aliases={1 + len(operands) + i: i for i in range(len(results))},
            compiler_params=small,
            cost_estimate=cheap,
            name="finish",
        )(place, *operands, *results)
    return tuple(results)


def solution(mesh):
    sharded = P(("ctx", "head"), None)
    return jax.shard_map(
        per_device,
        mesh=mesh,
        in_specs=(sharded,) * 4 + (P(),) * 4,
        out_specs=(sharded,) * 4 + (P(),),
        check_vma=False,
    )
```

```python
import functools
import math

import jax
import jax.numpy as jnp
from jax import lax
from jax.experimental import pallas as pl
from jax.experimental.pallas import tpu as pltpu
from jax.sharding import PartitionSpec as P

DH = 128
HIDDEN = -1e30
LOG2E = 1.4426950408889634


def other_ctx(c, near):
    odd = lax.rem(c, 2)
    return c + 1 - 2 * odd if near else c - 1 + 2 * odd


def prep_kernel(
    place_ref, span_ref, noise_ref, mask_ref, table_ref, bias_ref, gate_ref, slot_ref, *, sizes
):
    ctx_count, groups, rows, span_total, level_count, by_span = sizes
    c, h = lax.div(place_ref[0], groups), lax.rem(place_ref[0], groups)
    tokens = groups * rows
    total = ctx_count * tokens
    bf16, f32 = jnp.bfloat16, jnp.float32

    def block_of(ctx, k):
        return ctx * groups + lax.rem(h - k + groups, groups)

    def spans_of(ctx, k):
        at = jnp.clip(ctx, 0, ctx_count - 1)
        return span_ref[pl.ds(block_of(at, k), 1), :]

    def as_column(row):
        return jnp.broadcast_to(row.astype(f32), (rows, rows)).T[:, :1].astype(jnp.int32)

    across = lax.broadcasted_iota(jnp.int32, (1, rows), 1)
    down = lax.broadcasted_iota(jnp.int32, (rows, 1), 0)
    span_lane = lax.broadcasted_iota(jnp.int32, (rows, span_total), 1)
    span_down = lax.broadcasted_iota(jnp.int32, (span_total, rows), 0)
    level_lane = lax.broadcasted_iota(jnp.int32, (rows, level_count), 1)
    query_span = [spans_of(c, k) for k in range(groups)]
    query_pos = [block_of(c, k) * rows + across for k in range(groups)]
    mask_low = mask_ref[...].astype(bf16)
    allowed_q = [
        lax.dot_general(
            mask_low,
            (span_down == row).astype(bf16),
            (((0,), (0,)), ((), ())),
            preferred_element_type=f32,
        ).astype(bf16)
        for row in query_span
    ]
    noise = noise_ref[...].astype(f32)
    for i, ctx in enumerate((c, other_ctx(c, True), other_ctx(c, False))):
        for k in range(groups):
            key_span = as_column(spans_of(ctx, k))
            key_pos = block_of(ctx, k) * rows + down
            valid = (key_pos >= 0) & (key_pos < total)
            onehot = key_span == span_lane
            at = slice((i * groups + k) * rows, (i * groups + k + 1) * rows)
            for p in range(groups):
                allowed = jnp.dot(
                    onehot.astype(bf16), allowed_q[p], preferred_element_type=f32
                )
                visible = (
                    (allowed > 0.5)
                    & (key_span <= query_span[p])
                    & (query_pos[p] - key_pos < tokens)
                    & valid
                )
                bias_ref[at, p * rows : (p + 1) * rows] = jnp.where(visible, 0.0, HIDDEN)
            if i > 0:
                continue
            level = jnp.sum(jnp.where(onehot, noise, 0.0), axis=1, keepdims=True)
            level_onehot = (level.astype(jnp.int32) == level_lane).astype(f32)
            gate_ref[at, :] = jnp.dot(
                level_onehot,
                table_ref[...],
                precision=lax.Precision.HIGHEST,
                preferred_element_type=f32,
            )
            if by_span:
                slot_ref[:, at] = (span_down == query_span[k]).astype(bf16)
            else:
                slot_ref[:, at] = level_onehot.T.astype(bf16)


def attention_kernel(
    place_ref,
    qo_own_ref, kv_own_ref, qo_ref, kv_ref,
    near_own_ref, near_far_ref, side_own_ref, side_far_ref,
    gate_ref, bias_ref, slot_ref,
    *rest, rows, tokens, q_size, heads, apart,
):
    back_ref, own_ref, far_ref, near_grad_ref, *side_grad_refs = rest[-8 - apart : -3]
    mixed_ref, dq_ref, sums_ref = rest[-3:]
    scale = 1.0 / math.sqrt(DH)
    bf16, f32 = jnp.bfloat16, jnp.float32
    tile = 32

    def dot(left, right, left_dim, right_dim):
        return lax.dot_general(
            left, right, (((left_dim,), (right_dim,)), ((), ())), preferred_element_type=f32
        )

    def load(j):
        at = slice(j * DH, (j + 1) * DH)
        keys, values = [], []
        for ref in (
            kv_own_ref, kv_ref, near_own_ref, near_far_ref, side_own_ref, side_far_ref
        ):
            keys.append(ref[0, :, at])
            values.append(ref[1, :, at])
        keys, values = jnp.concatenate(keys, axis=0), jnp.concatenate(values, axis=0)
        queries = jnp.concatenate([qo_own_ref[0, :, at], qo_ref[0, :, at]], axis=0)
        cotangent = jnp.concatenate([qo_own_ref[1, :, at], qo_ref[1, :, at]], axis=0)
        blocks = []
        for start in range(0, tokens, q_size):
            span = slice(start, start + q_size)
            q, o = queries[span], cotangent[span].astype(f32)
            gate = gate_ref[span, at]
            g = (gate * o).astype(bf16)
            blocks.append((q, o, gate, g, dot(keys, q, 1, 1), dot(values, g, 1, 1)))
        return keys, values, blocks

    def work(j, keys, values, blocks):
        at = slice(j * DH, (j + 1) * DH)
        keys_t, values_t = keys.T, values.T
        key_grad = value_grad = sums = None
        for number, (q, o, gate, g, scores, prob_grad) in enumerate(blocks):
            start = number * q_size
            span = slice(start, start + q_size)
            count = scores.shape[0]
            tiles = [slice(r, r + tile) for r in range(0, count, tile)]
            raised, top = [], None
            for t in tiles:
                part = scores[t] * (scale * LOG2E) + bias_ref[t, span]
                raised.append(part)
                high = jnp.max(part.reshape(tile // 8, 8, q_size), axis=0)
                top = high if top is None else jnp.maximum(top, high)
            top = jnp.max(top, axis=0, keepdims=True)
            total = None
            for i in range(len(tiles)):
                raised[i] = jnp.exp2(raised[i] - top)
                part = jnp.sum(raised[i].reshape(tile // 8, 8, q_size), axis=0)
                total = part if total is None else total + part
            inverse = 1.0 / jnp.sum(total, axis=0, keepdims=True)
            low = jnp.concatenate([(part * inverse).astype(bf16) for part in raised], axis=0)
            attended_t = dot(values_t, low, 1, 0).astype(bf16)
            row_dot = jnp.sum(g.T.astype(f32) * attended_t.astype(f32), axis=0, keepdims=True)
            attended = attended_t.T.astype(f32)
            score_grad = jnp.concatenate(
                [
                    (part * ((prob_grad[t] - row_dot) * inverse)).astype(bf16)
                    for part, t in zip(raised, tiles)
                ],
                axis=0,
            )
            query_grad = (dot(keys_t, score_grad, 1, 0) * scale).astype(bf16).T
            mixed = (gate * attended).astype(bf16)
            if start == 0:
                mixed_ref[:, at] = mixed[:rows]
                dq_ref[:, at] = query_grad[:rows]
                back_ref[0, : q_size - rows, at] = mixed[rows:]
                back_ref[1, : q_size - rows, at] = query_grad[rows:]
            else:
                back_ref[0, start - rows : start - rows + q_size, at] = mixed
                back_ref[1, start - rows : start - rows + q_size, at] = query_grad
            dk, dv = dot(score_grad, q, 1, 0), dot(low, g, 1, 0)
            part = dot(slot_ref[:, span], (o * attended).astype(bf16), 1, 0)
            key_grad = dk if key_grad is None else key_grad + dk
            value_grad = dv if value_grad is None else value_grad + dv
            sums = part if sums is None else sums + part
        sums_ref[:, at] = sums.astype(bf16)
        for i, grad in ((0, key_grad * scale), (1, value_grad)):
            own_ref[i, :, at] = grad[:rows]
            far_ref[i, :, at] = grad[rows:tokens]
            low = grad[tokens:].astype(bf16)
            near_grad_ref[i, :, at] = low[:tokens]
            if apart:
                side_grad_refs[0][i, :, at] = low[tokens : tokens + rows]
                side_grad_refs[1][i, :, at] = low[tokens + rows :]
            else:
                side_grad_refs[0][i, :, at] = low[tokens:]

    ready = load(0)
    for j in range(heads):
        following = load(j + 1) if j + 1 < heads else None
        work(j, *ready)
        ready = following


def pack_kernel(place_ref, first_ref, second_ref, own_ref, *rest, groups):
    *far_refs, sems = rest
    rows, width = own_ref.shape[1:]
    copies = []

    def copy(ref, start, to):
        cols = pl.ds(pl.multiple_of(start, DH), to.shape[1])
        copies.append(pltpu.make_async_copy(ref.at[:, cols], to, sems.at[len(copies)]))
        copies[-1].start()

    for k in (*range(1, groups), 0):
        start = lax.rem(place_ref[0] + k, groups) * width
        for i, ref in enumerate((first_ref, second_ref)):
            if k == 0:
                copy(ref, start, own_ref.at[i])
                continue
            for p, far_ref in enumerate(far_refs):
                at = pl.ds((k - 1) * rows, rows)
                copy(ref, start + p * far_ref.shape[2], far_ref.at[i, at])
    for one in copies:
        one.wait()


def far_sum_kernel(part_ref, near_ref, side_ref, out_ref):
    far = slice(near_ref.shape[1] - part_ref.shape[1], None)
    total = part_ref[...] + near_ref[:, far].astype(jnp.float32)
    side = side_ref[:, side_ref.shape[1] - part_ref.shape[1] :].astype(jnp.float32)
    out_ref[...] = (total + side).astype(out_ref.dtype)


def finish_kernel(place_ref, part_ref, near_ref, side_ref, *refs, groups, parts, p, gate):
    slabs, refs = refs[: 2 * (groups - 1)], refs[2 * (groups - 1) :]
    slot_refs = refs[1 : 1 + groups] if gate else ()
    scratch = 3 if gate else 2
    total_ref, *gate_scratch, sems = refs[-scratch:]
    outs = refs[-scratch - (5 if gate else 4) : -scratch]
    part_width = part_ref.shape[2]
    width = part_width * parts
    copies = []

    def send(source, to):
        copies.append(pltpu.make_async_copy(source, to, sems.at[len(copies)]))
        copies[-1].start()

    def place_slab(slab, first, second, k):
        start = lax.rem(place_ref[0] + k, groups) * width + p * part_width
        cols = pl.ds(pl.multiple_of(start, DH), part_width)
        for i, ref in enumerate((first, second)):
            send(slab.at[i], ref.at[:, cols])

    for k in range(1, groups):
        place_slab(slabs[k - 1], outs[0], outs[1], k)
        place_slab(slabs[groups + k - 2], outs[2], outs[3], k)
    near, side = (ref[:, : part_ref.shape[1]].astype(jnp.float32) for ref in (near_ref, side_ref))
    total_ref[...] = (part_ref[...] + near + side).astype(total_ref.dtype)
    place_slab(total_ref, outs[2], outs[3], 0)
    if gate:
        noise_ref, gate_ref = refs[0], gate_scratch[0]
        by_span = noise_ref.shape[1] == slot_refs[0].shape[0]
        levels = lax.broadcasted_iota(jnp.int32, (gate_ref.shape[0], noise_ref.shape[1]), 0)
        onehot = (levels == noise_ref[...]).astype(jnp.bfloat16)
        for j, ref in enumerate(slot_refs):
            if by_span:
                sums = jnp.dot(onehot, ref[...], preferred_element_type=jnp.float32)
            else:
                sums = ref[...].astype(jnp.float32)
            start = lax.bitwise_xor(lax.rem(place_ref[0], groups), j) * width
            cols = pl.ds(pl.multiple_of(start, DH), width)
            gate_ref[:, cols] = sums
            send(gate_ref.at[:, cols], outs[4].at[:, cols])
    for one in copies:
        one.wait()


def per_device(
    queries, key_rows, value_rows, out_cotangent, gate_table, span_ids, noise_level, block_mask
):
    groups = lax.axis_size("head")
    ctx_count = lax.axis_size("ctx")
    rows, full_width = queries.shape
    width = full_width // groups
    heads = width // DH
    tokens = rows * groups
    far_rows = tokens - rows
    parts = 2 if heads % 2 == 0 else 1
    part_width = width // parts
    part_heads = heads // parts
    span_total = noise_level.shape[0]
    level_count = gate_table.shape[0]
    by_span = span_total <= level_count // 2
    slots = span_total if by_span else level_count
    c = lax.axis_index("ctx")
    h = lax.axis_index("head")
    place = (c * groups + h).astype(jnp.int32).reshape(1)
    head_at = lambda place: lax.rem(place[0], groups)
    bf16, f32 = jnp.bfloat16, jnp.float32
    tie = lax.optimization_barrier

    near_pairs = [(i, i ^ 1) for i in range(ctx_count)]
    side_of = [i - 1 + 2 * (i % 2) for i in range(ctx_count)]
    side_pairs = [(i, j if 0 <= j < ctx_count else i) for i, j in enumerate(side_of)]

    whole = lambda shape: pl.BlockSpec(shape, lambda i, place: (0,) * len(shape))
    limit = (26 if tokens <= 256 else 56) * 1024 * 1024
    params = pltpu.CompilerParams(vmem_limit_bytes=limit)
    alone = pltpu.CompilerParams(vmem_limit_bytes=56 * 1024 * 1024)
    cheap = pl.CostEstimate(flops=1, bytes_accessed=1, transcendentals=0)
    in_vmem = pl.BlockSpec(memory_space=pltpu.VMEM)
    anywhere = pl.BlockSpec(memory_space=pl.ANY)
    small = pltpu.CompilerParams(vmem_limit_bytes=(12 if tokens <= 256 else 36) * 1024 * 1024)

    def pack(first, second, params):
        far_shape = (2, far_rows, part_width)
        return pl.pallas_call(
            functools.partial(pack_kernel, groups=groups),
            grid_spec=pltpu.PrefetchScalarGridSpec(
                num_scalar_prefetch=1,
                in_specs=[anywhere] * 2,
                out_specs=[in_vmem] * (1 + parts),
                scratch_shapes=[pltpu.SemaphoreType.DMA((2 + 2 * (groups - 1) * parts,))],
            ),
            out_shape=[jax.ShapeDtypeStruct((2, rows, width), bf16)]
            + [jax.ShapeDtypeStruct(far_shape, bf16)] * parts,
            compiler_params=params,
            cost_estimate=cheap,
            name="pack",
        )(place, first, second)

    def to_peers(slab):
        arrived = []
        for k in range(1, groups):
            part = slab if groups == 2 else slab[:, (k - 1) * rows : k * rows]
            pairs = [(i, (i + k) % groups) for i in range(groups)]
            arrived.append(lax.ppermute(part, "head", pairs))
        return arrived[0] if groups == 2 else jnp.concatenate(arrived, axis=1)

    def from_peers(slab):
        arrived = []
        for k in range(1, groups):
            part = slab if groups == 2 else slab[:, (k - 1) * rows : k * rows]
            pairs = [(i, (i - k) % groups) for i in range(groups)]
            arrived.append(lax.ppermute(part, "head", pairs))
        return arrived

    kv_own, *kv_sent = pack(key_rows, value_rows, alone)
    qo_own, *qo_sent = pack(queries, out_cotangent, small)
    side_own = lax.ppermute(kv_own, "ctx", side_pairs)
    near_own = lax.ppermute(kv_own, "ctx", near_pairs)
    kv_far = [to_peers(slab) for slab in kv_sent]
    side_far = [lax.ppermute(slab, "ctx", side_pairs) for slab in kv_far]
    near_far = [lax.ppermute(slab, "ctx", near_pairs) for slab in kv_far]
    qo_far = [
        to_peers(tie((slab, *done))[0])
        for slab, done in zip(qo_sent, (kv_far[:1], (*kv_far[1:], side_own, near_own)))
    ]

    sizes = (ctx_count, groups, rows, span_total, level_count, by_span)
    whole = lambda shape: pl.BlockSpec(shape, lambda i, place: (0,) * len(shape))
    bias, gate, slot = pl.pallas_call(
        functools.partial(prep_kernel, sizes=sizes),
        grid_spec=pltpu.PrefetchScalarGridSpec(
            num_scalar_prefetch=1,
            grid=(1,),
            in_specs=[
                whole((ctx_count * groups, rows)),
                whole((1, span_total)),
                whole((span_total, span_total)),
                pl.BlockSpec((level_count, width), lambda i, place: (0, head_at(place))),
            ],
            out_specs=[
                whole((3 * tokens, tokens)),
                whole((tokens, width)),
                whole((slots, tokens)),
            ],
        ),
        out_shape=[
            jax.ShapeDtypeStruct((3 * tokens, tokens), f32),
            jax.ShapeDtypeStruct((tokens, width), f32),
            jax.ShapeDtypeStruct((slots, tokens), bf16),
        ],
        compiler_params=small,
        cost_estimate=cheap,
        name="prep",
    )(
        place,
        span_ids.reshape(ctx_count * groups, rows),
        noise_level.reshape(1, span_total),
        block_mask,
        gate_table,
    )

    batch = next(n for n in (3, 2, 1) if part_heads % n == 0) if tokens <= 256 else 1
    steps = part_heads // batch
    block = batch * DH
    q_size = min(256, tokens)

    def attention(p, joint):
        pair = lambda count: pl.BlockSpec((2, count, block), lambda i, place: (0, 0, i))
        at_part = lambda count: pl.BlockSpec(
            (2, count, block), lambda i, place: (0, 0, p * steps + i)
        )
        at_head = pl.BlockSpec(
            (rows, block), lambda i, place: (0, (head_at(place) * parts + p) * steps + i)
        )
        column = lambda count: pl.BlockSpec((count, block), lambda i, place: (0, p * steps + i))
        struct = jax.ShapeDtypeStruct
        side_counts = (rows, far_rows) if p + 1 == parts else (tokens,)
        inputs = [
            qo_own, kv_own, qo_far[p], kv_far[p],
            near_own, near_far[p], side_own, side_far[p],
            gate, bias, slot,
        ]
        return pl.pallas_call(
            functools.partial(
                attention_kernel,
                rows=rows, tokens=tokens, q_size=q_size, heads=batch, apart=p + 1 == parts,
            ),
            grid_spec=pltpu.PrefetchScalarGridSpec(
                num_scalar_prefetch=1,
                grid=(steps,),
                in_specs=[
                    at_part(rows), at_part(rows), pair(far_rows), pair(far_rows),
                    at_part(rows), pair(far_rows), at_part(rows), pair(far_rows),
                    column(tokens), whole((3 * tokens, tokens)), whole((slots, tokens)),
                ]
                + [pl.BlockSpec(memory_space=pl.ANY)] * len(joint),
                out_specs=[
                    pair(far_rows), pair(rows), pair(far_rows), pair(tokens),
                    *[pair(count) for count in side_counts],
                    at_head, at_head, column(slots),
                ],
            ),
            out_shape=[
                struct((2, far_rows, part_width), bf16),
                struct((2, rows, part_width), f32),
                struct((2, far_rows, part_width), f32),
                struct((2, tokens, part_width), bf16),
                *[struct((2, count, part_width), bf16) for count in side_counts],
                struct((rows, full_width), bf16),
                struct((rows, full_width), bf16),
                struct((slots, width), bf16),
            ],
            input_output_aliases={1 + len(inputs) + i: 4 + len(side_counts) + i for i in range(len(joint))},
            compiler_params=params,
            cost_estimate=cheap,
            name="attention",
        )(place, *inputs, *joint)

    def shifted(array, step):
        return lax.ppermute(array, "ctx", [(i, i ^ step) for i in range(ctx_count)])

    def rounds(steps, sums):
        for one, two in zip(steps[::2], [*steps[1::2], None]):
            if two is None:
                sums = sums + shifted(sums, one)
                continue
            across = [shifted(sums, step) for step in (one, two, one ^ two)]
            sums = (sums + across[0]) + (across[1] + across[2])
        return sums

    bits = [1 << n for n in range(ctx_count.bit_length() - 1)]
    def summed(p):
        far_grad = pl.pallas_call(
            far_sum_kernel,
            in_specs=[in_vmem] * 3,
            out_specs=in_vmem,
            out_shape=jax.ShapeDtypeStruct((2, far_rows, part_width), bf16),
            compiler_params=small,
            cost_estimate=cheap,
            name="far_sum",
        )(far[p], near_back[p], side_back_far[p])
        far_sent.append(far_grad)
        grad_far.append(from_peers(far_grad))

    joint, own, far = (), [], []
    back_far, side_back_far, near_back, side_back_own, far_sent, grad_far = [], [], [], [], [], []
    for p in range(parts):
        back, own_part, far_part, near_grad, *rest = attention(p, joint)
        side_grads, joint = rest[:-3], rest[-3:]
        if p + 1 < parts:
            side_grads, *_ = tie((side_grads, side_far[p + 1], near_far[p + 1], qo_far[p + 1]))
        if p > 0:
            side_grads, side_back_far = tie(
                (side_grads, side_back_far)
            )
            joint, back_far = tie((joint, back_far))
        own.append(own_part)
        far.append(far_part)
        side_back_far.append(lax.ppermute(side_grads[-1], "ctx", side_pairs))
        near_back.append(lax.ppermute(near_grad, "ctx", near_pairs))
        back_far.append(from_peers(back))
        if p > 0:
            sums = rounds(bits[2:], joint[2])
            side_back_far[p - 1], sums, _ = tie((side_back_far[p - 1], sums, back_far[p]))
            summed(p - 1)
        if p + 1 < parts:
            side_back_own.append(side_back_far[p])
            continue
        side_grad_own, _ = tie((side_grads[0], side_back_far[p]))
        side_back_own.append(lax.ppermute(side_grad_own, "ctx", side_pairs))
    mixed, query_grad = joint[:2]
    if parts == 1:
        sums = rounds(bits[2:], joint[2])

    sums = rounds(bits[:1], sums)
    side_back_far, sums, back_far, grad_far = tie((side_back_far, sums, back_far, grad_far))
    summed(parts - 1)

    def to_all(before, after, sums):
        slabs = [rounds(before, sums)]
        for step in (1 << n for n in range(groups.bit_length() - 1)):
            pairs = [(i, i ^ step) for i in range(groups)]
            slabs = slabs + [lax.ppermute(slab, "head", pairs) for slab in slabs]
        return [rounds(after, slab) for slab in slabs]

    sums, _ = tie((sums, far_sent[-1]))
    slabs = to_all(bits[1:2], [], sums)
    results = [mixed, query_grad]
    struct = jax.ShapeDtypeStruct
    for p in range(parts):
        gate = p + 1 == parts
        operands = [own[p], near_back[p], side_back_own[p], *back_far[p], *grad_far[p]]
        if gate:
            operands += [noise_level.reshape(1, span_total), *slabs]
        scratch = [pltpu.VMEM((2, rows, part_width), bf16)]
        if gate:
            scratch.append(pltpu.VMEM((level_count, full_width), f32))
        scratch.append(pltpu.SemaphoreType.DMA((4 * groups - 2 + groups,)))
        results = pl.pallas_call(
            functools.partial(finish_kernel, groups=groups, parts=parts, p=p, gate=gate),
            grid_spec=pltpu.PrefetchScalarGridSpec(
                num_scalar_prefetch=1,
                in_specs=[in_vmem] * len(operands) + [anywhere] * len(results),
                out_specs=[anywhere] * (4 + gate),
                scratch_shapes=scratch,
            ),
            out_shape=[struct((rows, full_width), bf16)] * 4
            + [struct((level_count, full_width), f32)] * gate,
            input_output_aliases={1 + len(operands) + i: i for i in range(len(results))},
            compiler_params=small,
            cost_estimate=cheap,
            name="finish",
        )(place, *operands, *results)
    return tuple(results)


def solution(mesh):
    sharded = P(("ctx", "head"), None)
    return jax.shard_map(
        per_device,
        mesh=mesh,
        in_specs=(sharded,) * 4 + (P(),) * 4,
        out_specs=(sharded,) * 4 + (P(),),
        check_vma=False,
    )
```

```python
import functools
import math

import jax
import jax.numpy as jnp
from jax import lax
from jax.experimental import pallas as pl
from jax.experimental.pallas import tpu as pltpu
from jax.sharding import PartitionSpec as P

DH = 128
HIDDEN = -1e30
LOG2E = 1.4426950408889634


def other_ctx(c, near):
    odd = lax.rem(c, 2)
    return c + 1 - 2 * odd if near else c - 1 + 2 * odd


def prep_kernel(
    place_ref, span_ref, noise_ref, mask_ref, table_ref, bias_ref, gate_ref, slot_ref, *, sizes
):
    ctx_count, groups, rows, span_total, level_count, by_span = sizes
    c, h = lax.div(place_ref[0], groups), lax.rem(place_ref[0], groups)
    tokens = groups * rows
    total = ctx_count * tokens
    bf16, f32 = jnp.bfloat16, jnp.float32

    def block_of(ctx, k):
        return ctx * groups + lax.rem(h - k + groups, groups)

    def spans_of(ctx, k):
        at = jnp.clip(ctx, 0, ctx_count - 1)
        return span_ref[pl.ds(block_of(at, k), 1), :]

    def as_column(row):
        return jnp.broadcast_to(row.astype(f32), (rows, rows)).T[:, :1].astype(jnp.int32)

    across = lax.broadcasted_iota(jnp.int32, (1, rows), 1)
    down = lax.broadcasted_iota(jnp.int32, (rows, 1), 0)
    span_lane = lax.broadcasted_iota(jnp.int32, (rows, span_total), 1)
    span_down = lax.broadcasted_iota(jnp.int32, (span_total, rows), 0)
    level_lane = lax.broadcasted_iota(jnp.int32, (rows, level_count), 1)
    query_span = [spans_of(c, k) for k in range(groups)]
    query_pos = [block_of(c, k) * rows + across for k in range(groups)]
    mask_low = mask_ref[...].astype(bf16)
    allowed_q = [
        lax.dot_general(
            mask_low,
            (span_down == row).astype(bf16),
            (((0,), (0,)), ((), ())),
            preferred_element_type=f32,
        ).astype(bf16)
        for row in query_span
    ]
    noise = noise_ref[...].astype(f32)
    for i, ctx in enumerate((c, other_ctx(c, True), other_ctx(c, False))):
        for k in range(groups):
            key_span = as_column(spans_of(ctx, k))
            key_pos = block_of(ctx, k) * rows + down
            valid = (key_pos >= 0) & (key_pos < total)
            onehot = key_span == span_lane
            at = slice((i * groups + k) * rows, (i * groups + k + 1) * rows)
            for p in range(groups):
                allowed = jnp.dot(
                    onehot.astype(bf16), allowed_q[p], preferred_element_type=f32
                )
                visible = (
                    (allowed > 0.5)
                    & (key_span <= query_span[p])
                    & (query_pos[p] - key_pos < tokens)
                    & valid
                )
                bias_ref[at, p * rows : (p + 1) * rows] = jnp.where(visible, 0.0, HIDDEN)
            if i > 0:
                continue
            level = jnp.sum(jnp.where(onehot, noise, 0.0), axis=1, keepdims=True)
            level_onehot = (level.astype(jnp.int32) == level_lane).astype(f32)
            gate_ref[at, :] = jnp.dot(
                level_onehot,
                table_ref[...],
                precision=lax.Precision.HIGHEST,
                preferred_element_type=f32,
            )
            if by_span:
                slot_ref[:, at] = (span_down == query_span[k]).astype(bf16)
            else:
                slot_ref[:, at] = level_onehot.T.astype(bf16)


def attention_kernel(
    place_ref,
    qo_own_ref, kv_own_ref, qo_ref, kv_ref,
    near_own_ref, near_far_ref, side_own_ref, side_far_ref,
    gate_ref, bias_ref, slot_ref,
    *rest, rows, tokens, q_size, heads, apart,
):
    back_ref, own_ref, far_ref, near_grad_ref, *side_grad_refs = rest[-8 - apart : -3]
    mixed_ref, dq_ref, sums_ref = rest[-3:]
    scale = 1.0 / math.sqrt(DH)
    bf16, f32 = jnp.bfloat16, jnp.float32
    tile = 32

    def dot(left, right, left_dim, right_dim):
        return lax.dot_general(
            left, right, (((left_dim,), (right_dim,)), ((), ())), preferred_element_type=f32
        )

    def load(j):
        at = slice(j * DH, (j + 1) * DH)
        keys, values = [], []
        for ref in (
            kv_own_ref, kv_ref, near_own_ref, near_far_ref, side_own_ref, side_far_ref
        ):
            keys.append(ref[0, :, at])
            values.append(ref[1, :, at])
        keys, values = jnp.concatenate(keys, axis=0), jnp.concatenate(values, axis=0)
        queries = jnp.concatenate([qo_own_ref[0, :, at], qo_ref[0, :, at]], axis=0)
        cotangent = jnp.concatenate([qo_own_ref[1, :, at], qo_ref[1, :, at]], axis=0)
        blocks = []
        for start in range(0, tokens, q_size):
            span = slice(start, start + q_size)
            q, o = queries[span], cotangent[span].astype(f32)
            gate = gate_ref[span, at]
            g = (gate * o).astype(bf16)
            blocks.append((q, o, gate, g, dot(keys, q, 1, 1), dot(values, g, 1, 1)))
        return keys, values, blocks

    def work(j, keys, values, blocks):
        at = slice(j * DH, (j + 1) * DH)
        keys_t, values_t = keys.T, values.T
        key_grad = value_grad = sums = None
        for number, (q, o, gate, g, scores, prob_grad) in enumerate(blocks):
            start = number * q_size
            span = slice(start, start + q_size)
            count = scores.shape[0]
            tiles = [slice(r, r + tile) for r in range(0, count, tile)]
            raised, top = [], None
            for t in tiles:
                part = scores[t] * (scale * LOG2E) + bias_ref[t, span]
                raised.append(part)
                high = jnp.max(part.reshape(tile // 8, 8, q_size), axis=0)
                top = high if top is None else jnp.maximum(top, high)
            top = jnp.max(top, axis=0, keepdims=True)
            total = None
            for i in range(len(tiles)):
                raised[i] = jnp.exp2(raised[i] - top)
                part = jnp.sum(raised[i].reshape(tile // 8, 8, q_size), axis=0)
                total = part if total is None else total + part
            inverse = 1.0 / jnp.sum(total, axis=0, keepdims=True)
            low = jnp.concatenate([(part * inverse).astype(bf16) for part in raised], axis=0)
            attended_t = dot(values_t, low, 1, 0).astype(bf16)
            row_dot = jnp.sum(g.T.astype(f32) * attended_t.astype(f32), axis=0, keepdims=True)
            attended = attended_t.T.astype(f32)
            score_grad = jnp.concatenate(
                [
                    (part * ((prob_grad[t] - row_dot) * inverse)).astype(bf16)
                    for part, t in zip(raised, tiles)
                ],
                axis=0,
            )
            query_grad = (dot(keys_t, score_grad, 1, 0) * scale).astype(bf16).T
            mixed = (gate * attended).astype(bf16)
            if start == 0:
                mixed_ref[:, at] = mixed[:rows]
                dq_ref[:, at] = query_grad[:rows]
                back_ref[0, : q_size - rows, at] = mixed[rows:]
                back_ref[1, : q_size - rows, at] = query_grad[rows:]
            else:
                back_ref[0, start - rows : start - rows + q_size, at] = mixed
                back_ref[1, start - rows : start - rows + q_size, at] = query_grad
            dk, dv = dot(score_grad, q, 1, 0), dot(low, g, 1, 0)
            part = dot(slot_ref[:, span], (o * attended).astype(bf16), 1, 0)
            key_grad = dk if key_grad is None else key_grad + dk
            value_grad = dv if value_grad is None else value_grad + dv
            sums = part if sums is None else sums + part
        sums_ref[:, at] = sums.astype(bf16)
        for i, grad in ((0, key_grad * scale), (1, value_grad)):
            own_ref[i, :, at] = grad[:rows]
            far_ref[i, :, at] = grad[rows:tokens]
            low = grad[tokens:].astype(bf16)
            near_grad_ref[i, :, at] = low[:tokens]
            if apart:
                side_grad_refs[0][i, :, at] = low[tokens : tokens + rows]
                side_grad_refs[1][i, :, at] = low[tokens + rows :]
            else:
                side_grad_refs[0][i, :, at] = low[tokens:]

    ready = load(0)
    for j in range(heads):
        following = load(j + 1) if j + 1 < heads else None
        work(j, *ready)
        ready = following


def pack_kernel(place_ref, first_ref, second_ref, own_ref, *rest, groups):
    *far_refs, sems = rest
    rows, width = own_ref.shape[1:]
    copies = []

    def copy(ref, start, to):
        cols = pl.ds(pl.multiple_of(start, DH), to.shape[1])
        copies.append(pltpu.make_async_copy(ref.at[:, cols], to, sems.at[len(copies)]))
        copies[-1].start()

    for k in (*range(1, groups), 0):
        start = lax.rem(place_ref[0] + k, groups) * width
        for i, ref in enumerate((first_ref, second_ref)):
            if k == 0:
                copy(ref, start, own_ref.at[i])
                continue
            for p, far_ref in enumerate(far_refs):
                at = pl.ds((k - 1) * rows, rows)
                copy(ref, start + p * far_ref.shape[2], far_ref.at[i, at])
    for one in copies:
        one.wait()


def far_sum_kernel(part_ref, near_ref, side_ref, out_ref):
    far = slice(near_ref.shape[1] - part_ref.shape[1], None)
    total = part_ref[...] + near_ref[:, far].astype(jnp.float32)
    side = side_ref[:, side_ref.shape[1] - part_ref.shape[1] :].astype(jnp.float32)
    out_ref[...] = (total + side).astype(out_ref.dtype)


def finish_kernel(place_ref, part_ref, near_ref, side_ref, *refs, groups, parts, p, gate):
    slabs, refs = refs[: 2 * (groups - 1)], refs[2 * (groups - 1) :]
    slot_refs = refs[1 : 1 + groups] if gate else ()
    scratch = 3 if gate else 2
    total_ref, *gate_scratch, sems = refs[-scratch:]
    outs = refs[-scratch - (5 if gate else 4) : -scratch]
    part_width = part_ref.shape[2]
    width = part_width * parts
    copies = []

    def send(source, to):
        copies.append(pltpu.make_async_copy(source, to, sems.at[len(copies)]))
        copies[-1].start()

    def place_slab(slab, first, second, k):
        start = lax.rem(place_ref[0] + k, groups) * width + p * part_width
        cols = pl.ds(pl.multiple_of(start, DH), part_width)
        for i, ref in enumerate((first, second)):
            send(slab.at[i], ref.at[:, cols])

    for k in range(1, groups):
        place_slab(slabs[k - 1], outs[0], outs[1], k)
        place_slab(slabs[groups + k - 2], outs[2], outs[3], k)
    near, side = (ref[:, : part_ref.shape[1]].astype(jnp.float32) for ref in (near_ref, side_ref))
    total_ref[...] = (part_ref[...] + near + side).astype(total_ref.dtype)
    place_slab(total_ref, outs[2], outs[3], 0)
    if gate:
        noise_ref, gate_ref = refs[0], gate_scratch[0]
        by_span = noise_ref.shape[1] == slot_refs[0].shape[0]
        levels = lax.broadcasted_iota(jnp.int32, (gate_ref.shape[0], noise_ref.shape[1]), 0)
        onehot = (levels == noise_ref[...]).astype(jnp.bfloat16)
        for j, ref in enumerate(slot_refs):
            if by_span:
                sums = jnp.dot(onehot, ref[...], preferred_element_type=jnp.float32)
            else:
                sums = ref[...].astype(jnp.float32)
            start = lax.bitwise_xor(lax.rem(place_ref[0], groups), j) * width
            cols = pl.ds(pl.multiple_of(start, DH), width)
            gate_ref[:, cols] = sums
            send(gate_ref.at[:, cols], outs[4].at[:, cols])
    for one in copies:
        one.wait()


def per_device(
    queries, key_rows, value_rows, out_cotangent, gate_table, span_ids, noise_level, block_mask
):
    groups = lax.axis_size("head")
    ctx_count = lax.axis_size("ctx")
    rows, full_width = queries.shape
    width = full_width // groups
    heads = width // DH
    tokens = rows * groups
    far_rows = tokens - rows
    parts = 2 if heads % 2 == 0 else 1
    part_width = width // parts
    part_heads = heads // parts
    span_total = noise_level.shape[0]
    level_count = gate_table.shape[0]
    by_span = span_total <= level_count // 2
    slots = span_total if by_span else level_count
    c = lax.axis_index("ctx")
    h = lax.axis_index("head")
    place = (c * groups + h).astype(jnp.int32).reshape(1)
    head_at = lambda place: lax.rem(place[0], groups)
    bf16, f32 = jnp.bfloat16, jnp.float32
    tie = lax.optimization_barrier

    near_pairs = [(i, i ^ 1) for i in range(ctx_count)]
    side_pairs = [(i, (i - 1 + 2 * (i % 2)) % ctx_count) for i in range(ctx_count)]

    whole = lambda shape: pl.BlockSpec(shape, lambda i, place: (0,) * len(shape))
    limit = (26 if tokens <= 256 else 56) * 1024 * 1024
    params = pltpu.CompilerParams(vmem_limit_bytes=limit)
    alone = pltpu.CompilerParams(vmem_limit_bytes=56 * 1024 * 1024)
    cheap = pl.CostEstimate(flops=1, bytes_accessed=1, transcendentals=0)
    in_vmem = pl.BlockSpec(memory_space=pltpu.VMEM)
    anywhere = pl.BlockSpec(memory_space=pl.ANY)
    small = pltpu.CompilerParams(vmem_limit_bytes=(12 if tokens <= 256 else 36) * 1024 * 1024)

    def pack(first, second, params):
        far_shape = (2, far_rows, part_width)
        return pl.pallas_call(
            functools.partial(pack_kernel, groups=groups),
            grid_spec=pltpu.PrefetchScalarGridSpec(
                num_scalar_prefetch=1,
                in_specs=[anywhere] * 2,
                out_specs=[in_vmem] * (1 + parts),
                scratch_shapes=[pltpu.SemaphoreType.DMA((2 + 2 * (groups - 1) * parts,))],
            ),
            out_shape=[jax.ShapeDtypeStruct((2, rows, width), bf16)]
            + [jax.ShapeDtypeStruct(far_shape, bf16)] * parts,
            compiler_params=params,
            cost_estimate=cheap,
            name="pack",
        )(place, first, second)

    def to_peers(slab):
        arrived = []
        for k in range(1, groups):
            part = slab if groups == 2 else slab[:, (k - 1) * rows : k * rows]
            pairs = [(i, (i + k) % groups) for i in range(groups)]
            arrived.append(lax.ppermute(part, "head", pairs))
        return arrived[0] if groups == 2 else jnp.concatenate(arrived, axis=1)

    def from_peers(slab):
        arrived = []
        for k in range(1, groups):
            part = slab if groups == 2 else slab[:, (k - 1) * rows : k * rows]
            pairs = [(i, (i - k) % groups) for i in range(groups)]
            arrived.append(lax.ppermute(part, "head", pairs))
        return arrived

    kv_own, *kv_sent = pack(key_rows, value_rows, alone)
    qo_own, *qo_sent = pack(queries, out_cotangent, small)
    side_own = lax.ppermute(kv_own, "ctx", side_pairs)
    near_own = lax.ppermute(kv_own, "ctx", near_pairs)
    kv_far = [to_peers(slab) for slab in kv_sent]
    side_far = [lax.ppermute(slab, "ctx", side_pairs) for slab in kv_far]
    near_far = [lax.ppermute(slab, "ctx", near_pairs) for slab in kv_far]
    qo_far = [
        to_peers(tie((slab, *done))[0])
        for slab, done in zip(qo_sent, (kv_far[:1], (*kv_far[1:], side_own, near_own)))
    ]

    sizes = (ctx_count, groups, rows, span_total, level_count, by_span)
    whole = lambda shape: pl.BlockSpec(shape, lambda i, place: (0,) * len(shape))
    bias, gate, slot = pl.pallas_call(
        functools.partial(prep_kernel, sizes=sizes),
        grid_spec=pltpu.PrefetchScalarGridSpec(
            num_scalar_prefetch=1,
            grid=(1,),
            in_specs=[
                whole((ctx_count * groups, rows)),
                whole((1, span_total)),
                whole((span_total, span_total)),
                pl.BlockSpec((level_count, width), lambda i, place: (0, head_at(place))),
            ],
            out_specs=[
                whole((3 * tokens, tokens)),
                whole((tokens, width)),
                whole((slots, tokens)),
            ],
        ),
        out_shape=[
            jax.ShapeDtypeStruct((3 * tokens, tokens), f32),
            jax.ShapeDtypeStruct((tokens, width), f32),
            jax.ShapeDtypeStruct((slots, tokens), bf16),
        ],
        compiler_params=small,
        cost_estimate=cheap,
        name="prep",
    )(
        place,
        span_ids.reshape(ctx_count * groups, rows),
        noise_level.reshape(1, span_total),
        block_mask,
        gate_table,
    )

    batch = next(n for n in (3, 2, 1) if part_heads % n == 0) if tokens <= 256 else 1
    steps = part_heads // batch
    block = batch * DH
    q_size = min(256, tokens)

    def attention(p, joint):
        pair = lambda count: pl.BlockSpec((2, count, block), lambda i, place: (0, 0, i))
        at_part = lambda count: pl.BlockSpec(
            (2, count, block), lambda i, place: (0, 0, p * steps + i)
        )
        at_head = pl.BlockSpec(
            (rows, block), lambda i, place: (0, (head_at(place) * parts + p) * steps + i)
        )
        column = lambda count: pl.BlockSpec((count, block), lambda i, place: (0, p * steps + i))
        struct = jax.ShapeDtypeStruct
        side_counts = (rows, far_rows) if p + 1 == parts else (tokens,)
        inputs = [
            qo_own, kv_own, qo_far[p], kv_far[p],
            near_own, near_far[p], side_own, side_far[p],
            gate, bias, slot,
        ]
        return pl.pallas_call(
            functools.partial(
                attention_kernel,
                rows=rows, tokens=tokens, q_size=q_size, heads=batch, apart=p + 1 == parts,
            ),
            grid_spec=pltpu.PrefetchScalarGridSpec(
                num_scalar_prefetch=1,
                grid=(steps,),
                in_specs=[
                    at_part(rows), at_part(rows), pair(far_rows), pair(far_rows),
                    at_part(rows), pair(far_rows), at_part(rows), pair(far_rows),
                    column(tokens), whole((3 * tokens, tokens)), whole((slots, tokens)),
                ]
                + [pl.BlockSpec(memory_space=pl.ANY)] * len(joint),
                out_specs=[
                    pair(far_rows), pair(rows), pair(far_rows), pair(tokens),
                    *[pair(count) for count in side_counts],
                    at_head, at_head, column(slots),
                ],
            ),
            out_shape=[
                struct((2, far_rows, part_width), bf16),
                struct((2, rows, part_width), f32),
                struct((2, far_rows, part_width), f32),
                struct((2, tokens, part_width), bf16),
                *[struct((2, count, part_width), bf16) for count in side_counts],
                struct((rows, full_width), bf16),
                struct((rows, full_width), bf16),
                struct((slots, width), bf16),
            ],
            input_output_aliases={1 + len(inputs) + i: 4 + len(side_counts) + i for i in range(len(joint))},
            compiler_params=params,
            cost_estimate=cheap,
            name="attention",
        )(place, *inputs, *joint)

    def shifted(array, step):
        return lax.ppermute(array, "ctx", [(i, i ^ step) for i in range(ctx_count)])

    def rounds(steps, sums):
        for one, two in zip(steps[::2], [*steps[1::2], None]):
            if two is None:
                sums = sums + shifted(sums, one)
                continue
            across = [shifted(sums, step) for step in (one, two, one ^ two)]
            sums = (sums + across[0]) + (across[1] + across[2])
        return sums

    bits = [1 << n for n in range(ctx_count.bit_length() - 1)]
    def summed(p):
        far_grad = pl.pallas_call(
            far_sum_kernel,
            in_specs=[in_vmem] * 3,
            out_specs=in_vmem,
            out_shape=jax.ShapeDtypeStruct((2, far_rows, part_width), bf16),
            compiler_params=small,
            cost_estimate=cheap,
            name="far_sum",
        )(far[p], near_back[p], side_back_far[p])
        far_sent.append(far_grad)
        grad_far.append(from_peers(far_grad))

    joint, own, far = (), [], []
    back_far, side_back_far, near_back, side_back_own, far_sent, grad_far = [], [], [], [], [], []
    for p in range(parts):
        back, own_part, far_part, near_grad, *rest = attention(p, joint)
        side_grads, joint = rest[:-3], rest[-3:]
        if p + 1 < parts:
            side_grads, *_ = tie((side_grads, side_far[p + 1], near_far[p + 1], qo_far[p + 1]))
        if p > 0:
            side_grads, side_back_far = tie(
                (side_grads, side_back_far)
            )
            joint, back_far = tie((joint, back_far))
        own.append(own_part)
        far.append(far_part)
        side_back_far.append(lax.ppermute(side_grads[-1], "ctx", side_pairs))
        near_back.append(lax.ppermute(near_grad, "ctx", near_pairs))
        back_far.append(from_peers(back))
        if p > 0:
            sums = rounds(bits[2:], joint[2])
            side_back_far[p - 1], sums, _ = tie((side_back_far[p - 1], sums, back_far[p]))
            summed(p - 1)
        if p + 1 < parts:
            side_back_own.append(side_back_far[p])
            continue
        side_grad_own, _ = tie((side_grads[0], side_back_far[p]))
        side_back_own.append(lax.ppermute(side_grad_own, "ctx", side_pairs))
    mixed, query_grad = joint[:2]
    if parts == 1:
        sums = rounds(bits[2:], joint[2])

    sums = rounds(bits[:1], sums)
    side_back_far, sums, back_far, grad_far = tie((side_back_far, sums, back_far, grad_far))
    summed(parts - 1)

    def to_all(before, after, sums):
        slabs = [rounds(before, sums)]
        for step in (1 << n for n in range(groups.bit_length() - 1)):
            pairs = [(i, i ^ step) for i in range(groups)]
            slabs = slabs + [lax.ppermute(slab, "head", pairs) for slab in slabs]
        return [rounds(after, slab) for slab in slabs]

    sums, _ = tie((sums, far_sent[-1]))
    slabs = to_all(bits[1:2], [], sums)
    results = [mixed, query_grad]
    struct = jax.ShapeDtypeStruct
    for p in range(parts):
        gate = p + 1 == parts
        operands = [own[p], near_back[p], side_back_own[p], *back_far[p], *grad_far[p]]
        if gate:
            operands += [noise_level.reshape(1, span_total), *slabs]
        scratch = [pltpu.VMEM((2, rows, part_width), bf16)]
        if gate:
            scratch.append(pltpu.VMEM((level_count, full_width), f32))
        scratch.append(pltpu.SemaphoreType.DMA((4 * groups - 2 + groups,)))
        results = pl.pallas_call(
            functools.partial(finish_kernel, groups=groups, parts=parts, p=p, gate=gate),
            grid_spec=pltpu.PrefetchScalarGridSpec(
                num_scalar_prefetch=1,
                in_specs=[in_vmem] * len(operands) + [anywhere] * len(results),
                out_specs=[anywhere] * (4 + gate),
                scratch_shapes=scratch,
            ),
            out_shape=[struct((rows, full_width), bf16)] * 4
            + [struct((level_count, full_width), f32)] * gate,
            input_output_aliases={1 + len(operands) + i: i for i in range(len(results))},
            compiler_params=small,
            cost_estimate=cheap,
            name="finish",
        )(place, *operands, *results)
    return tuple(results)


def solution(mesh):
    sharded = P(("ctx", "head"), None)
    return jax.shard_map(
        per_device,
        mesh=mesh,
        in_specs=(sharded,) * 4 + (P(),) * 4,
        out_specs=(sharded,) * 4 + (P(),),
        check_vma=False,
    )
```

```python
import functools
import math

import jax
import jax.numpy as jnp
from jax import lax
from jax.experimental import pallas as pl
from jax.experimental.pallas import tpu as pltpu
from jax.sharding import PartitionSpec as P

DH = 128
HIDDEN = -1e30
LOG2E = 1.4426950408889634


def other_ctx(c, near):
    odd = lax.rem(c, 2)
    return c + 1 - 2 * odd if near else c - 1 + 2 * odd


def prep_kernel(
    place_ref, span_ref, noise_ref, mask_ref, table_ref, bias_ref, gate_ref, slot_ref, *, sizes
):
    ctx_count, groups, rows, span_total, level_count, by_span = sizes
    c, h = lax.div(place_ref[0], groups), lax.rem(place_ref[0], groups)
    tokens = groups * rows
    total = ctx_count * tokens
    bf16, f32 = jnp.bfloat16, jnp.float32

    def block_of(ctx, k):
        return ctx * groups + lax.rem(h - k + groups, groups)

    def spans_of(ctx, k):
        at = jnp.clip(ctx, 0, ctx_count - 1)
        return span_ref[pl.ds(block_of(at, k), 1), :]

    def as_column(row):
        return jnp.broadcast_to(row.astype(f32), (rows, rows)).T[:, :1].astype(jnp.int32)

    across = lax.broadcasted_iota(jnp.int32, (1, rows), 1)
    down = lax.broadcasted_iota(jnp.int32, (rows, 1), 0)
    span_lane = lax.broadcasted_iota(jnp.int32, (rows, span_total), 1)
    span_down = lax.broadcasted_iota(jnp.int32, (span_total, rows), 0)
    level_lane = lax.broadcasted_iota(jnp.int32, (rows, level_count), 1)
    query_span = [spans_of(c, k) for k in range(groups)]
    query_pos = [block_of(c, k) * rows + across for k in range(groups)]
    mask_low = mask_ref[...].astype(bf16)
    allowed_q = [
        lax.dot_general(
            mask_low,
            (span_down == row).astype(bf16),
            (((0,), (0,)), ((), ())),
            preferred_element_type=f32,
        ).astype(bf16)
        for row in query_span
    ]
    noise = noise_ref[...].astype(f32)
    for i, ctx in enumerate((c, other_ctx(c, True), other_ctx(c, False))):
        for k in range(groups):
            key_span = as_column(spans_of(ctx, k))
            key_pos = block_of(ctx, k) * rows + down
            valid = (key_pos >= 0) & (key_pos < total)
            onehot = key_span == span_lane
            at = slice((i * groups + k) * rows, (i * groups + k + 1) * rows)
            for p in range(groups):
                allowed = jnp.dot(
                    onehot.astype(bf16), allowed_q[p], preferred_element_type=f32
                )
                visible = (
                    (allowed > 0.5)
                    & (key_span <= query_span[p])
                    & (query_pos[p] - key_pos < tokens)
                    & valid
                )
                bias_ref[at, p * rows : (p + 1) * rows] = jnp.where(visible, 0.0, HIDDEN)
            if i > 0:
                continue
            level = jnp.sum(jnp.where(onehot, noise, 0.0), axis=1, keepdims=True)
            level_onehot = (level.astype(jnp.int32) == level_lane).astype(f32)
            gate_ref[at, :] = jnp.dot(
                level_onehot,
                table_ref[...],
                precision=lax.Precision.HIGHEST,
                preferred_element_type=f32,
            )
            if by_span:
                slot_ref[:, at] = (span_down == query_span[k]).astype(bf16)
            else:
                slot_ref[:, at] = level_onehot.T.astype(bf16)


def attention_kernel(
    place_ref,
    qo_own_ref, kv_own_ref, qo_ref, kv_ref,
    near_own_ref, near_far_ref, side_own_ref, side_far_ref,
    gate_ref, bias_ref, slot_ref,
    *rest, rows, tokens, q_size, heads, steps, offset, apart,
):
    back_ref, own_ref, far_ref, near_grad_ref, result_ref, *side_grad_refs, sums_ref = rest[
        -7 - apart :
    ]
    scale = 1.0 / math.sqrt(DH)
    bf16, f32 = jnp.bfloat16, jnp.float32
    tile = 32

    def dot(left, right, left_dim, right_dim):
        return lax.dot_general(
            left, right, (((left_dim,), (right_dim,)), ((), ())), preferred_element_type=f32
        )

    def columns(j):
        start = pl.multiple_of(j * DH, DH)
        return pl.ds(start, DH), pl.ds(pl.multiple_of(start + offset, DH), DH)

    def load(j):
        at, at_all = columns(j)
        keys, values = [], []
        for ref, cols in (
            (kv_own_ref, at_all), (kv_ref, at), (near_own_ref, at_all), (near_far_ref, at),
            (side_own_ref, at_all), (side_far_ref, at),
        ):
            keys.append(ref[0, :, cols])
            values.append(ref[1, :, cols])
        keys, values = jnp.concatenate(keys, axis=0), jnp.concatenate(values, axis=0)
        queries = jnp.concatenate([qo_own_ref[0, :, at_all], qo_ref[0, :, at]], axis=0)
        cotangent = jnp.concatenate([qo_own_ref[1, :, at_all], qo_ref[1, :, at]], axis=0)
        blocks = []
        for start in range(0, tokens, q_size):
            span = slice(start, start + q_size)
            q, o = queries[span], cotangent[span].astype(f32)
            gate = gate_ref[span, at_all]
            g = (gate * o).astype(bf16)
            blocks.append((q, o, gate, g, dot(keys, q, 1, 1), dot(values, g, 1, 1)))
        return keys, values, blocks

    def work(j, keys, values, blocks):
        at, at_all = columns(j)
        keys_t, values_t = keys.T, values.T
        key_grad = value_grad = sums = None
        for number, (q, o, gate, g, scores, prob_grad) in enumerate(blocks):
            start = number * q_size
            span = slice(start, start + q_size)
            count = scores.shape[0]
            tiles = [slice(r, r + tile) for r in range(0, count, tile)]
            raised, top = [], None
            for t in tiles:
                part = scores[t] * (scale * LOG2E) + bias_ref[t, span]
                raised.append(part)
                high = jnp.max(part.reshape(tile // 8, 8, q_size), axis=0)
                top = high if top is None else jnp.maximum(top, high)
            top = jnp.max(top, axis=0, keepdims=True)
            total = None
            for i in range(len(tiles)):
                raised[i] = jnp.exp2(raised[i] - top)
                part = jnp.sum(raised[i].reshape(tile // 8, 8, q_size), axis=0)
                total = part if total is None else total + part
            inverse = 1.0 / jnp.sum(total, axis=0, keepdims=True)
            low = jnp.concatenate([(part * inverse).astype(bf16) for part in raised], axis=0)
            attended_t = dot(values_t, low, 1, 0).astype(bf16)
            row_dot = jnp.sum(g.T.astype(f32) * attended_t.astype(f32), axis=0, keepdims=True)
            attended = attended_t.T.astype(f32)
            score_grad = jnp.concatenate(
                [
                    (part * ((prob_grad[t] - row_dot) * inverse)).astype(bf16)
                    for part, t in zip(raised, tiles)
                ],
                axis=0,
            )
            query_grad = (dot(keys_t, score_grad, 1, 0) * scale).astype(bf16).T
            mixed = (gate * attended).astype(bf16)
            if start == 0:
                result_ref[0, :, at] = mixed[:rows]
                result_ref[1, :, at] = query_grad[:rows]
                back_ref[0, : q_size - rows, at] = mixed[rows:]
                back_ref[1, : q_size - rows, at] = query_grad[rows:]
            else:
                back_ref[0, start - rows : start - rows + q_size, at] = mixed
                back_ref[1, start - rows : start - rows + q_size, at] = query_grad
            dk, dv = dot(score_grad, q, 1, 0), dot(low, g, 1, 0)
            part = dot(slot_ref[:, span], (o * attended).astype(bf16), 1, 0)
            key_grad = dk if key_grad is None else key_grad + dk
            value_grad = dv if value_grad is None else value_grad + dv
            sums = part if sums is None else sums + part
        sums_ref[:, at_all] = sums.astype(bf16)
        for i, grad in ((0, key_grad * scale), (1, value_grad)):
            own_ref[i, :, at] = grad[:rows]
            far_ref[i, :, at] = grad[rows:tokens]
            low = grad[tokens:].astype(bf16)
            near_grad_ref[i, :, at] = low[:tokens]
            if apart:
                side_grad_refs[0][i, :, at] = low[tokens : tokens + rows]
                side_grad_refs[1][i, :, at] = low[tokens + rows :]
            else:
                side_grad_refs[0][i, :, at] = low[tokens:]

    def some(step, carry):
        first = step * heads
        ready = load(first)
        for j in range(heads):
            following = load(first + j + 1) if j + 1 < heads else None
            work(first + j, *ready)
            ready = following
        return carry

    if steps == 1:
        some(0, 0)
    else:
        lax.fori_loop(0, steps, some, 0)


def pack_kernel(place_ref, first_ref, second_ref, own_ref, *rest, groups):
    *far_refs, sems = rest
    rows, width = own_ref.shape[1:]
    copies = []

    def copy(ref, start, to):
        cols = pl.ds(pl.multiple_of(start, DH), to.shape[1])
        copies.append(pltpu.make_async_copy(ref.at[:, cols], to, sems.at[len(copies)]))
        copies[-1].start()

    for k in (*range(1, groups), 0):
        start = lax.rem(place_ref[0] + k, groups) * width
        for i, ref in enumerate((first_ref, second_ref)):
            if k == 0:
                copy(ref, start, own_ref.at[i])
                continue
            for p, far_ref in enumerate(far_refs):
                at = pl.ds((k - 1) * rows, rows)
                copy(ref, start + p * far_ref.shape[2], far_ref.at[i, at])
    for one in copies:
        one.wait()


def far_sum_kernel(part_ref, near_ref, side_ref, out_ref):
    far = slice(near_ref.shape[1] - part_ref.shape[1], None)
    total = part_ref[...] + near_ref[:, far].astype(jnp.float32)
    side = side_ref[:, side_ref.shape[1] - part_ref.shape[1] :].astype(jnp.float32)
    out_ref[...] = (total + side).astype(out_ref.dtype)


def finish_kernel(
    place_ref, part_ref, near_ref, side_ref, result_ref, *refs, groups, parts, p, gate
):
    slabs, refs = refs[: 2 * (groups - 1)], refs[2 * (groups - 1) :]
    slot_refs = refs[1 : 1 + groups] if gate else ()
    scratch = 3 if gate else 2
    total_ref, *gate_scratch, sems = refs[-scratch:]
    outs = refs[-scratch - (5 if gate else 4) : -scratch]
    part_width = part_ref.shape[2]
    width = part_width * parts
    copies = []

    def send(source, to):
        copies.append(pltpu.make_async_copy(source, to, sems.at[len(copies)]))
        copies[-1].start()

    def place_slab(slab, first, second, k):
        start = lax.rem(place_ref[0] + k, groups) * width + p * part_width
        cols = pl.ds(pl.multiple_of(start, DH), part_width)
        for i, ref in enumerate((first, second)):
            send(slab.at[i], ref.at[:, cols])

    place_slab(result_ref, outs[0], outs[1], 0)
    for k in range(1, groups):
        place_slab(slabs[k - 1], outs[0], outs[1], k)
        place_slab(slabs[groups + k - 2], outs[2], outs[3], k)
    near, side = (ref[:, : part_ref.shape[1]].astype(jnp.float32) for ref in (near_ref, side_ref))
    total_ref[...] = (part_ref[...] + near + side).astype(total_ref.dtype)
    place_slab(total_ref, outs[2], outs[3], 0)
    if gate:
        noise_ref, gate_ref = refs[0], gate_scratch[0]
        by_span = noise_ref.shape[1] == slot_refs[0].shape[0]
        levels = lax.broadcasted_iota(jnp.int32, (gate_ref.shape[0], noise_ref.shape[1]), 0)
        onehot = (levels == noise_ref[...]).astype(jnp.bfloat16)
        for j, ref in enumerate(slot_refs):
            if by_span:
                sums = jnp.dot(onehot, ref[...], preferred_element_type=jnp.float32)
            else:
                sums = ref[...].astype(jnp.float32)
            start = lax.bitwise_xor(lax.rem(place_ref[0], groups), j) * width
            cols = pl.ds(pl.multiple_of(start, DH), width)
            gate_ref[:, cols] = sums
            send(gate_ref.at[:, cols], outs[4].at[:, cols])
    for one in copies:
        one.wait()


def per_device(
    queries, key_rows, value_rows, out_cotangent, gate_table, span_ids, noise_level, block_mask
):
    groups = lax.axis_size("head")
    ctx_count = lax.axis_size("ctx")
    rows, full_width = queries.shape
    width = full_width // groups
    heads = width // DH
    tokens = rows * groups
    far_rows = tokens - rows
    parts = 2 if heads % 2 == 0 else 1
    part_width = width // parts
    part_heads = heads // parts
    span_total = noise_level.shape[0]
    level_count = gate_table.shape[0]
    by_span = span_total <= level_count // 2
    slots = span_total if by_span else level_count
    c = lax.axis_index("ctx")
    h = lax.axis_index("head")
    place = (c * groups + h).astype(jnp.int32).reshape(1)
    head_at = lambda place: lax.rem(place[0], groups)
    bf16, f32 = jnp.bfloat16, jnp.float32
    tie = lax.optimization_barrier

    near_pairs = [(i, i ^ 1) for i in range(ctx_count)]
    side_pairs = [(i, (i - 1 + 2 * (i % 2)) % ctx_count) for i in range(ctx_count)]

    whole = lambda shape: pl.BlockSpec(shape, lambda i, place: (0,) * len(shape))
    limit = (26 if tokens <= 256 else 56) * 1024 * 1024
    params = pltpu.CompilerParams(vmem_limit_bytes=limit)
    alone = pltpu.CompilerParams(vmem_limit_bytes=56 * 1024 * 1024)
    cheap = pl.CostEstimate(flops=1, bytes_accessed=1, transcendentals=0)
    in_vmem = pl.BlockSpec(memory_space=pltpu.VMEM)
    anywhere = pl.BlockSpec(memory_space=pl.ANY)
    small = pltpu.CompilerParams(vmem_limit_bytes=(12 if tokens <= 256 else 36) * 1024 * 1024)

    def pack(first, second, params):
        far_shape = (2, far_rows, part_width)
        return pl.pallas_call(
            functools.partial(pack_kernel, groups=groups),
            grid_spec=pltpu.PrefetchScalarGridSpec(
                num_scalar_prefetch=1,
                in_specs=[anywhere] * 2,
                out_specs=[in_vmem] * (1 + parts),
                scratch_shapes=[pltpu.SemaphoreType.DMA((2 + 2 * (groups - 1) * parts,))],
            ),
            out_shape=[jax.ShapeDtypeStruct((2, rows, width), bf16)]
            + [jax.ShapeDtypeStruct(far_shape, bf16)] * parts,
            compiler_params=params,
            cost_estimate=cheap,
            name="pack",
        )(place, first, second)

    def to_peers(slab):
        arrived = []
        for k in range(1, groups):
            part = slab if groups == 2 else slab[:, (k - 1) * rows : k * rows]
            pairs = [(i, (i + k) % groups) for i in range(groups)]
            arrived.append(lax.ppermute(part, "head", pairs))
        return arrived[0] if groups == 2 else jnp.concatenate(arrived, axis=1)

    def from_peers(slab):
        arrived = []
        for k in range(1, groups):
            part = slab if groups == 2 else slab[:, (k - 1) * rows : k * rows]
            pairs = [(i, (i - k) % groups) for i in range(groups)]
            arrived.append(lax.ppermute(part, "head", pairs))
        return arrived

    kv_own, *kv_sent = pack(key_rows, value_rows, alone)
    qo_own, *qo_sent = pack(queries, out_cotangent, small)
    side_own = lax.ppermute(kv_own, "ctx", side_pairs)
    near_own = lax.ppermute(kv_own, "ctx", near_pairs)
    kv_far = [to_peers(slab) for slab in kv_sent]
    side_far = [lax.ppermute(slab, "ctx", side_pairs) for slab in kv_far]
    near_far = [lax.ppermute(slab, "ctx", near_pairs) for slab in kv_far]
    qo_far = [
        to_peers(tie((slab, *done))[0])
        for slab, done in zip(qo_sent, (kv_far[:1], (*kv_far[1:], side_own, near_own)))
    ]

    sizes = (ctx_count, groups, rows, span_total, level_count, by_span)
    whole = lambda shape: pl.BlockSpec(shape, lambda i, place: (0,) * len(shape))
    bias, gate, slot = pl.pallas_call(
        functools.partial(prep_kernel, sizes=sizes),
        grid_spec=pltpu.PrefetchScalarGridSpec(
            num_scalar_prefetch=1,
            grid=(1,),
            in_specs=[
                whole((ctx_count * groups, rows)),
                whole((1, span_total)),
                whole((span_total, span_total)),
                pl.BlockSpec((level_count, width), lambda i, place: (0, head_at(place))),
            ],
            out_specs=[
                whole((3 * tokens, tokens)),
                whole((tokens, width)),
                whole((slots, tokens)),
            ],
        ),
        out_shape=[
            jax.ShapeDtypeStruct((3 * tokens, tokens), f32),
            jax.ShapeDtypeStruct((tokens, width), f32),
            jax.ShapeDtypeStruct((slots, tokens), bf16),
        ],
        compiler_params=small,
        cost_estimate=cheap,
        name="prep",
    )(
        place,
        span_ids.reshape(ctx_count * groups, rows),
        noise_level.reshape(1, span_total),
        block_mask,
        gate_table,
    )

    direct = tokens <= 256
    batch = next(n for n in (3, 2, 1) if part_heads % n == 0) if direct else 1
    q_size = min(256, tokens)

    def attention(p, joint):
        pair = lambda count: pl.BlockSpec((2, count, DH), lambda i, place: (0, 0, i))
        at_part = lambda count: pl.BlockSpec(
            (2, count, DH), lambda i, place: (0, 0, p * part_heads + i)
        )
        column = lambda count: pl.BlockSpec(
            (count, DH), lambda i, place: (0, p * part_heads + i)
        )
        struct = jax.ShapeDtypeStruct
        side_counts = (rows, far_rows) if p + 1 == parts else (tokens,)
        inputs = [
            qo_own, kv_own, qo_far[p], kv_far[p],
            near_own, near_far[p], side_own, side_far[p],
            gate, bias, slot,
        ]
        in_specs = [
            at_part(rows), at_part(rows), pair(far_rows), pair(far_rows),
            at_part(rows), pair(far_rows), at_part(rows), pair(far_rows),
            column(tokens), whole((3 * tokens, tokens)), whole((slots, tokens)),
        ]
        counts = (far_rows, rows, far_rows, tokens, rows, *side_counts)
        out_specs = [*[pair(count) for count in counts], column(slots)]
        if direct:
            in_specs, out_specs = [in_vmem] * len(in_specs), [in_vmem] * len(out_specs)
        types = [f32 if i in (1, 2) else bf16 for i in range(len(counts))]
        return pl.pallas_call(
            functools.partial(
                attention_kernel,
                rows=rows, tokens=tokens, q_size=q_size, apart=p + 1 == parts, heads=batch,
                steps=part_heads // batch if direct else 1,
                offset=p * part_width if direct else 0,
            ),
            grid_spec=pltpu.PrefetchScalarGridSpec(
                num_scalar_prefetch=1,
                grid=(1,) if direct else (part_heads,),
                in_specs=in_specs + [anywhere] * len(joint),
                out_specs=out_specs,
            ),
            out_shape=[
                *[
                    struct((2, count, part_width), kind) for count, kind in zip(counts, types)
                ],
                struct((slots, width), bf16),
            ],
            input_output_aliases={1 + len(inputs) + i: len(counts) + i for i in range(len(joint))},
            compiler_params=params,
            cost_estimate=cheap,
            name="attention",
        )(place, *inputs, *joint)

    def shifted(array, step):
        return lax.ppermute(array, "ctx", [(i, i ^ step) for i in range(ctx_count)])

    def rounds(steps, sums):
        for one, two in zip(steps[::2], [*steps[1::2], None]):
            if two is None:
                sums = sums + shifted(sums, one)
                continue
            across = [shifted(sums, step) for step in (one, two, one ^ two)]
            sums = (sums + across[0]) + (across[1] + across[2])
        return sums

    bits = [1 << n for n in range(ctx_count.bit_length() - 1)]
    def summed(p):
        far_grad = pl.pallas_call(
            far_sum_kernel,
            in_specs=[in_vmem] * 3,
            out_specs=in_vmem,
            out_shape=jax.ShapeDtypeStruct((2, far_rows, part_width), bf16),
            compiler_params=small,
            cost_estimate=cheap,
            name="far_sum",
        )(far[p], near_back[p], side_back_far[p])
        far_sent.append(far_grad)
        grad_far.append(from_peers(far_grad))

    joint, own, far, own_results = (), [], [], []
    back_far, side_back_far, near_back, side_back_own, far_sent, grad_far = [], [], [], [], [], []
    for p in range(parts):
        back, own_part, far_part, near_grad, result, *rest = attention(p, joint)
        side_grads, joint = rest[:-1], rest[-1:]
        own_results.append(result)
        if p + 1 < parts:
            side_grads, *_ = tie((side_grads, side_far[p + 1], near_far[p + 1], qo_far[p + 1]))
        if p > 0:
            side_grads, side_back_far = tie(
                (side_grads, side_back_far)
            )
            joint, back_far = tie((joint, back_far))
        own.append(own_part)
        far.append(far_part)
        side_back_far.append(lax.ppermute(side_grads[-1], "ctx", side_pairs))
        near_back.append(lax.ppermute(near_grad, "ctx", near_pairs))
        back_far.append(from_peers(back))
        if p > 0:
            sums = rounds(bits[2:], joint[0])
            side_back_far[p - 1], sums, _ = tie((side_back_far[p - 1], sums, back_far[p]))
            summed(p - 1)
        if p + 1 < parts:
            side_back_own.append(side_back_far[p])
            continue
        side_grad_own, _ = tie((side_grads[0], side_back_far[p]))
        side_back_own.append(lax.ppermute(side_grad_own, "ctx", side_pairs))
    if parts == 1:
        sums = rounds(bits[2:], joint[0])

    sums = rounds(bits[:1], sums)
    side_back_far, sums, back_far, grad_far = tie((side_back_far, sums, back_far, grad_far))
    summed(parts - 1)

    def to_all(before, after, sums):
        slabs = [rounds(before, sums)]
        for step in (1 << n for n in range(groups.bit_length() - 1)):
            pairs = [(i, i ^ step) for i in range(groups)]
            slabs = slabs + [lax.ppermute(slab, "head", pairs) for slab in slabs]
        return [rounds(after, slab) for slab in slabs]

    sums, _ = tie((sums, far_sent[-1]))
    slabs = to_all(bits[1:2], [], sums)
    results = []
    struct = jax.ShapeDtypeStruct
    for p in range(parts):
        gate = p + 1 == parts
        operands = [own[p], near_back[p], side_back_own[p], own_results[p], *back_far[p], *grad_far[p]]
        if gate:
            operands += [noise_level.reshape(1, span_total), *slabs]
        scratch = [pltpu.VMEM((2, rows, part_width), bf16)]
        if gate:
            scratch.append(pltpu.VMEM((level_count, full_width), f32))
        scratch.append(pltpu.SemaphoreType.DMA((4 * groups + groups,)))
        results = pl.pallas_call(
            functools.partial(finish_kernel, groups=groups, parts=parts, p=p, gate=gate),
            grid_spec=pltpu.PrefetchScalarGridSpec(
                num_scalar_prefetch=1,
                in_specs=[in_vmem] * len(operands) + [anywhere] * len(results),
                out_specs=[anywhere] * (4 + gate),
                scratch_shapes=scratch,
            ),
            out_shape=[struct((rows, full_width), bf16)] * 4
            + [struct((level_count, full_width), f32)] * gate,
            input_output_aliases={1 + len(operands) + i: i for i in range(len(results))},
            compiler_params=small,
            cost_estimate=cheap,
            name="finish",
        )(place, *operands, *results)
    return tuple(results)


def solution(mesh):
    sharded = P(("ctx", "head"), None)
    return jax.shard_map(
        per_device,
        mesh=mesh,
        in_specs=(sharded,) * 4 + (P(),) * 4,
        out_specs=(sharded,) * 4 + (P(),),
        check_vma=False,
    )
```

```python
import functools
import math

import jax
import jax.numpy as jnp
from jax import lax
from jax.experimental import pallas as pl
from jax.experimental.pallas import tpu as pltpu
from jax.sharding import PartitionSpec as P

DH = 128
HIDDEN = -1e30
LOG2E = 1.4426950408889634


def other_ctx(c, near):
    odd = lax.rem(c, 2)
    return c + 1 - 2 * odd if near else c - 1 + 2 * odd


def prep_kernel(
    place_ref, span_ref, noise_ref, mask_ref, table_ref, bias_ref, gate_ref, slot_ref, *, sizes
):
    ctx_count, groups, rows, span_total, level_count, by_span = sizes
    c, h = lax.div(place_ref[0], groups), lax.rem(place_ref[0], groups)
    tokens = groups * rows
    total = ctx_count * tokens
    bf16, f32 = jnp.bfloat16, jnp.float32

    def block_of(ctx, k):
        return ctx * groups + lax.rem(h - k + groups, groups)

    def spans_of(ctx, k):
        at = jnp.clip(ctx, 0, ctx_count - 1)
        return span_ref[pl.ds(block_of(at, k), 1), :]

    def as_column(row):
        return jnp.broadcast_to(row.astype(f32), (rows, rows)).T[:, :1].astype(jnp.int32)

    across = lax.broadcasted_iota(jnp.int32, (1, rows), 1)
    down = lax.broadcasted_iota(jnp.int32, (rows, 1), 0)
    span_lane = lax.broadcasted_iota(jnp.int32, (rows, span_total), 1)
    span_down = lax.broadcasted_iota(jnp.int32, (span_total, rows), 0)
    level_lane = lax.broadcasted_iota(jnp.int32, (rows, level_count), 1)
    query_span = [spans_of(c, k) for k in range(groups)]
    query_pos = [block_of(c, k) * rows + across for k in range(groups)]
    mask_low = mask_ref[...].astype(bf16)
    allowed_q = [
        lax.dot_general(
            mask_low,
            (span_down == row).astype(bf16),
            (((0,), (0,)), ((), ())),
            preferred_element_type=f32,
        ).astype(bf16)
        for row in query_span
    ]
    noise = noise_ref[...].astype(f32)
    for i, ctx in enumerate((c, other_ctx(c, True), other_ctx(c, False))):
        for k in range(groups):
            key_span = as_column(spans_of(ctx, k))
            key_pos = block_of(ctx, k) * rows + down
            valid = (key_pos >= 0) & (key_pos < total)
            onehot = key_span == span_lane
            at = slice((i * groups + k) * rows, (i * groups + k + 1) * rows)
            for p in range(groups):
                allowed = jnp.dot(
                    onehot.astype(bf16), allowed_q[p], preferred_element_type=f32
                )
                visible = (
                    (allowed > 0.5)
                    & (key_span <= query_span[p])
                    & (query_pos[p] - key_pos < tokens)
                    & valid
                )
                bias_ref[at, p * rows : (p + 1) * rows] = jnp.where(visible, 0.0, HIDDEN)
            if i > 0:
                continue
            level = jnp.sum(jnp.where(onehot, noise, 0.0), axis=1, keepdims=True)
            level_onehot = (level.astype(jnp.int32) == level_lane).astype(f32)
            gate_ref[at, :] = jnp.dot(
                level_onehot,
                table_ref[...],
                precision=lax.Precision.HIGHEST,
                preferred_element_type=f32,
            )
            if by_span:
                slot_ref[:, at] = (span_down == query_span[k]).astype(bf16)
            else:
                slot_ref[:, at] = level_onehot.T.astype(bf16)


def attention_kernel(
    place_ref,
    qo_own_ref, kv_own_ref, qo_ref, kv_ref,
    near_own_ref, near_far_ref, side_own_ref, side_far_ref,
    gate_ref, bias_ref, slot_ref,
    *rest, rows, tokens, q_size, heads, steps, offset, apart,
):
    back_ref, own_ref, far_ref, near_grad_ref, result_ref, *side_grad_refs, sums_ref = rest[
        -7 - apart :
    ]
    scale = 1.0 / math.sqrt(DH)
    bf16, f32 = jnp.bfloat16, jnp.float32
    tile = 32

    def dot(left, right, left_dim, right_dim):
        return lax.dot_general(
            left, right, (((left_dim,), (right_dim,)), ((), ())), preferred_element_type=f32
        )

    def columns(j):
        start = pl.multiple_of(j * DH, DH)
        return pl.ds(start, DH), pl.ds(pl.multiple_of(start + offset, DH), DH)

    def load(j):
        at, at_all = columns(j)
        keys, values = [], []
        for ref, cols in (
            (kv_own_ref, at_all), (kv_ref, at), (near_own_ref, at_all), (near_far_ref, at),
            (side_own_ref, at_all), (side_far_ref, at),
        ):
            keys.append(ref[0, :, cols])
            values.append(ref[1, :, cols])
        keys, values = jnp.concatenate(keys, axis=0), jnp.concatenate(values, axis=0)
        queries = jnp.concatenate([qo_own_ref[0, :, at_all], qo_ref[0, :, at]], axis=0)
        cotangent = jnp.concatenate([qo_own_ref[1, :, at_all], qo_ref[1, :, at]], axis=0)
        blocks = []
        for start in range(0, tokens, q_size):
            span = slice(start, start + q_size)
            q, o = queries[span], cotangent[span].astype(f32)
            gate = gate_ref[span, at_all]
            g = (gate * o).astype(bf16)
            blocks.append((q, o, gate, g, dot(keys, q, 1, 1), dot(values, g, 1, 1)))
        return keys, values, blocks

    def work(j, keys, values, blocks):
        at, at_all = columns(j)
        keys_t, values_t = keys.T, values.T
        key_grad = value_grad = sums = None
        for number, (q, o, gate, g, scores, prob_grad) in enumerate(blocks):
            start = number * q_size
            span = slice(start, start + q_size)
            count = scores.shape[0]
            tiles = [slice(r, r + tile) for r in range(0, count, tile)]
            raised, top = [], None
            for t in tiles:
                part = scores[t] * (scale * LOG2E) + bias_ref[t, span]
                raised.append(part)
                high = jnp.max(part.reshape(tile // 8, 8, q_size), axis=0)
                top = high if top is None else jnp.maximum(top, high)
            top = jnp.max(top, axis=0, keepdims=True)
            total = None
            for i in range(len(tiles)):
                raised[i] = jnp.exp2(raised[i] - top)
                part = jnp.sum(raised[i].reshape(tile // 8, 8, q_size), axis=0)
                total = part if total is None else total + part
            inverse = 1.0 / jnp.sum(total, axis=0, keepdims=True)
            low = jnp.concatenate([(part * inverse).astype(bf16) for part in raised], axis=0)
            attended_t = dot(values_t, low, 1, 0).astype(bf16)
            row_dot = jnp.sum(g.T.astype(f32) * attended_t.astype(f32), axis=0, keepdims=True)
            attended = attended_t.T.astype(f32)
            score_grad = jnp.concatenate(
                [
                    (part * ((prob_grad[t] - row_dot) * inverse)).astype(bf16)
                    for part, t in zip(raised, tiles)
                ],
                axis=0,
            )
            query_grad = (dot(keys_t, score_grad, 1, 0) * scale).astype(bf16).T
            mixed = (gate * attended).astype(bf16)
            if start == 0:
                result_ref[0, :, at] = mixed[:rows]
                result_ref[1, :, at] = query_grad[:rows]
                back_ref[0, : q_size - rows, at] = mixed[rows:]
                back_ref[1, : q_size - rows, at] = query_grad[rows:]
            else:
                back_ref[0, start - rows : start - rows + q_size, at] = mixed
                back_ref[1, start - rows : start - rows + q_size, at] = query_grad
            dk, dv = dot(score_grad, q, 1, 0), dot(low, g, 1, 0)
            part = dot(slot_ref[:, span], (o * attended).astype(bf16), 1, 0)
            key_grad = dk if key_grad is None else key_grad + dk
            value_grad = dv if value_grad is None else value_grad + dv
            sums = part if sums is None else sums + part
        sums_ref[:, at_all] = sums.astype(bf16)
        for i, grad in ((0, key_grad * scale), (1, value_grad)):
            own_ref[i, :, at] = grad[:rows]
            far_ref[i, :, at] = grad[rows:tokens]
            low = grad[tokens:].astype(bf16)
            near_grad_ref[i, :, at] = low[:tokens]
            if apart:
                side_grad_refs[0][i, :, at] = low[tokens : tokens + rows]
                side_grad_refs[1][i, :, at] = low[tokens + rows :]
            else:
                side_grad_refs[0][i, :, at] = low[tokens:]

    def some(step, carry):
        first = step * heads
        ready = load(first)
        for j in range(heads):
            following = load(first + j + 1) if j + 1 < heads else None
            work(first + j, *ready)
            ready = following
        return carry

    if steps == 1:
        some(0, 0)
    else:
        lax.fori_loop(0, steps, some, 0)


def pack_kernel(place_ref, first_ref, second_ref, *rest, peers, groups):
    *slab_refs, sems = rest
    rows = first_ref.shape[0]
    width = first_ref.shape[1] // groups
    copies = []
    for number, k in enumerate(peers):
        start = lax.rem(place_ref[0] + k, groups) * width
        for i, ref in enumerate((first_ref, second_ref)):
            for p, slab_ref in enumerate(slab_refs):
                part = slab_ref.shape[2]
                cols = pl.ds(pl.multiple_of(start + p * part, DH), part)
                to = slab_ref.at[i, pl.ds(number * rows, rows)]
                copies.append(
                    pltpu.make_async_copy(ref.at[:, cols], to, sems.at[len(copies)])
                )
                copies[-1].start()
    for one in copies:
        one.wait()


def far_sum_kernel(part_ref, near_ref, side_ref, out_ref):
    far = slice(near_ref.shape[1] - part_ref.shape[1], None)
    total = part_ref[...] + near_ref[:, far].astype(jnp.float32)
    side = side_ref[:, side_ref.shape[1] - part_ref.shape[1] :].astype(jnp.float32)
    out_ref[...] = (total + side).astype(out_ref.dtype)


def finish_kernel(
    place_ref, part_ref, near_ref, side_ref, result_ref, *refs, groups, parts, p, gate
):
    slabs, refs = refs[: 2 * (groups - 1)], refs[2 * (groups - 1) :]
    slot_refs = refs[1 : 1 + groups] if gate else ()
    scratch = 3 if gate else 2
    total_ref, *gate_scratch, sems = refs[-scratch:]
    outs = refs[-scratch - (5 if gate else 4) : -scratch]
    part_width = part_ref.shape[2]
    width = part_width * parts
    copies = []

    def send(source, to):
        copies.append(pltpu.make_async_copy(source, to, sems.at[len(copies)]))
        copies[-1].start()

    def place_slab(slab, first, second, k):
        start = lax.rem(place_ref[0] + k, groups) * width + p * part_width
        cols = pl.ds(pl.multiple_of(start, DH), part_width)
        for i, ref in enumerate((first, second)):
            send(slab.at[i], ref.at[:, cols])

    place_slab(result_ref, outs[0], outs[1], 0)
    for k in range(1, groups):
        place_slab(slabs[k - 1], outs[0], outs[1], k)
        place_slab(slabs[groups + k - 2], outs[2], outs[3], k)
    near, side = (ref[:, : part_ref.shape[1]].astype(jnp.float32) for ref in (near_ref, side_ref))
    total_ref[...] = (part_ref[...] + near + side).astype(total_ref.dtype)
    place_slab(total_ref, outs[2], outs[3], 0)
    if gate:
        noise_ref, gate_ref = refs[0], gate_scratch[0]
        by_span = noise_ref.shape[1] == slot_refs[0].shape[0]
        levels = lax.broadcasted_iota(jnp.int32, (gate_ref.shape[0], noise_ref.shape[1]), 0)
        onehot = (levels == noise_ref[...]).astype(jnp.bfloat16)
        for j, ref in enumerate(slot_refs):
            if by_span:
                sums = jnp.dot(onehot, ref[...], preferred_element_type=jnp.float32)
            else:
                sums = ref[...].astype(jnp.float32)
            start = lax.bitwise_xor(lax.rem(place_ref[0], groups), j) * width
            cols = pl.ds(pl.multiple_of(start, DH), width)
            gate_ref[:, cols] = sums
            send(gate_ref.at[:, cols], outs[4].at[:, cols])
    for one in copies:
        one.wait()


def per_device(
    queries, key_rows, value_rows, out_cotangent, gate_table, span_ids, noise_level, block_mask
):
    groups = lax.axis_size("head")
    ctx_count = lax.axis_size("ctx")
    rows, full_width = queries.shape
    width = full_width // groups
    heads = width // DH
    tokens = rows * groups
    far_rows = tokens - rows
    parts = 2 if heads % 2 == 0 else 1
    part_width = width // parts
    part_heads = heads // parts
    span_total = noise_level.shape[0]
    level_count = gate_table.shape[0]
    by_span = span_total <= level_count // 2
    slots = span_total if by_span else level_count
    c = lax.axis_index("ctx")
    h = lax.axis_index("head")
    place = (c * groups + h).astype(jnp.int32).reshape(1)
    head_at = lambda place: lax.rem(place[0], groups)
    bf16, f32 = jnp.bfloat16, jnp.float32
    tie = lax.optimization_barrier

    near_pairs = [(i, i ^ 1) for i in range(ctx_count)]
    side_pairs = [(i, (i - 1 + 2 * (i % 2)) % ctx_count) for i in range(ctx_count)]

    whole = lambda shape: pl.BlockSpec(shape, lambda i, place: (0,) * len(shape))
    limit = (26 if tokens <= 256 else 56) * 1024 * 1024
    params = pltpu.CompilerParams(vmem_limit_bytes=limit)
    alone = pltpu.CompilerParams(vmem_limit_bytes=56 * 1024 * 1024)
    cheap = pl.CostEstimate(flops=1, bytes_accessed=1, transcendentals=0)
    in_vmem = pl.BlockSpec(memory_space=pltpu.VMEM)
    anywhere = pl.BlockSpec(memory_space=pl.ANY)
    small = pltpu.CompilerParams(vmem_limit_bytes=(12 if tokens <= 256 else 36) * 1024 * 1024)

    def pack(first, second, peers, count, params):
        shape = (2, len(peers) * rows, width // count)
        return pl.pallas_call(
            functools.partial(pack_kernel, peers=peers, groups=groups),
            grid_spec=pltpu.PrefetchScalarGridSpec(
                num_scalar_prefetch=1,
                in_specs=[anywhere] * 2,
                out_specs=[in_vmem] * count,
                scratch_shapes=[pltpu.SemaphoreType.DMA((2 * len(peers) * count,))],
            ),
            out_shape=[jax.ShapeDtypeStruct(shape, bf16)] * count,
            compiler_params=params,
            cost_estimate=cheap,
            name="pack",
        )(place, first, second)

    def to_peers(slab):
        arrived = []
        for k in range(1, groups):
            part = slab if groups == 2 else slab[:, (k - 1) * rows : k * rows]
            pairs = [(i, (i + k) % groups) for i in range(groups)]
            arrived.append(lax.ppermute(part, "head", pairs))
        return arrived[0] if groups == 2 else jnp.concatenate(arrived, axis=1)

    def from_peers(slab):
        arrived = []
        for k in range(1, groups):
            part = slab if groups == 2 else slab[:, (k - 1) * rows : k * rows]
            pairs = [(i, (i - k) % groups) for i in range(groups)]
            arrived.append(lax.ppermute(part, "head", pairs))
        return arrived

    others = tuple(range(1, groups))
    (kv_own,) = pack(key_rows, value_rows, (0,), 1, alone)
    kv_sent = pack(key_rows, value_rows, others, parts, alone)
    (qo_own,) = pack(queries, out_cotangent, (0,), 1, small)
    qo_sent = pack(queries, out_cotangent, others, parts, small)
    side_own = lax.ppermute(kv_own, "ctx", side_pairs)
    near_own = lax.ppermute(kv_own, "ctx", near_pairs)
    kv_far = [to_peers(slab) for slab in kv_sent]
    side_far = [lax.ppermute(slab, "ctx", side_pairs) for slab in kv_far]
    near_far = [lax.ppermute(slab, "ctx", near_pairs) for slab in kv_far]
    qo_far = [
        to_peers(tie((slab, *done))[0])
        for slab, done in zip(qo_sent, (kv_far[:1], (*kv_far[1:], side_own, near_own)))
    ]

    sizes = (ctx_count, groups, rows, span_total, level_count, by_span)
    whole = lambda shape: pl.BlockSpec(shape, lambda i, place: (0,) * len(shape))
    bias, gate, slot = pl.pallas_call(
        functools.partial(prep_kernel, sizes=sizes),
        grid_spec=pltpu.PrefetchScalarGridSpec(
            num_scalar_prefetch=1,
            grid=(1,),
            in_specs=[
                whole((ctx_count * groups, rows)),
                whole((1, span_total)),
                whole((span_total, span_total)),
                pl.BlockSpec((level_count, width), lambda i, place: (0, head_at(place))),
            ],
            out_specs=[
                whole((3 * tokens, tokens)),
                whole((tokens, width)),
                whole((slots, tokens)),
            ],
        ),
        out_shape=[
            jax.ShapeDtypeStruct((3 * tokens, tokens), f32),
            jax.ShapeDtypeStruct((tokens, width), f32),
            jax.ShapeDtypeStruct((slots, tokens), bf16),
        ],
        compiler_params=small,
        cost_estimate=cheap,
        name="prep",
    )(
        place,
        span_ids.reshape(ctx_count * groups, rows),
        noise_level.reshape(1, span_total),
        block_mask,
        gate_table,
    )

    direct = tokens <= 256
    batch = next(n for n in (3, 2, 1) if part_heads % n == 0) if direct else 1
    q_size = min(256, tokens)

    def attention(p, joint):
        pair = lambda count: pl.BlockSpec((2, count, DH), lambda i, place: (0, 0, i))
        at_part = lambda count: pl.BlockSpec(
            (2, count, DH), lambda i, place: (0, 0, p * part_heads + i)
        )
        column = lambda count: pl.BlockSpec(
            (count, DH), lambda i, place: (0, p * part_heads + i)
        )
        struct = jax.ShapeDtypeStruct
        side_counts = (rows, far_rows) if p + 1 == parts else (tokens,)
        inputs = [
            qo_own, kv_own, qo_far[p], kv_far[p],
            near_own, near_far[p], side_own, side_far[p],
            gate, bias, slot,
        ]
        in_specs = [
            at_part(rows), at_part(rows), pair(far_rows), pair(far_rows),
            at_part(rows), pair(far_rows), at_part(rows), pair(far_rows),
            column(tokens), whole((3 * tokens, tokens)), whole((slots, tokens)),
        ]
        counts = (far_rows, rows, far_rows, tokens, rows, *side_counts)
        out_specs = [*[pair(count) for count in counts], column(slots)]
        if direct:
            in_specs, out_specs = [in_vmem] * len(in_specs), [in_vmem] * len(out_specs)
        types = [f32 if i in (1, 2) else bf16 for i in range(len(counts))]
        return pl.pallas_call(
            functools.partial(
                attention_kernel,
                rows=rows, tokens=tokens, q_size=q_size, apart=p + 1 == parts, heads=batch,
                steps=part_heads // batch if direct else 1,
                offset=p * part_width if direct else 0,
            ),
            grid_spec=pltpu.PrefetchScalarGridSpec(
                num_scalar_prefetch=1,
                grid=(1,) if direct else (part_heads,),
                in_specs=in_specs + [anywhere] * len(joint),
                out_specs=out_specs,
            ),
            out_shape=[
                *[
                    struct((2, count, part_width), kind) for count, kind in zip(counts, types)
                ],
                struct((slots, width), bf16),
            ],
            input_output_aliases={1 + len(inputs) + i: len(counts) + i for i in range(len(joint))},
            compiler_params=params,
            cost_estimate=cheap,
            name="attention",
        )(place, *inputs, *joint)

    def shifted(array, step):
        return lax.ppermute(array, "ctx", [(i, i ^ step) for i in range(ctx_count)])

    def rounds(steps, sums):
        for one, two in zip(steps[::2], [*steps[1::2], None]):
            if two is None:
                sums = sums + shifted(sums, one)
                continue
            across = [shifted(sums, step) for step in (one, two, one ^ two)]
            sums = (sums + across[0]) + (across[1] + across[2])
        return sums

    bits = [1 << n for n in range(ctx_count.bit_length() - 1)]
    def summed(p):
        far_grad = pl.pallas_call(
            far_sum_kernel,
            in_specs=[in_vmem] * 3,
            out_specs=in_vmem,
            out_shape=jax.ShapeDtypeStruct((2, far_rows, part_width), bf16),
            compiler_params=small,
            cost_estimate=cheap,
            name="far_sum",
        )(far[p], near_back[p], side_back_far[p])
        far_sent.append(far_grad)
        grad_far.append(from_peers(far_grad))

    joint, own, far, own_results = (), [], [], []
    back_far, side_back_far, near_back, side_back_own, far_sent, grad_far = [], [], [], [], [], []
    for p in range(parts):
        back, own_part, far_part, near_grad, result, *rest = attention(p, joint)
        side_grads, joint = rest[:-1], rest[-1:]
        own_results.append(result)
        if p + 1 < parts:
            side_grads, *_ = tie((side_grads, side_far[p + 1], near_far[p + 1], qo_far[p + 1]))
        if p > 0:
            side_grads, side_back_far = tie(
                (side_grads, side_back_far)
            )
            joint, back_far = tie((joint, back_far))
        own.append(own_part)
        far.append(far_part)
        side_back_far.append(lax.ppermute(side_grads[-1], "ctx", side_pairs))
        near_back.append(lax.ppermute(near_grad, "ctx", near_pairs))
        back_far.append(from_peers(back))
        if p > 0:
            sums = rounds(bits[2:], joint[0])
            side_back_far[p - 1], sums, _ = tie((side_back_far[p - 1], sums, back_far[p]))
            summed(p - 1)
        if p + 1 < parts:
            side_back_own.append(side_back_far[p])
            continue
        side_grad_own, _ = tie((side_grads[0], side_back_far[p]))
        side_back_own.append(lax.ppermute(side_grad_own, "ctx", side_pairs))
    if parts == 1:
        sums = rounds(bits[2:], joint[0])

    sums = rounds(bits[1:2], rounds(bits[:1], sums))
    side_back_far, sums, back_far, grad_far = tie((side_back_far, sums, back_far, grad_far))
    summed(parts - 1)

    def to_all(before, after, sums):
        slabs = [rounds(before, sums)]
        for step in (1 << n for n in range(groups.bit_length() - 1)):
            pairs = [(i, i ^ step) for i in range(groups)]
            slabs = slabs + [lax.ppermute(slab, "head", pairs) for slab in slabs]
        return [rounds(after, slab) for slab in slabs]

    sums, _ = tie((sums, far_sent[-1]))
    slabs = to_all([], [], sums)
    results = []
    struct = jax.ShapeDtypeStruct
    for p in range(parts):
        gate = p + 1 == parts
        operands = [own[p], near_back[p], side_back_own[p], own_results[p], *back_far[p], *grad_far[p]]
        if gate:
            operands += [noise_level.reshape(1, span_total), *slabs]
        scratch = [pltpu.VMEM((2, rows, part_width), bf16)]
        if gate:
            scratch.append(pltpu.VMEM((level_count, full_width), f32))
        scratch.append(pltpu.SemaphoreType.DMA((4 * groups + groups,)))
        results = pl.pallas_call(
            functools.partial(finish_kernel, groups=groups, parts=parts, p=p, gate=gate),
            grid_spec=pltpu.PrefetchScalarGridSpec(
                num_scalar_prefetch=1,
                in_specs=[in_vmem] * len(operands) + [anywhere] * len(results),
                out_specs=[anywhere] * (4 + gate),
                scratch_shapes=scratch,
            ),
            out_shape=[struct((rows, full_width), bf16)] * 4
            + [struct((level_count, full_width), f32)] * gate,
            input_output_aliases={1 + len(operands) + i: i for i in range(len(results))},
            compiler_params=small,
            cost_estimate=cheap,
            name="finish",
        )(place, *operands, *results)
    return tuple(results)


def solution(mesh):
    sharded = P(("ctx", "head"), None)
    return jax.shard_map(
        per_device,
        mesh=mesh,
        in_specs=(sharded,) * 4 + (P(),) * 4,
        out_specs=(sharded,) * 4 + (P(),),
        check_vma=False,
    )
```

```python
import functools
import math

import jax
import jax.numpy as jnp
from jax import lax
from jax.experimental import pallas as pl
from jax.experimental.pallas import tpu as pltpu
from jax.sharding import PartitionSpec as P

DH = 128
HIDDEN = -1e30
LOG2E = 1.4426950408889634


def other_ctx(c, near):
    odd = lax.rem(c, 2)
    return c + 1 - 2 * odd if near else c - 1 + 2 * odd


def prep_kernel(
    place_ref, span_ref, noise_ref, mask_ref, table_ref, bias_ref, gate_ref, slot_ref, *, sizes
):
    ctx_count, groups, rows, span_total, level_count, by_span = sizes
    c, h = lax.div(place_ref[0], groups), lax.rem(place_ref[0], groups)
    tokens = groups * rows
    total = ctx_count * tokens
    bf16, f32 = jnp.bfloat16, jnp.float32

    def block_of(ctx, k):
        return ctx * groups + lax.rem(h - k + groups, groups)

    def spans_of(ctx, k):
        at = jnp.clip(ctx, 0, ctx_count - 1)
        return span_ref[pl.ds(block_of(at, k), 1), :]

    def as_column(row):
        return jnp.broadcast_to(row.astype(f32), (rows, rows)).T[:, :1].astype(jnp.int32)

    across = lax.broadcasted_iota(jnp.int32, (1, rows), 1)
    down = lax.broadcasted_iota(jnp.int32, (rows, 1), 0)
    span_lane = lax.broadcasted_iota(jnp.int32, (rows, span_total), 1)
    span_down = lax.broadcasted_iota(jnp.int32, (span_total, rows), 0)
    level_lane = lax.broadcasted_iota(jnp.int32, (rows, level_count), 1)
    query_span = [spans_of(c, k) for k in range(groups)]
    query_pos = [block_of(c, k) * rows + across for k in range(groups)]
    mask_low = mask_ref[...].astype(bf16)
    allowed_q = [
        lax.dot_general(
            mask_low,
            (span_down == row).astype(bf16),
            (((0,), (0,)), ((), ())),
            preferred_element_type=f32,
        ).astype(bf16)
        for row in query_span
    ]
    noise = noise_ref[...].astype(f32)
    for i, ctx in enumerate((c, other_ctx(c, True), other_ctx(c, False))):
        for k in range(groups):
            key_span = as_column(spans_of(ctx, k))
            key_pos = block_of(ctx, k) * rows + down
            valid = (key_pos >= 0) & (key_pos < total)
            onehot = key_span == span_lane
            at = slice((i * groups + k) * rows, (i * groups + k + 1) * rows)
            for p in range(groups):
                allowed = jnp.dot(
                    onehot.astype(bf16), allowed_q[p], preferred_element_type=f32
                )
                visible = (
                    (allowed > 0.5)
                    & (key_span <= query_span[p])
                    & (query_pos[p] - key_pos < tokens)
                    & valid
                )
                bias_ref[at, p * rows : (p + 1) * rows] = jnp.where(visible, 0.0, HIDDEN)
            if i > 0:
                continue
            level = jnp.sum(jnp.where(onehot, noise, 0.0), axis=1, keepdims=True)
            level_onehot = (level.astype(jnp.int32) == level_lane).astype(f32)
            gate_ref[at, :] = jnp.dot(
                level_onehot,
                table_ref[...],
                precision=lax.Precision.HIGHEST,
                preferred_element_type=f32,
            )
            if by_span:
                slot_ref[:, at] = (span_down == query_span[k]).astype(bf16)
            else:
                slot_ref[:, at] = level_onehot.T.astype(bf16)


def attention_kernel(
    place_ref,
    qo_own_ref, kv_own_ref, qo_ref, kv_ref,
    near_own_ref, near_far_ref, side_own_ref, side_far_ref,
    gate_ref, bias_ref, slot_ref,
    *rest, rows, tokens, q_size, heads, steps, offset, apart,
):
    back_ref, own_ref, far_ref, near_grad_ref, result_ref, *side_grad_refs, sums_ref = rest[
        -7 - apart :
    ]
    scale = 1.0 / math.sqrt(DH)
    bf16, f32 = jnp.bfloat16, jnp.float32
    tile = 32

    def dot(left, right, left_dim, right_dim):
        return lax.dot_general(
            left, right, (((left_dim,), (right_dim,)), ((), ())), preferred_element_type=f32
        )

    def columns(j):
        start = pl.multiple_of(j * DH, DH)
        return pl.ds(start, DH), pl.ds(pl.multiple_of(start + offset, DH), DH)

    def load(j):
        at, at_all = columns(j)
        keys, values = [], []
        for ref, cols in (
            (kv_own_ref, at_all), (kv_ref, at), (near_own_ref, at_all), (near_far_ref, at),
            (side_own_ref, at_all), (side_far_ref, at),
        ):
            keys.append(ref[0, :, cols])
            values.append(ref[1, :, cols])
        keys, values = jnp.concatenate(keys, axis=0), jnp.concatenate(values, axis=0)
        queries = jnp.concatenate([qo_own_ref[0, :, at_all], qo_ref[0, :, at]], axis=0)
        cotangent = jnp.concatenate([qo_own_ref[1, :, at_all], qo_ref[1, :, at]], axis=0)
        blocks = []
        for start in range(0, tokens, q_size):
            span = slice(start, start + q_size)
            q, o = queries[span], cotangent[span].astype(f32)
            gate = gate_ref[span, at_all]
            g = (gate * o).astype(bf16)
            blocks.append((q, o, gate, g, dot(keys, q, 1, 1), dot(values, g, 1, 1)))
        return keys, values, blocks

    def work(j, keys, values, blocks):
        at, at_all = columns(j)
        keys_t, values_t = keys.T, values.T
        key_grad = value_grad = sums = None
        for number, (q, o, gate, g, scores, prob_grad) in enumerate(blocks):
            start = number * q_size
            span = slice(start, start + q_size)
            count = scores.shape[0]
            tiles = [slice(r, r + tile) for r in range(0, count, tile)]
            raised, top = [], None
            for t in tiles:
                part = scores[t] * (scale * LOG2E) + bias_ref[t, span]
                raised.append(part)
                high = jnp.max(part.reshape(tile // 8, 8, q_size), axis=0)
                top = high if top is None else jnp.maximum(top, high)
            top = jnp.max(top, axis=0, keepdims=True)
            total = None
            for i in range(len(tiles)):
                raised[i] = jnp.exp2(raised[i] - top)
                part = jnp.sum(raised[i].reshape(tile // 8, 8, q_size), axis=0)
                total = part if total is None else total + part
            inverse = 1.0 / jnp.sum(total, axis=0, keepdims=True)
            low = jnp.concatenate([(part * inverse).astype(bf16) for part in raised], axis=0)
            attended_t = dot(values_t, low, 1, 0).astype(bf16)
            row_dot = jnp.sum(g.T.astype(f32) * attended_t.astype(f32), axis=0, keepdims=True)
            attended = attended_t.T.astype(f32)
            score_grad = jnp.concatenate(
                [
                    (part * ((prob_grad[t] - row_dot) * inverse)).astype(bf16)
                    for part, t in zip(raised, tiles)
                ],
                axis=0,
            )
            query_grad = (dot(keys_t, score_grad, 1, 0) * scale).astype(bf16).T
            mixed = (gate * attended).astype(bf16)
            if start == 0:
                result_ref[0, :, at] = mixed[:rows]
                result_ref[1, :, at] = query_grad[:rows]
                back_ref[0, : q_size - rows, at] = mixed[rows:]
                back_ref[1, : q_size - rows, at] = query_grad[rows:]
            else:
                back_ref[0, start - rows : start - rows + q_size, at] = mixed
                back_ref[1, start - rows : start - rows + q_size, at] = query_grad
            dk, dv = dot(score_grad, q, 1, 0), dot(low, g, 1, 0)
            part = dot(slot_ref[:, span], (o * attended).astype(bf16), 1, 0)
            key_grad = dk if key_grad is None else key_grad + dk
            value_grad = dv if value_grad is None else value_grad + dv
            sums = part if sums is None else sums + part
        sums_ref[:, at_all] = sums.astype(bf16)
        for i, grad in ((0, key_grad * scale), (1, value_grad)):
            own_ref[i, :, at] = grad[:rows]
            far_ref[i, :, at] = grad[rows:tokens]
            low = grad[tokens:].astype(bf16)
            near_grad_ref[i, :, at] = low[:tokens]
            if apart:
                side_grad_refs[0][i, :, at] = low[tokens : tokens + rows]
                side_grad_refs[1][i, :, at] = low[tokens + rows :]
            else:
                side_grad_refs[0][i, :, at] = low[tokens:]

    def some(step, carry):
        first = step * heads
        ready = load(first)
        for j in range(heads):
            following = load(first + j + 1) if j + 1 < heads else None
            work(first + j, *ready)
            ready = following
        return carry

    if steps == 1:
        some(0, 0)
    else:
        lax.fori_loop(0, steps, some, 0)


def pack_kernel(place_ref, first_ref, second_ref, own_ref, *rest, groups):
    *far_refs, sems = rest
    rows, width = own_ref.shape[1:]
    copies = []

    def copy(ref, start, to):
        cols = pl.ds(pl.multiple_of(start, DH), to.shape[1])
        copies.append(pltpu.make_async_copy(ref.at[:, cols], to, sems.at[len(copies)]))
        copies[-1].start()

    for k in (*range(1, groups), 0):
        start = lax.rem(place_ref[0] + k, groups) * width
        for i, ref in enumerate((first_ref, second_ref)):
            if k == 0:
                copy(ref, start, own_ref.at[i])
                continue
            for p, far_ref in enumerate(far_refs):
                at = pl.ds((k - 1) * rows, rows)
                copy(ref, start + p * far_ref.shape[2], far_ref.at[i, at])
    for one in copies:
        one.wait()


def far_sum_kernel(part_ref, near_ref, side_ref, out_ref):
    far = slice(near_ref.shape[1] - part_ref.shape[1], None)
    total = part_ref[...] + near_ref[:, far].astype(jnp.float32)
    side = side_ref[:, side_ref.shape[1] - part_ref.shape[1] :].astype(jnp.float32)
    out_ref[...] = (total + side).astype(out_ref.dtype)


def finish_kernel(
    place_ref, part_ref, near_ref, side_ref, result_ref, *refs, groups, parts, p, gate
):
    slabs, refs = refs[: 2 * (groups - 1)], refs[2 * (groups - 1) :]
    slot_refs = refs[1 : 1 + groups] if gate else ()
    scratch = 3 if gate else 2
    total_ref, *gate_scratch, sems = refs[-scratch:]
    outs = refs[-scratch - (5 if gate else 4) : -scratch]
    part_width = part_ref.shape[2]
    width = part_width * parts
    copies = []

    def send(source, to):
        copies.append(pltpu.make_async_copy(source, to, sems.at[len(copies)]))
        copies[-1].start()

    def place_slab(slab, first, second, k):
        start = lax.rem(place_ref[0] + k, groups) * width + p * part_width
        cols = pl.ds(pl.multiple_of(start, DH), part_width)
        for i, ref in enumerate((first, second)):
            send(slab.at[i], ref.at[:, cols])

    place_slab(result_ref, outs[0], outs[1], 0)
    for k in range(1, groups):
        place_slab(slabs[k - 1], outs[0], outs[1], k)
        place_slab(slabs[groups + k - 2], outs[2], outs[3], k)
    near, side = (ref[:, : part_ref.shape[1]].astype(jnp.float32) for ref in (near_ref, side_ref))
    total_ref[...] = (part_ref[...] + near + side).astype(total_ref.dtype)
    place_slab(total_ref, outs[2], outs[3], 0)
    if gate:
        noise_ref, gate_ref = refs[0], gate_scratch[0]
        by_span = noise_ref.shape[1] == slot_refs[0].shape[0]
        levels = lax.broadcasted_iota(jnp.int32, (gate_ref.shape[0], noise_ref.shape[1]), 0)
        onehot = (levels == noise_ref[...]).astype(jnp.bfloat16)
        for j, ref in enumerate(slot_refs):
            if by_span:
                sums = jnp.dot(onehot, ref[...], preferred_element_type=jnp.float32)
            else:
                sums = ref[...].astype(jnp.float32)
            start = lax.bitwise_xor(lax.rem(place_ref[0], groups), j) * width
            cols = pl.ds(pl.multiple_of(start, DH), width)
            gate_ref[:, cols] = sums
            send(gate_ref.at[:, cols], outs[4].at[:, cols])
    for one in copies:
        one.wait()


def per_device(
    queries, key_rows, value_rows, out_cotangent, gate_table, span_ids, noise_level, block_mask
):
    groups = lax.axis_size("head")
    ctx_count = lax.axis_size("ctx")
    rows, full_width = queries.shape
    width = full_width // groups
    heads = width // DH
    tokens = rows * groups
    far_rows = tokens - rows
    parts = 2 if heads % 2 == 0 else 1
    part_width = width // parts
    part_heads = heads // parts
    span_total = noise_level.shape[0]
    level_count = gate_table.shape[0]
    by_span = span_total <= level_count // 2
    slots = span_total if by_span else level_count
    c = lax.axis_index("ctx")
    h = lax.axis_index("head")
    place = (c * groups + h).astype(jnp.int32).reshape(1)
    head_at = lambda place: lax.rem(place[0], groups)
    bf16, f32 = jnp.bfloat16, jnp.float32
    tie = lax.optimization_barrier

    near_pairs = [(i, i ^ 1) for i in range(ctx_count)]
    side_pairs = [(i, (i - 1 + 2 * (i % 2)) % ctx_count) for i in range(ctx_count)]

    whole = lambda shape: pl.BlockSpec(shape, lambda i, place: (0,) * len(shape))
    limit = (26 if tokens <= 256 else 56) * 1024 * 1024
    params = pltpu.CompilerParams(vmem_limit_bytes=limit)
    alone = pltpu.CompilerParams(vmem_limit_bytes=56 * 1024 * 1024)
    cheap = pl.CostEstimate(flops=1, bytes_accessed=1, transcendentals=0)
    in_vmem = pl.BlockSpec(memory_space=pltpu.VMEM)
    anywhere = pl.BlockSpec(memory_space=pl.ANY)
    small = pltpu.CompilerParams(vmem_limit_bytes=(12 if tokens <= 256 else 36) * 1024 * 1024)

    def pack(first, second, params):
        far_shape = (2, far_rows, part_width)
        return pl.pallas_call(
            functools.partial(pack_kernel, groups=groups),
            grid_spec=pltpu.PrefetchScalarGridSpec(
                num_scalar_prefetch=1,
                in_specs=[anywhere] * 2,
                out_specs=[in_vmem] * (1 + parts),
                scratch_shapes=[pltpu.SemaphoreType.DMA((2 + 2 * (groups - 1) * parts,))],
            ),
            out_shape=[jax.ShapeDtypeStruct((2, rows, width), bf16)]
            + [jax.ShapeDtypeStruct(far_shape, bf16)] * parts,
            compiler_params=params,
            cost_estimate=cheap,
            name="pack",
        )(place, first, second)

    def to_peers(slab):
        arrived = []
        for k in range(1, groups):
            part = slab if groups == 2 else slab[:, (k - 1) * rows : k * rows]
            pairs = [(i, (i + k) % groups) for i in range(groups)]
            arrived.append(lax.ppermute(part, "head", pairs))
        return arrived[0] if groups == 2 else jnp.concatenate(arrived, axis=1)

    def from_peers(slab):
        arrived = []
        for k in range(1, groups):
            part = slab if groups == 2 else slab[:, (k - 1) * rows : k * rows]
            pairs = [(i, (i - k) % groups) for i in range(groups)]
            arrived.append(lax.ppermute(part, "head", pairs))
        return arrived

    kv_own, *kv_sent = pack(key_rows, value_rows, alone)
    qo_own, *qo_sent = pack(queries, out_cotangent, small)
    side_own = lax.ppermute(kv_own, "ctx", side_pairs)
    near_own = lax.ppermute(kv_own, "ctx", near_pairs)
    kv_far = [to_peers(slab) for slab in kv_sent]
    side_far = [lax.ppermute(slab, "ctx", side_pairs) for slab in kv_far]
    near_far = [lax.ppermute(slab, "ctx", near_pairs) for slab in kv_far]
    qo_far = [
        to_peers(tie((slab, *done))[0])
        for slab, done in zip(qo_sent, (kv_far[:1], (*kv_far[1:], side_own, near_own)))
    ]

    sizes = (ctx_count, groups, rows, span_total, level_count, by_span)
    whole = lambda shape: pl.BlockSpec(shape, lambda i, place: (0,) * len(shape))
    bias, gate, slot = pl.pallas_call(
        functools.partial(prep_kernel, sizes=sizes),
        grid_spec=pltpu.PrefetchScalarGridSpec(
            num_scalar_prefetch=1,
            grid=(1,),
            in_specs=[
                whole((ctx_count * groups, rows)),
                whole((1, span_total)),
                whole((span_total, span_total)),
                pl.BlockSpec((level_count, width), lambda i, place: (0, head_at(place))),
            ],
            out_specs=[
                whole((3 * tokens, tokens)),
                whole((tokens, width)),
                whole((slots, tokens)),
            ],
        ),
        out_shape=[
            jax.ShapeDtypeStruct((3 * tokens, tokens), f32),
            jax.ShapeDtypeStruct((tokens, width), f32),
            jax.ShapeDtypeStruct((slots, tokens), bf16),
        ],
        compiler_params=small,
        cost_estimate=cheap,
        name="prep",
    )(
        place,
        span_ids.reshape(ctx_count * groups, rows),
        noise_level.reshape(1, span_total),
        block_mask,
        gate_table,
    )

    direct = tokens <= 256
    batch = next(n for n in (3, 2, 1) if part_heads % n == 0) if direct else 1
    q_size = min(256, tokens)

    def attention(p, joint):
        pair = lambda count: pl.BlockSpec((2, count, DH), lambda i, place: (0, 0, i))
        at_part = lambda count: pl.BlockSpec(
            (2, count, DH), lambda i, place: (0, 0, p * part_heads + i)
        )
        column = lambda count: pl.BlockSpec(
            (count, DH), lambda i, place: (0, p * part_heads + i)
        )
        struct = jax.ShapeDtypeStruct
        side_counts = (rows, far_rows) if p + 1 == parts else (tokens,)
        inputs = [
            qo_own, kv_own, qo_far[p], kv_far[p],
            near_own, near_far[p], side_own, side_far[p],
            gate, bias, slot,
        ]
        in_specs = [
            at_part(rows), at_part(rows), pair(far_rows), pair(far_rows),
            at_part(rows), pair(far_rows), at_part(rows), pair(far_rows),
            column(tokens), whole((3 * tokens, tokens)), whole((slots, tokens)),
        ]
        counts = (far_rows, rows, far_rows, tokens, rows, *side_counts)
        out_specs = [*[pair(count) for count in counts], column(slots)]
        if direct:
            in_specs, out_specs = [in_vmem] * len(in_specs), [in_vmem] * len(out_specs)
        types = [f32 if i in (1, 2) else bf16 for i in range(len(counts))]
        return pl.pallas_call(
            functools.partial(
                attention_kernel,
                rows=rows, tokens=tokens, q_size=q_size, apart=p + 1 == parts, heads=batch,
                steps=part_heads // batch if direct else 1,
                offset=p * part_width if direct else 0,
            ),
            grid_spec=pltpu.PrefetchScalarGridSpec(
                num_scalar_prefetch=1,
                grid=(1,) if direct else (part_heads,),
                in_specs=in_specs + [anywhere] * len(joint),
                out_specs=out_specs,
            ),
            out_shape=[
                *[
                    struct((2, count, part_width), kind) for count, kind in zip(counts, types)
                ],
                struct((slots, width), bf16),
            ],
            input_output_aliases={1 + len(inputs) + i: len(counts) + i for i in range(len(joint))},
            compiler_params=params,
            cost_estimate=cheap,
            name="attention",
        )(place, *inputs, *joint)

    def shifted(array, step):
        return lax.ppermute(array, "ctx", [(i, i ^ step) for i in range(ctx_count)])

    def rounds(steps, sums):
        for one, two in zip(steps[::2], [*steps[1::2], None]):
            if two is None:
                sums = sums + shifted(sums, one)
                continue
            across = [shifted(sums, step) for step in (one, two, one ^ two)]
            sums = (sums + across[0]) + (across[1] + across[2])
        return sums

    bits = [1 << n for n in range(ctx_count.bit_length() - 1)]
    def summed(p):
        far_grad = pl.pallas_call(
            far_sum_kernel,
            in_specs=[in_vmem] * 3,
            out_specs=in_vmem,
            out_shape=jax.ShapeDtypeStruct((2, far_rows, part_width), bf16),
            compiler_params=small,
            cost_estimate=cheap,
            name="far_sum",
        )(far[p], near_back[p], side_back_far[p])
        far_sent.append(far_grad)
        grad_far.append(from_peers(far_grad))

    joint, own, far, own_results = (), [], [], []
    back_far, side_back_far, near_back, side_back_own, far_sent, grad_far = [], [], [], [], [], []
    for p in range(parts):
        back, own_part, far_part, near_grad, result, *rest = attention(p, joint)
        side_grads, joint = rest[:-1], rest[-1:]
        own_results.append(result)
        if p + 1 < parts:
            side_grads, *_ = tie((side_grads, side_far[p + 1], near_far[p + 1], qo_far[p + 1]))
        if p > 0:
            side_grads, side_back_far = tie(
                (side_grads, side_back_far)
            )
            joint, back_far = tie((joint, back_far))
        own.append(own_part)
        far.append(far_part)
        side_back_far.append(lax.ppermute(side_grads[-1], "ctx", side_pairs))
        near_back.append(lax.ppermute(near_grad, "ctx", near_pairs))
        back_far.append(from_peers(back))
        if p > 0:
            sums = rounds(bits[2:], rounds(bits[:1], joint[0]))
            side_back_far[p - 1], sums, _ = tie((side_back_far[p - 1], sums, back_far[p]))
            summed(p - 1)
        if p + 1 < parts:
            side_back_own.append(side_back_far[p])
            continue
        side_grad_own, _ = tie((side_grads[0], side_back_far[p]))
        side_back_own.append(lax.ppermute(side_grad_own, "ctx", side_pairs))
    if parts == 1:
        sums = rounds(bits[2:], rounds(bits[:1], joint[0]))

    sums = rounds(bits[1:2], sums)
    side_back_far, sums, back_far, grad_far = tie((side_back_far, sums, back_far, grad_far))
    summed(parts - 1)

    def to_all(before, after, sums):
        slabs = [rounds(before, sums)]
        for step in (1 << n for n in range(groups.bit_length() - 1)):
            pairs = [(i, i ^ step) for i in range(groups)]
            slabs = slabs + [lax.ppermute(slab, "head", pairs) for slab in slabs]
        return [rounds(after, slab) for slab in slabs]

    sums, _ = tie((sums, far_sent[-1]))
    slabs = to_all([], [], sums)
    results = []
    struct = jax.ShapeDtypeStruct
    for p in range(parts):
        gate = p + 1 == parts
        operands = [own[p], near_back[p], side_back_own[p], own_results[p], *back_far[p], *grad_far[p]]
        if gate:
            operands += [noise_level.reshape(1, span_total), *slabs]
        scratch = [pltpu.VMEM((2, rows, part_width), bf16)]
        if gate:
            scratch.append(pltpu.VMEM((level_count, full_width), f32))
        scratch.append(pltpu.SemaphoreType.DMA((4 * groups + groups,)))
        results = pl.pallas_call(
            functools.partial(finish_kernel, groups=groups, parts=parts, p=p, gate=gate),
            grid_spec=pltpu.PrefetchScalarGridSpec(
                num_scalar_prefetch=1,
                in_specs=[in_vmem] * len(operands) + [anywhere] * len(results),
                out_specs=[anywhere] * (4 + gate),
                scratch_shapes=scratch,
            ),
            out_shape=[struct((rows, full_width), bf16)] * 4
            + [struct((level_count, full_width), f32)] * gate,
            input_output_aliases={1 + len(operands) + i: i for i in range(len(results))},
            compiler_params=small,
            cost_estimate=cheap,
            name="finish",
        )(place, *operands, *results)
    return tuple(results)


def solution(mesh):
    sharded = P(("ctx", "head"), None)
    return jax.shard_map(
        per_device,
        mesh=mesh,
        in_specs=(sharded,) * 4 + (P(),) * 4,
        out_specs=(sharded,) * 4 + (P(),),
        check_vma=False,
    )
```

```python
import functools
import math

import jax
import jax.numpy as jnp
from jax import lax
from jax.experimental import pallas as pl
from jax.experimental.pallas import tpu as pltpu
from jax.sharding import PartitionSpec as P

DH = 128
HIDDEN = -1e30
LOG2E = 1.4426950408889634


def other_ctx(c, near):
    odd = lax.rem(c, 2)
    return c + 1 - 2 * odd if near else c - 1 + 2 * odd


def prep_kernel(
    place_ref, span_ref, noise_ref, mask_ref, table_ref, bias_ref, gate_ref, slot_ref, *, sizes
):
    ctx_count, groups, rows, span_total, level_count, by_span = sizes
    c, h = lax.div(place_ref[0], groups), lax.rem(place_ref[0], groups)
    tokens = groups * rows
    total = ctx_count * tokens
    bf16, f32 = jnp.bfloat16, jnp.float32

    def block_of(ctx, k):
        return ctx * groups + lax.rem(h - k + groups, groups)

    def spans_of(ctx, k):
        at = jnp.clip(ctx, 0, ctx_count - 1)
        return span_ref[pl.ds(block_of(at, k), 1), :]

    def as_column(row):
        return jnp.broadcast_to(row.astype(f32), (rows, rows)).T[:, :1].astype(jnp.int32)

    across = lax.broadcasted_iota(jnp.int32, (1, rows), 1)
    down = lax.broadcasted_iota(jnp.int32, (rows, 1), 0)
    span_lane = lax.broadcasted_iota(jnp.int32, (rows, span_total), 1)
    span_down = lax.broadcasted_iota(jnp.int32, (span_total, rows), 0)
    level_lane = lax.broadcasted_iota(jnp.int32, (rows, level_count), 1)
    query_span = [spans_of(c, k) for k in range(groups)]
    query_pos = [block_of(c, k) * rows + across for k in range(groups)]
    mask_low = mask_ref[...].astype(bf16)
    allowed_q = [
        lax.dot_general(
            mask_low,
            (span_down == row).astype(bf16),
            (((0,), (0,)), ((), ())),
            preferred_element_type=f32,
        ).astype(bf16)
        for row in query_span
    ]
    noise = noise_ref[...].astype(f32)
    for i, ctx in enumerate((c, other_ctx(c, True), other_ctx(c, False))):
        for k in range(groups):
            key_span = as_column(spans_of(ctx, k))
            key_pos = block_of(ctx, k) * rows + down
            valid = (key_pos >= 0) & (key_pos < total)
            onehot = key_span == span_lane
            at = slice((i * groups + k) * rows, (i * groups + k + 1) * rows)
            for p in range(groups):
                allowed = jnp.dot(
                    onehot.astype(bf16), allowed_q[p], preferred_element_type=f32
                )
                visible = (
                    (allowed > 0.5)
                    & (key_span <= query_span[p])
                    & (query_pos[p] - key_pos < tokens)
                    & valid
                )
                bias_ref[at, p * rows : (p + 1) * rows] = jnp.where(visible, 0.0, HIDDEN)
            if i > 0:
                continue
            level = jnp.sum(jnp.where(onehot, noise, 0.0), axis=1, keepdims=True)
            level_onehot = (level.astype(jnp.int32) == level_lane).astype(f32)
            gate_ref[at, :] = jnp.dot(
                level_onehot,
                table_ref[...],
                precision=lax.Precision.HIGHEST,
                preferred_element_type=f32,
            )
            if by_span:
                slot_ref[:, at] = (span_down == query_span[k]).astype(bf16)
            else:
                slot_ref[:, at] = level_onehot.T.astype(bf16)


def attention_kernel(
    place_ref,
    qo_own_ref, kv_own_ref, qo_ref, kv_ref,
    near_own_ref, near_far_ref, side_own_ref, side_far_ref,
    gate_ref, bias_ref, slot_ref,
    *rest, rows, tokens, q_size, heads, steps, offset, apart,
):
    back_ref, own_ref, far_ref, near_grad_ref, result_ref, *side_grad_refs, sums_ref = rest[
        -7 - apart :
    ]
    scale = 1.0 / math.sqrt(DH)
    bf16, f32 = jnp.bfloat16, jnp.float32
    tile = 32

    def dot(left, right, left_dim, right_dim):
        return lax.dot_general(
            left, right, (((left_dim,), (right_dim,)), ((), ())), preferred_element_type=f32
        )

    def columns(j):
        start = pl.multiple_of(j * DH, DH)
        return pl.ds(start, DH), pl.ds(pl.multiple_of(start + offset, DH), DH)

    def load(j):
        at, at_all = columns(j)
        keys, values = [], []
        for ref, cols in (
            (kv_own_ref, at_all), (kv_ref, at), (near_own_ref, at_all), (near_far_ref, at),
            (side_own_ref, at_all), (side_far_ref, at),
        ):
            keys.append(ref[0, :, cols])
            values.append(ref[1, :, cols])
        keys, values = jnp.concatenate(keys, axis=0), jnp.concatenate(values, axis=0)
        queries = jnp.concatenate([qo_own_ref[0, :, at_all], qo_ref[0, :, at]], axis=0)
        cotangent = jnp.concatenate([qo_own_ref[1, :, at_all], qo_ref[1, :, at]], axis=0)
        blocks = []
        for start in range(0, tokens, q_size):
            span = slice(start, start + q_size)
            q, o = queries[span], cotangent[span].astype(f32)
            gate = gate_ref[span, at_all]
            g = (gate * o).astype(bf16)
            blocks.append((q, o, gate, g, dot(keys, q, 1, 1), dot(values, g, 1, 1)))
        return keys, values, blocks

    def work(j, keys, values, blocks):
        at, at_all = columns(j)
        keys_t, values_t = keys.T, values.T
        key_grad = value_grad = sums = None
        for number, (q, o, gate, g, scores, prob_grad) in enumerate(blocks):
            start = number * q_size
            span = slice(start, start + q_size)
            count = scores.shape[0]
            tiles = [slice(r, r + tile) for r in range(0, count, tile)]
            raised, top = [], None
            for t in tiles:
                part = scores[t] * (scale * LOG2E) + bias_ref[t, span]
                raised.append(part)
                high = jnp.max(part.reshape(tile // 8, 8, q_size), axis=0)
                top = high if top is None else jnp.maximum(top, high)
            top = jnp.max(top, axis=0, keepdims=True)
            total = None
            for i in range(len(tiles)):
                raised[i] = jnp.exp2(raised[i] - top)
                part = jnp.sum(raised[i].reshape(tile // 8, 8, q_size), axis=0)
                total = part if total is None else total + part
            inverse = 1.0 / jnp.sum(total, axis=0, keepdims=True)
            low = jnp.concatenate([(part * inverse).astype(bf16) for part in raised], axis=0)
            attended_t = dot(values_t, low, 1, 0).astype(bf16)
            row_dot = jnp.sum(g.T.astype(f32) * attended_t.astype(f32), axis=0, keepdims=True)
            attended = attended_t.T.astype(f32)
            score_grad = jnp.concatenate(
                [
                    (part * ((prob_grad[t] - row_dot) * inverse)).astype(bf16)
                    for part, t in zip(raised, tiles)
                ],
                axis=0,
            )
            query_grad = (dot(keys_t, score_grad, 1, 0) * scale).astype(bf16).T
            mixed = (gate * attended).astype(bf16)
            if start == 0:
                result_ref[0, :, at] = mixed[:rows]
                result_ref[1, :, at] = query_grad[:rows]
                back_ref[0, : q_size - rows, at] = mixed[rows:]
                back_ref[1, : q_size - rows, at] = query_grad[rows:]
            else:
                back_ref[0, start - rows : start - rows + q_size, at] = mixed
                back_ref[1, start - rows : start - rows + q_size, at] = query_grad
            dk, dv = dot(score_grad, q, 1, 0), dot(low, g, 1, 0)
            part = dot(slot_ref[:, span], (o * attended).astype(bf16), 1, 0)
            key_grad = dk if key_grad is None else key_grad + dk
            value_grad = dv if value_grad is None else value_grad + dv
            sums = part if sums is None else sums + part
        sums_ref[:, at_all] = sums.astype(bf16)
        for i, grad in ((0, key_grad * scale), (1, value_grad)):
            own_ref[i, :, at] = grad[:rows]
            far_ref[i, :, at] = grad[rows:tokens]
            low = grad[tokens:].astype(bf16)
            near_grad_ref[i, :, at] = low[:tokens]
            if apart:
                side_grad_refs[0][i, :, at] = low[tokens : tokens + rows]
                side_grad_refs[1][i, :, at] = low[tokens + rows :]
            else:
                side_grad_refs[0][i, :, at] = low[tokens:]

    def some(step, carry):
        first = step * heads
        ready = load(first)
        for j in range(heads):
            following = load(first + j + 1) if j + 1 < heads else None
            work(first + j, *ready)
            ready = following
        return carry

    if steps == 1:
        some(0, 0)
    else:
        lax.fori_loop(0, steps, some, 0)


def pack_kernel(place_ref, first_ref, second_ref, own_ref, *rest, groups):
    *far_refs, sems = rest
    rows, width = own_ref.shape[1:]
    copies = []

    def copy(ref, start, to):
        cols = pl.ds(pl.multiple_of(start, DH), to.shape[1])
        copies.append(pltpu.make_async_copy(ref.at[:, cols], to, sems.at[len(copies)]))
        copies[-1].start()

    for k in (*range(1, groups), 0):
        start = lax.rem(place_ref[0] + k, groups) * width
        for i, ref in enumerate((first_ref, second_ref)):
            if k == 0:
                copy(ref, start, own_ref.at[i])
                continue
            for p, far_ref in enumerate(far_refs):
                at = pl.ds((k - 1) * rows, rows)
                copy(ref, start + p * far_ref.shape[2], far_ref.at[i, at])
    for one in copies:
        one.wait()


def far_sum_kernel(part_ref, near_ref, side_ref, out_ref):
    far = slice(near_ref.shape[1] - part_ref.shape[1], None)
    total = part_ref[...] + near_ref[:, far].astype(jnp.float32)
    side = side_ref[:, side_ref.shape[1] - part_ref.shape[1] :].astype(jnp.float32)
    out_ref[...] = (total + side).astype(out_ref.dtype)


def finish_kernel(
    place_ref, part_ref, near_ref, side_ref, result_ref, *refs, groups, parts, p, gate
):
    slabs, refs = refs[: 2 * (groups - 1)], refs[2 * (groups - 1) :]
    slot_refs = refs[1 : 1 + groups] if gate else ()
    scratch = 3 if gate else 2
    total_ref, *gate_scratch, sems = refs[-scratch:]
    outs = refs[-scratch - (5 if gate else 4) : -scratch]
    part_width = part_ref.shape[2]
    width = part_width * parts
    copies = []

    def send(source, to):
        copies.append(pltpu.make_async_copy(source, to, sems.at[len(copies)]))
        copies[-1].start()

    def place_slab(slab, first, second, k):
        start = lax.rem(place_ref[0] + k, groups) * width + p * part_width
        cols = pl.ds(pl.multiple_of(start, DH), part_width)
        for i, ref in enumerate((first, second)):
            send(slab.at[i], ref.at[:, cols])

    place_slab(result_ref, outs[0], outs[1], 0)
    for k in range(1, groups):
        place_slab(slabs[k - 1], outs[0], outs[1], k)
        place_slab(slabs[groups + k - 2], outs[2], outs[3], k)
    near, side = (ref[:, : part_ref.shape[1]].astype(jnp.float32) for ref in (near_ref, side_ref))
    total_ref[...] = (part_ref[...] + near + side).astype(total_ref.dtype)
    place_slab(total_ref, outs[2], outs[3], 0)
    if gate:
        noise_ref, gate_ref = refs[0], gate_scratch[0]
        by_span = noise_ref.shape[1] == slot_refs[0].shape[0]
        levels = lax.broadcasted_iota(jnp.int32, (gate_ref.shape[0], noise_ref.shape[1]), 0)
        onehot = (levels == noise_ref[...]).astype(jnp.bfloat16)
        for j, ref in enumerate(slot_refs):
            if by_span:
                sums = jnp.dot(onehot, ref[...], preferred_element_type=jnp.float32)
            else:
                sums = ref[...].astype(jnp.float32)
            start = lax.bitwise_xor(lax.rem(place_ref[0], groups), j) * width
            cols = pl.ds(pl.multiple_of(start, DH), width)
            gate_ref[:, cols] = sums
            send(gate_ref.at[:, cols], outs[4].at[:, cols])
    for one in copies:
        one.wait()


def per_device(
    queries, key_rows, value_rows, out_cotangent, gate_table, span_ids, noise_level, block_mask
):
    groups = lax.axis_size("head")
    ctx_count = lax.axis_size("ctx")
    rows, full_width = queries.shape
    width = full_width // groups
    heads = width // DH
    tokens = rows * groups
    far_rows = tokens - rows
    parts = 2 if heads % 2 == 0 else 1
    part_width = width // parts
    part_heads = heads // parts
    span_total = noise_level.shape[0]
    level_count = gate_table.shape[0]
    by_span = span_total <= level_count // 2
    slots = span_total if by_span else level_count
    c = lax.axis_index("ctx")
    h = lax.axis_index("head")
    place = (c * groups + h).astype(jnp.int32).reshape(1)
    head_at = lambda place: lax.rem(place[0], groups)
    bf16, f32 = jnp.bfloat16, jnp.float32
    tie = lax.optimization_barrier

    near_pairs = [(i, i ^ 1) for i in range(ctx_count)]
    side_pairs = [(i, (i - 1 + 2 * (i % 2)) % ctx_count) for i in range(ctx_count)]

    whole = lambda shape: pl.BlockSpec(shape, lambda i, place: (0,) * len(shape))
    limit = (26 if tokens <= 256 else 56) * 1024 * 1024
    params = pltpu.CompilerParams(vmem_limit_bytes=limit)
    alone = pltpu.CompilerParams(vmem_limit_bytes=56 * 1024 * 1024)
    cheap = pl.CostEstimate(flops=1, bytes_accessed=1, transcendentals=0)
    in_vmem = pl.BlockSpec(memory_space=pltpu.VMEM)
    anywhere = pl.BlockSpec(memory_space=pl.ANY)
    small = pltpu.CompilerParams(vmem_limit_bytes=(12 if tokens <= 256 else 36) * 1024 * 1024)

    def pack(first, second, params):
        far_shape = (2, far_rows, part_width)
        return pl.pallas_call(
            functools.partial(pack_kernel, groups=groups),
            grid_spec=pltpu.PrefetchScalarGridSpec(
                num_scalar_prefetch=1,
                in_specs=[anywhere] * 2,
                out_specs=[in_vmem] * (1 + parts),
                scratch_shapes=[pltpu.SemaphoreType.DMA((2 + 2 * (groups - 1) * parts,))],
            ),
            out_shape=[jax.ShapeDtypeStruct((2, rows, width), bf16)]
            + [jax.ShapeDtypeStruct(far_shape, bf16)] * parts,
            compiler_params=params,
            cost_estimate=cheap,
            name="pack",
        )(place, first, second)

    def to_peers(slab):
        arrived = []
        for k in range(1, groups):
            part = slab if groups == 2 else slab[:, (k - 1) * rows : k * rows]
            pairs = [(i, (i + k) % groups) for i in range(groups)]
            arrived.append(lax.ppermute(part, "head", pairs))
        return arrived[0] if groups == 2 else jnp.concatenate(arrived, axis=1)

    def from_peers(slab):
        arrived = []
        for k in range(1, groups):
            part = slab if groups == 2 else slab[:, (k - 1) * rows : k * rows]
            pairs = [(i, (i - k) % groups) for i in range(groups)]
            arrived.append(lax.ppermute(part, "head", pairs))
        return arrived

    kv_own, *kv_sent = pack(key_rows, value_rows, alone)
    qo_own, *qo_sent = pack(queries, out_cotangent, small)
    side_own = lax.ppermute(kv_own, "ctx", side_pairs)
    near_own = lax.ppermute(kv_own, "ctx", near_pairs)
    kv_far = [to_peers(slab) for slab in kv_sent]
    side_far = [lax.ppermute(slab, "ctx", side_pairs) for slab in kv_far]
    near_far = [lax.ppermute(slab, "ctx", near_pairs) for slab in kv_far]
    qo_far = [
        to_peers(tie((slab, *done))[0])
        for slab, done in zip(qo_sent, (kv_far[:1], (*kv_far[1:], side_own, near_own)))
    ]

    sizes = (ctx_count, groups, rows, span_total, level_count, by_span)
    whole = lambda shape: pl.BlockSpec(shape, lambda i, place: (0,) * len(shape))
    bias, gate, slot = pl.pallas_call(
        functools.partial(prep_kernel, sizes=sizes),
        grid_spec=pltpu.PrefetchScalarGridSpec(
            num_scalar_prefetch=1,
            grid=(1,),
            in_specs=[
                whole((ctx_count * groups, rows)),
                whole((1, span_total)),
                whole((span_total, span_total)),
                pl.BlockSpec((level_count, width), lambda i, place: (0, head_at(place))),
            ],
            out_specs=[
                whole((3 * tokens, tokens)),
                whole((tokens, width)),
                whole((slots, tokens)),
            ],
        ),
        out_shape=[
            jax.ShapeDtypeStruct((3 * tokens, tokens), f32),
            jax.ShapeDtypeStruct((tokens, width), f32),
            jax.ShapeDtypeStruct((slots, tokens), bf16),
        ],
        compiler_params=small,
        cost_estimate=cheap,
        name="prep",
    )(
        place,
        span_ids.reshape(ctx_count * groups, rows),
        noise_level.reshape(1, span_total),
        block_mask,
        gate_table,
    )

    direct = tokens <= 256
    batch = next(n for n in (6, 3, 2, 1) if part_heads % n == 0) if direct else 1
    q_size = min(256, tokens)

    def attention(p, joint):
        pair = lambda count: pl.BlockSpec((2, count, DH), lambda i, place: (0, 0, i))
        at_part = lambda count: pl.BlockSpec(
            (2, count, DH), lambda i, place: (0, 0, p * part_heads + i)
        )
        column = lambda count: pl.BlockSpec(
            (count, DH), lambda i, place: (0, p * part_heads + i)
        )
        struct = jax.ShapeDtypeStruct
        side_counts = (rows, far_rows) if p + 1 == parts else (tokens,)
        inputs = [
            qo_own, kv_own, qo_far[p], kv_far[p],
            near_own, near_far[p], side_own, side_far[p],
            gate, bias, slot,
        ]
        in_specs = [
            at_part(rows), at_part(rows), pair(far_rows), pair(far_rows),
            at_part(rows), pair(far_rows), at_part(rows), pair(far_rows),
            column(tokens), whole((3 * tokens, tokens)), whole((slots, tokens)),
        ]
        counts = (far_rows, rows, far_rows, tokens, rows, *side_counts)
        out_specs = [*[pair(count) for count in counts], column(slots)]
        if direct:
            in_specs, out_specs = [in_vmem] * len(in_specs), [in_vmem] * len(out_specs)
        types = [f32 if i in (1, 2) else bf16 for i in range(len(counts))]
        return pl.pallas_call(
            functools.partial(
                attention_kernel,
                rows=rows, tokens=tokens, q_size=q_size, apart=p + 1 == parts, heads=batch,
                steps=part_heads // batch if direct else 1,
                offset=p * part_width if direct else 0,
            ),
            grid_spec=pltpu.PrefetchScalarGridSpec(
                num_scalar_prefetch=1,
                grid=(1,) if direct else (part_heads,),
                in_specs=in_specs + [anywhere] * len(joint),
                out_specs=out_specs,
            ),
            out_shape=[
                *[
                    struct((2, count, part_width), kind) for count, kind in zip(counts, types)
                ],
                struct((slots, width), bf16),
            ],
            input_output_aliases={1 + len(inputs) + i: len(counts) + i for i in range(len(joint))},
            compiler_params=params,
            cost_estimate=cheap,
            name="attention",
        )(place, *inputs, *joint)

    def shifted(array, step):
        return lax.ppermute(array, "ctx", [(i, i ^ step) for i in range(ctx_count)])

    def rounds(steps, sums):
        for one, two in zip(steps[::2], [*steps[1::2], None]):
            if two is None:
                sums = sums + shifted(sums, one)
                continue
            across = [shifted(sums, step) for step in (one, two, one ^ two)]
            sums = (sums + across[0]) + (across[1] + across[2])
        return sums

    bits = [1 << n for n in range(ctx_count.bit_length() - 1)]
    def summed(p):
        far_grad = pl.pallas_call(
            far_sum_kernel,
            in_specs=[in_vmem] * 3,
            out_specs=in_vmem,
            out_shape=jax.ShapeDtypeStruct((2, far_rows, part_width), bf16),
            compiler_params=small,
            cost_estimate=cheap,
            name="far_sum",
        )(far[p], near_back[p], side_back_far[p])
        far_sent.append(far_grad)
        grad_far.append(from_peers(far_grad))

    joint, own, far, own_results = (), [], [], []
    back_far, side_back_far, near_back, side_back_own, far_sent, grad_far = [], [], [], [], [], []
    for p in range(parts):
        back, own_part, far_part, near_grad, result, *rest = attention(p, joint)
        side_grads, joint = rest[:-1], rest[-1:]
        own_results.append(result)
        if p + 1 < parts:
            side_grads, *_ = tie((side_grads, side_far[p + 1], near_far[p + 1], qo_far[p + 1]))
        if p > 0:
            side_grads, side_back_far = tie(
                (side_grads, side_back_far)
            )
            joint, back_far = tie((joint, back_far))
        own.append(own_part)
        far.append(far_part)
        side_back_far.append(lax.ppermute(side_grads[-1], "ctx", side_pairs))
        near_back.append(lax.ppermute(near_grad, "ctx", near_pairs))
        back_far.append(from_peers(back))
        if p > 0:
            sums = rounds(bits[2:], rounds(bits[:1], joint[0]))
            side_back_far[p - 1], sums, _ = tie((side_back_far[p - 1], sums, back_far[p]))
            summed(p - 1)
        if p + 1 < parts:
            side_back_own.append(side_back_far[p])
            continue
        side_grad_own, _ = tie((side_grads[0], side_back_far[p]))
        side_back_own.append(lax.ppermute(side_grad_own, "ctx", side_pairs))
    if parts == 1:
        sums = rounds(bits[2:], rounds(bits[:1], joint[0]))

    sums = rounds(bits[1:2], sums)
    side_back_far, sums, back_far, grad_far = tie((side_back_far, sums, back_far, grad_far))
    summed(parts - 1)

    def to_all(before, after, sums):
        slabs = [rounds(before, sums)]
        for step in (1 << n for n in range(groups.bit_length() - 1)):
            pairs = [(i, i ^ step) for i in range(groups)]
            slabs = slabs + [lax.ppermute(slab, "head", pairs) for slab in slabs]
        return [rounds(after, slab) for slab in slabs]

    sums, _ = tie((sums, far_sent[-1]))
    slabs = to_all([], [], sums)
    results = []
    struct = jax.ShapeDtypeStruct
    for p in range(parts):
        gate = p + 1 == parts
        operands = [own[p], near_back[p], side_back_own[p], own_results[p], *back_far[p], *grad_far[p]]
        if gate:
            operands += [noise_level.reshape(1, span_total), *slabs]
        scratch = [pltpu.VMEM((2, rows, part_width), bf16)]
        if gate:
            scratch.append(pltpu.VMEM((level_count, full_width), f32))
        scratch.append(pltpu.SemaphoreType.DMA((4 * groups + groups,)))
        results = pl.pallas_call(
            functools.partial(finish_kernel, groups=groups, parts=parts, p=p, gate=gate),
            grid_spec=pltpu.PrefetchScalarGridSpec(
                num_scalar_prefetch=1,
                in_specs=[in_vmem] * len(operands) + [anywhere] * len(results),
                out_specs=[anywhere] * (4 + gate),
                scratch_shapes=scratch,
            ),
            out_shape=[struct((rows, full_width), bf16)] * 4
            + [struct((level_count, full_width), f32)] * gate,
            input_output_aliases={1 + len(operands) + i: i for i in range(len(results))},
            compiler_params=small,
            cost_estimate=cheap,
            name="finish",
        )(place, *operands, *results)
    return tuple(results)


def solution(mesh):
    sharded = P(("ctx", "head"), None)
    return jax.shard_map(
        per_device,
        mesh=mesh,
        in_specs=(sharded,) * 4 + (P(),) * 4,
        out_specs=(sharded,) * 4 + (P(),),
        check_vma=False,
    )
```
